256 devices in a mesh: work: 32 (over z, y_hi, core), tp: 8 (over x, y_lo).
Axes of the slice: x: 4, y: 4 (y_hi: 2, y_lo: 2; y = y_hi * 2 + y_lo), z: 8, core: 2. Of those that a mesh axis runs over, the one named last changes fastest.
Arguments:
- queries: bfloat16 [32, 16, 40, 128], P('work', None, 'tp'), may hold values from -6 to 6
- new_keys: bfloat16 [32, 16, 8, 128], P('work', None, 'tp'), may hold values from -24 to 24
- new_values: bfloat16 [32, 16, 8, 128], P('work', None, 'tp'), may hold values from -24 to 24
- cache_keys: bfloat16 [32, 4096, 8, 128], P('work', None, 'tp'), may hold values from -96 to 96
- cache_values: bfloat16 [32, 4096, 8, 128], P('work', None, 'tp'), may hold values from -24 to 24
- lengths: int32 [32], P('work'), may hold values from 1024 to 4096, as said below
- positions: int32 [32, 16], P('work'), may hold values from 0 to 32767, as said below
- out_weight: bfloat16 [5120, 5120], P('tp'), may hold values from -0.078125 to 0.078125
Outputs:
- layer_out: bfloat16 [32, 16, 5120], P('work', None, 'tp')
The draws below stay inside these ranges and needn't reach their ends.
Inputs may be any that keep to these rules, and one draw needn't show every extreme that they name: `lengths`: every worker's cache holds at least 1024 live rows; some worker's cache is full and some holds exactly 1024. Each worker's new tokens have consecutive positions.
All inputs are finite; a program needn't handle non-finite values.
Results may differ from the reference program's by a relative error of at most 0.022.
The reference program's roundings to bfloat16 on the way count: a program that leaves them out, or rounds other values in their place, can miss the bound.
Values may be sent and summed in bfloat16 or wider, within the bound.
A program may use at most 192 MiB of HBM per device.

```python
import math
import jax
import jax.numpy as jnp
from jax import lax

D = 5120
H = 40
KVH = 8
HD = 128
CACHE = 4096
NEW = 4
MAXPOS = 32768
ROWS = 16
WORKERS = 32


def draw_lengths(key, part):
    key = jax.random.fold_in(key, 11)
    key_base, key_order = jax.random.split(key)
    picked = jax.random.randint(key_base, (WORKERS,), CACHE // 4, CACHE + 1)
    order = jax.random.permutation(key_order, WORKERS)
    picked = picked.at[order[0]].set(CACHE)
    picked = picked.at[order[1]].set(CACHE // 4)
    return picked.astype(jnp.int32)


def draw_positions(key, part):
    key = jax.random.fold_in(key, 23)
    key_base, key_order = jax.random.split(key)
    starts = jax.random.randint(key_base, (WORKERS,), 0, MAXPOS - ROWS + 1)
    order = jax.random.permutation(key_order, WORKERS)
    starts = starts.at[order[0]].set(0)
    starts = starts.at[order[1]].set(MAXPOS - ROWS)
    return (starts[:, None] + jnp.arange(ROWS)[None, :]).astype(jnp.int32)


def draw_cache_keys(key, part):
    key = jax.random.fold_in(key, 37)
    key_base = jax.random.fold_in(key, 0)
    extent = (WORKERS, CACHE, KVH, HD)
    filled = 2.0 * jax.random.normal(key_base, extent, jnp.float32)
    return filled.astype(jnp.bfloat16)


def block_scale(key, shape, cuts, least, largest):
    factor_of, own = 1.0, jax.random.fold_in(key, 6)
    for position, shards_of in cuts:
        steps = jnp.exp(jax.random.uniform(jax.random.fold_in(own, position), (shards_of,), jnp.float32, least / len(cuts), largest / len(cuts)))
        factor_of = factor_of * jnp.repeat(steps, shape[position] // shards_of).reshape([-1 if axis == position else 1 for axis in range(len(shape))])
    return factor_of


def normal_values(rng, shape, spread, most, cuts=(), kind=jnp.bfloat16):
    array = jax.random.normal(rng, shape, jnp.float32) * spread
    if len(cuts) > 0:
        array = block_scale(rng, shape, cuts, -0.22, 0.18) * array
    return jnp.clip(array, min=-most, max=most).astype(kind)


def setup_inputs(seed: int = 0) -> dict:
    splits = jax.random.split(jax.random.key(seed), 9)
    return {
        "queries": normal_values(splits[0], (WORKERS, ROWS, H, HD), 1.0, 6.0, ((0, 32), (2, 8))),
        "new_keys": normal_values(splits[1], (WORKERS, ROWS, KVH, HD), 4.0, 24.0, ((0, 32), (2, 8))),
        "new_values": normal_values(splits[2], (WORKERS, ROWS, KVH, HD), 4.0, 24.0, ((0, 32), (2, 8))),
        "cache_keys": draw_cache_keys(jax.random.fold_in(splits[8], 71), 0),
        "cache_values": normal_values(splits[4], (WORKERS, CACHE, KVH, HD), 4.0, 24.0, ((0, 32), (2, 8))),
        "lengths": draw_lengths(jax.random.fold_in(splits[8], 71), 0),
        "positions": draw_positions(jax.random.fold_in(splits[8], 71), 0),
        "out_weight": normal_values(splits[7], (H * HD, D), (H * HD) ** -0.5, 0.078125, ((0, 8),)),
    }


rope_base = 1000000.0


def rotate_pairs(values, places):
    middle = values.shape[-1] // 2
    ladder = jnp.arange(middle).astype(jnp.float32) * (2.0 / values.shape[-1])
    inverse = jnp.exp(ladder * (-math.log(rope_base)))
    angles = places.astype(jnp.float32)[:, :, None] * inverse
    cosine = jnp.cos(angles)[:, :, None, :]
    sine_part = jnp.sin(angles)[:, :, None, :]
    first = values[..., :middle]
    second = values[..., middle:]
    return jnp.concatenate([first * cosine - second * sine_part, second * cosine + first * sine_part], axis=-1)


def reference(queries, new_keys, new_values, cache_keys, cache_values, lengths, positions, out_weight):
    group = H // KVH
    rotated_q = rotate_pairs(queries.astype(jnp.float32), positions).astype(jnp.bfloat16)
    rotated_k = rotate_pairs(new_keys.astype(jnp.float32), positions).astype(jnp.bfloat16)
    query_five = rotated_q.astype(jnp.float32).reshape(WORKERS, ROWS, KVH, group, HD)
    row_ids = jnp.arange(ROWS)
    period_ids = row_ids // NEW
    worker_ids = jnp.arange(WORKERS)
    slot_ids = jnp.arange(CACHE)

    def per_owner(owner):
        keys = jnp.concatenate([cache_keys[owner], rotated_k[owner]], axis=0).astype(jnp.float32)
        values = jnp.concatenate([cache_values[owner], new_values[owner]], axis=0).astype(jnp.float32)
        scores = jnp.einsum('wrkgd,nkd->wrkgn', query_five, keys) * (HD ** -0.5)
        live = jnp.broadcast_to((slot_ids < lengths[owner])[None, None, :], (WORKERS, ROWS, CACHE))
        earlier = period_ids[None, None, :] < period_ids[None, :, None]
        same = (worker_ids[:, None, None] == owner) & (period_ids[None, None, :] == period_ids[None, :, None]) & (row_ids[None, None, :] <= row_ids[None, :, None])
        visible = jnp.concatenate([live, earlier | same], axis=2)
        masked = jnp.where(visible[:, :, None, None, :], scores, -jnp.inf)
        peak = jnp.max(masked, axis=-1)
        expd = jnp.exp(masked - peak[..., None])
        total = jnp.sum(expd, axis=-1)
        weights = expd.astype(jnp.bfloat16).astype(jnp.float32)
        output = jnp.einsum('wrkgn,nkd->wrkgd', weights, values)
        normed = (output / total[..., None]).astype(jnp.bfloat16).astype(jnp.float32)
        return peak, total, normed

    peaks, totals, normeds = lax.map(per_owner, worker_ids)
    summit = jnp.max(peaks, axis=0)
    scaling = jnp.exp(peaks - summit) * totals
    numer = jnp.sum(scaling[..., None] * normeds, axis=0)
    denom = jnp.sum(scaling, axis=0)
    attention = (numer / denom[..., None]).astype(jnp.bfloat16)
    flat = attention.reshape(WORKERS * ROWS, H * HD)
    result = jnp.dot(flat, out_weight, preferred_element_type=jnp.float32)
    return result.astype(jnp.bfloat16).reshape(WORKERS, ROWS, D)
```

```python
import math

import jax
import jax.numpy as jnp
from jax import lax
from jax.experimental import pallas as pl
from jax.experimental.pallas import tpu as pltpu
from jax.sharding import PartitionSpec as P

MESH = pl.DeviceIdType.MESH
F32 = jnp.float32
BF16 = jnp.bfloat16

HEADS = 5
ROWS = 16
HD = 128
CACHE = 4096
BLOCK = HEADS * ROWS
PAIR = 2 * CACHE
ALL = PAIR + 128
CHUNK = 2048
CHUNKS = PAIR // CHUNK
TILE = 2 * BLOCK
SLOTS = 16
TP = 8
COLS = 640
PLANES = 8
ORDER = (0, 3, 5, 2, 6, 4, 1, 7)
LEAST = 1024

SCALE2 = HD**-0.5 * math.log2(math.e)
LOG_BASE = math.log(1000000.0)


def cos_sin(angle):
    turn = jnp.floor(angle * (2.0 / math.pi) + 0.5)
    rest = angle - turn * 1.5703125
    rest = rest - turn * 4.837512969970703125e-4
    rest = rest - turn * 7.54978995489188e-8
    z = rest * rest
    sine = rest + rest * z * ((-1.9515295891e-4 * z + 8.3321608736e-3) * z - 1.6666654611e-1)
    cosine = 1.0 - 0.5 * z + z * z * (
        (2.443315711809948e-5 * z - 1.388731625493765e-3) * z + 4.166664568298827e-2
    )
    quarter = turn.astype(jnp.int32) & 3
    odd = (quarter & 1) == 1
    c = jnp.where(odd, sine, cosine)
    s = jnp.where(odd, cosine, sine)
    c = jnp.where((quarter == 1) | (quarter == 2), -c, c)
    s = jnp.where(quarter >= 2, -s, s)
    return c, s


def kernel(
    pos_ref, len_ref, q_ref, nk_ref, nv_ref, ck_ref, cv_ref, w_ref, out_ref,
    kall, vaug, wv, qbuf, nsend, nrecv, lsend, lrecv, s0, s1, t0, t1, mx0, mx1, acc,
    psend, precv, lens,
    loc_sem, pair_send, pair_recv, q_send, q_recv, n_send, n_recv, l_send, l_recv, p_send, p_recv,
):
    me = lax.axis_index("work")
    t = lax.axis_index("tp")
    z = me // 4
    yh = (me // 2) % 2
    c = me % 2
    slot_me = me // 2

    def device(slot):
        return {"work": 2 * slot + c, "tp": t}

    sibling = {"work": 2 * slot_me + 1 - c, "tp": t}

    copy_k = pltpu.make_async_copy(ck_ref, kall.at[pl.ds(0, CACHE)], loc_sem.at[0])
    copy_v = pltpu.make_async_copy(
        cv_ref, vaug.at[pl.ds(0, CACHE), pl.ds(0, HD)], loc_sem.at[1]
    )
    copy_k.start()
    copy_v.start()
    copy_w = [
        pltpu.make_async_copy(w_ref.at[:, pl.ds(k * COLS, COLS)], wv.at[k], loc_sem.at[2 + k])
        for k in range(TP)
    ]
    for k in range(TP):
        copy_w[k].start()

    barrier = pltpu.get_barrier_semaphore()

    def greet(i, _):
        pl.semaphore_signal(
            barrier, inc=1, device_id=device((slot_me + i) % SLOTS), device_id_type=MESH
        )
        return 0

    lax.fori_loop(1, SLOTS, greet, 0)
    pl.semaphore_signal(barrier, inc=1, device_id=sibling, device_id_type=MESH)

    def greet_tp(i, _):
        pl.semaphore_signal(
            barrier, inc=1, device_id={"work": me, "tp": (t + i) % TP}, device_id_type=MESH
        )
        return 0

    lax.fori_loop(1, TP, greet_tp, 0)

    lane = lax.broadcasted_iota(jnp.int32, (ROWS, HD), 1)
    place = pos_ref[0] + lax.broadcasted_iota(jnp.int32, (ROWS, HD), 0)
    ladder = (lane % (HD // 2)).astype(F32) * (2.0 / HD)
    angle = place.astype(F32) * jnp.exp(ladder * -LOG_BASE)
    cosine, sine = cos_sin(angle)
    sine = jnp.where(lane < HD // 2, -sine, sine)

    def rotated(x):
        x = x.astype(F32)
        return (x * cosine + pltpu.roll(x, HD // 2, 1) * sine).astype(BF16)

    for g in range(HEADS):
        qbuf[slot_me, g * ROWS : (g + 1) * ROWS, :] = rotated(q_ref[g * ROWS : (g + 1) * ROWS, :])
    kall[PAIR : PAIR + ROWS, :] = rotated(nk_ref[...])
    kall[PAIR + 2 * ROWS :, :] = jnp.zeros((128 - 2 * ROWS, HD), BF16)
    vaug[PAIR : PAIR + ROWS, 0:HD] = nv_ref[...]
    vaug[PAIR + 2 * ROWS :, 0:HD] = jnp.zeros((128 - 2 * ROWS, HD), BF16)
    vaug[PAIR:, HD:] = jnp.ones((128, HD), BF16)
    lens[0] = jnp.full((8, HD), len_ref[0], jnp.int32).astype(F32)

    pl.semaphore_wait(barrier, SLOTS - 1 + 1 + TP - 1)

    def send_q(i):
        for b in range(2):
            to = 2 * ((z + ORDER[i]) % PLANES) + b
            copy = pltpu.make_async_remote_copy(
                qbuf.at[slot_me], qbuf.at[slot_me],
                q_send.at[2 * i + b], q_recv.at[slot_me],
                device_id=device(to), device_id_type=MESH,
            )
            if ORDER[i] == 0:
                @pl.when(yh != b)
                def _():
                    copy.start()
            else:
                copy.start()

    pair = [
        pltpu.make_async_remote_copy(
            src, dst, pair_send.at[k], pair_recv.at[k], device_id=sibling, device_id_type=MESH
        )
        for k, (src, dst) in enumerate(
            (
                (lens.at[0], lens.at[1]),
                (kall.at[pl.ds(PAIR, ROWS)], kall.at[pl.ds(PAIR + ROWS, ROWS)]),
                (nv_ref, vaug.at[pl.ds(PAIR + ROWS, ROWS), pl.ds(0, HD)]),
                (ck_ref, kall.at[pl.ds(CACHE, CACHE)]),
                (cv_ref, vaug.at[pl.ds(CACHE, CACHE), pl.ds(0, HD)]),
            )
        )
    ]
    for copy in pair[:4]:
        copy.start()
    for i in range(PLANES):
        send_q(i)
    pair[4].start()

    def live_of(base, r0, size):
        rows = lax.broadcasted_iota(jnp.int32, (size, HD), 0).astype(F32) + r0.astype(F32)
        return jnp.where(rows < lens[base // CACHE, 0:1, :], 1.0, 0.0).astype(BF16)

    STEP = 512

    def mask_keys(base):
        first = kall[base : base + 16, :].astype(F32)[0:1, :]
        first = jnp.broadcast_to(first, (STEP, HD)).astype(BF16)

        def body(j, _):
            r0 = pl.multiple_of(j * STEP, STEP)
            live = live_of(base, r0, STEP)
            rows = pl.ds(base + r0, STEP)
            kall[rows, :] = kall[rows, :] * live + first * (1.0 - live)
            return 0

        lax.fori_loop(LEAST // STEP, CACHE // STEP, body, 0)

    def mask_values(base):
        vaug[base : base + LEAST, HD:] = jnp.ones((LEAST, HD), BF16)

        def body(j, _):
            r0 = pl.multiple_of(j * STEP, STEP)
            live = live_of(base, r0, STEP)
            rows = pl.ds(base + r0, STEP)
            vaug[rows, 0:HD] = vaug[rows, 0:HD] * live
            vaug[rows, HD:] = live
            return 0

        lax.fori_loop(LEAST // STEP, CACHE // STEP, body, 0)

    NT = (((1,), (1,)), ((), ()))

    def plane(i):
        return (z + ORDER[i]) % PLANES

    def wait_q(i):
        for b in range(2):
            slot = 2 * plane(i) + b
            copy = pltpu.make_async_remote_copy(
                qbuf.at[slot], qbuf.at[slot], q_send.at[2 * i + b], q_recv.at[slot],
                device_id=device(slot), device_id_type=MESH,
            )
            if ORDER[i] == 0:
                @pl.when(yh != b)
                def _():
                    copy.wait_recv()
            else:
                copy.wait_recv()

    def tile_q(i):
        return qbuf[pl.ds(2 * plane(i), 2)].reshape(TILE, HD)

    def scores(q, j, s_ref, mx):
        keys = kall[pl.ds(pl.multiple_of(j * CHUNK, CHUNK), CHUNK), :]
        s = lax.dot_general(q, keys, NT, preferred_element_type=F32)
        s_ref[j] = s
        top = mx[...]
        for u in range(CHUNK // HD):
            top = jnp.maximum(top, s[:, u * HD : (u + 1) * HD])
        mx[...] = top

    def new_scores(i, q, t_ref, mx):
        row = lax.broadcasted_iota(jnp.int32, (TILE, HD), 0)
        col = lax.broadcasted_iota(jnp.int32, (TILE, HD), 1)
        r, r2 = row & 15, col & 15
        seen = (r2 >> 2) < (r >> 2)
        if ORDER[i] == 0:
            here = jnp.where(row >= BLOCK, 1, 0) == yh
            seen = seen | (here & (col < ROWS) & ((r2 >> 2) == (r >> 2)) & (r2 <= r))
        s = lax.dot_general(q, kall[PAIR:, :], NT, preferred_element_type=F32)
        s = jnp.where(seen & (col < 2 * ROWS), s, -1e30)
        t_ref[...] = s
        mx[...] = s

    def close_max(mx):
        mx[...] = jnp.broadcast_to(jnp.max(mx[...], axis=1, keepdims=True), (TILE, HD))

    def weights(s, top):
        return jnp.exp2((s - top) * SCALE2).astype(BF16)

    def values(j, s_ref, mx):
        top = mx[...]
        p = jnp.concatenate(
            [weights(s_ref[j, :, u * HD : (u + 1) * HD], top) for u in range(CHUNK // HD)], axis=1
        )
        v = vaug[pl.ds(pl.multiple_of(j * CHUNK, CHUNK), CHUNK), :]
        acc[...] += jnp.dot(p, v, preferred_element_type=F32)

    def new_values(t_ref, mx):
        p = weights(t_ref[...], mx[...])
        acc[...] = jnp.dot(p, vaug[PAIR:, :], preferred_element_type=F32)

    def result_copies(i, b):
        slot = 2 * plane(i) + b
        return [
            pltpu.make_async_remote_copy(
                src.at[2 * i + b], dst.at[slot_me], send.at[2 * i + b], recv.at[slot_me],
                device_id=device(slot), device_id_type=MESH,
            )
            for src, dst, send, recv in (
                (nsend, nrecv, n_send, n_recv), (lsend, lrecv, l_send, l_recv)
            )
        ]

    def finish(i, mx):
        total = acc[:, HD:]
        n = (acc[:, :HD] / total).astype(BF16)
        level = mx[...] * SCALE2 + jnp.log(total) * math.log2(math.e)
        for b in range(2):
            part = slice(b * BLOCK, (b + 1) * BLOCK)
            flat = jnp.concatenate([level[part], jnp.zeros((HD - BLOCK, HD), F32)], axis=0)
            flat = jnp.transpose(flat)[0:8, :]
            nsend[2 * i + b] = n[part]
            lsend[2 * i + b] = flat
            copies = result_copies(i, b)
            if ORDER[i] == 0:
                @pl.when(yh != b)
                def _():
                    for copy in copies:
                        copy.start()

                @pl.when(yh == b)
                def _():
                    nrecv[slot_me] = n[part]
                    lrecv[slot_me] = flat
            else:
                for copy in copies:
                    copy.start()

    s_refs, t_refs, mx_refs = (s0, s1), (t0, t1), (mx0, mx1)

    copy_k.wait()
    mask_keys(0)
    wait_q(0)
    pair[0].wait_recv()
    pair[1].wait_recv()
    pair[2].wait_recv()
    q = tile_q(0)
    new_scores(0, q, t0, mx0)

    def first(j, _):
        scores(q, j, s0, mx0)
        return 0

    lax.fori_loop(0, CHUNKS // 2, first, 0)
    copy_v.wait()
    mask_values(0)
    pair[3].wait_recv()
    mask_keys(CACHE)
    lax.fori_loop(CHUNKS // 2, CHUNKS, first, 0)
    close_max(mx0)
    pair[4].wait_recv()
    mask_values(CACHE)

    for i in range(PLANES):
        now, later = i % 2, (i + 1) % 2
        new_values(t_refs[now], mx_refs[now])
        if i + 1 < PLANES:
            wait_q(i + 1)
            q = tile_q(i + 1)
            new_scores(i + 1, q, t_refs[later], mx_refs[later])

            def both(j, _, q=q, now=now, later=later):
                scores(q, j, s_refs[later], mx_refs[later])
                values(j, s_refs[now], mx_refs[now])
                return 0

            lax.fori_loop(0, CHUNKS, both, 0)
            close_max(mx_refs[later])
        else:

            def last(j, _, now=now):
                values(j, s_refs[now], mx_refs[now])
                return 0

            lax.fori_loop(0, CHUNKS, last, 0)
        finish(i, mx_refs[now])

    def wait_results(i, _):
        slot = (slot_me + i) % SLOTS
        for dst, send, recv in ((nrecv, n_send, n_recv), (lrecv, l_send, l_recv)):
            pltpu.make_async_remote_copy(
                dst.at[slot], dst.at[slot], send.at[0], recv.at[slot],
                device_id=device(slot), device_id_type=MESH,
            ).wait_recv()
        return 0

    lax.fori_loop(1, SLOTS, wait_results, 0)
    levels = [lrecv[v] for v in range(SLOTS)]
    summit = levels[0]
    for v in range(1, SLOTS):
        summit = jnp.maximum(summit, levels[v])
    shares = [jnp.exp2(level - summit) for level in levels]
    denom = shares[0]
    for v in range(1, SLOTS):
        denom = denom + shares[v]
    row = lax.broadcasted_iota(jnp.int32, (8, HD), 0)
    packed = []
    for half in range(2):
        rows = jnp.zeros((8, HD), F32)
        for v in range(8):
            rows = jnp.where(row == v, shares[8 * half + v], rows)
        packed.append(rows / denom)
    packed.append(jnp.zeros((HD - SLOTS, HD), F32))
    share = jnp.transpose(jnp.concatenate(packed, axis=0))[0:BLOCK, :]
    attention = jnp.zeros((BLOCK, HD), F32)
    for v in range(SLOTS):
        attention = attention + nrecv[v].astype(F32) * share[:, v : v + 1]
    attention = attention.astype(BF16)
    flat = jnp.concatenate(
        [attention[g * ROWS : (g + 1) * ROWS, :] for g in range(HEADS)], axis=1
    )

    for k in range(TP):
        copy_w[k].wait()
    sums = []
    for i in (4, 5, 3, 2, 6, 7, 1):
        peer = (t + i) % TP
        psend[i] = jnp.dot(flat, wv[peer], preferred_element_type=F32).astype(BF16)
        copy = pltpu.make_async_remote_copy(
            psend.at[i], precv.at[t], p_send.at[i], p_recv.at[t],
            device_id={"work": me, "tp": peer}, device_id_type=MESH,
        )
        copy.start()
        sums.append(copy)
    total = jnp.dot(flat, wv[t], preferred_element_type=F32)
    for i in (1, 7, 2, 6, 3, 5, 4):
        peer = (t + i) % TP
        pltpu.make_async_remote_copy(
            psend.at[i], precv.at[peer], p_send.at[i], p_recv.at[peer],
            device_id={"work": me, "tp": peer}, device_id_type=MESH,
        ).wait_recv()
        total = total + precv[peer].astype(F32)
    out_ref[...] = total.astype(BF16)

    for copy in sums:
        copy.wait_send()
    for copy in pair:
        copy.wait_send()
    for i in range(PLANES):
        for b in range(2):
            copies = result_copies(i, b) + [
                pltpu.make_async_remote_copy(
                    qbuf.at[slot_me], qbuf.at[slot_me], q_send.at[2 * i + b], q_recv.at[slot_me],
                    device_id=device(2 * plane(i) + b), device_id_type=MESH,
                )
            ]
            if ORDER[i] == 0:
                @pl.when(yh != b)
                def _():
                    for copy in copies:
                        copy.wait_send()
            else:
                for copy in copies:
                    copy.wait_send()


def per_device(
    queries, new_keys, new_values, cache_keys, cache_values, lengths, positions, out_weight
):
    vmem = pl.BlockSpec(memory_space=pltpu.VMEM)
    smem = pl.BlockSpec(memory_space=pltpu.SMEM)
    anywhere = pl.BlockSpec(memory_space=pl.ANY)
    dma = pltpu.SemaphoreType.DMA
    out = pl.pallas_call(
        kernel,
        out_shape=jax.ShapeDtypeStruct((ROWS, COLS), BF16),
        in_specs=[smem, smem, vmem, vmem, vmem, anywhere, anywhere, anywhere],
        out_specs=vmem,
        scratch_shapes=[
            pltpu.VMEM((ALL, HD), BF16),
            pltpu.VMEM((ALL, 2 * HD), BF16),
            pltpu.VMEM((TP, COLS, COLS), BF16),
            pltpu.VMEM((SLOTS, BLOCK, HD), BF16),
            pltpu.VMEM((SLOTS, BLOCK, HD), BF16),
            pltpu.VMEM((SLOTS, BLOCK, HD), BF16),
            pltpu.VMEM((SLOTS, 8, HD), F32),
            pltpu.VMEM((SLOTS, 8, HD), F32),
            pltpu.VMEM((CHUNKS, TILE, CHUNK), F32),
            pltpu.VMEM((CHUNKS, TILE, CHUNK), F32),
            pltpu.VMEM((TILE, HD), F32),
            pltpu.VMEM((TILE, HD), F32),
            pltpu.VMEM((TILE, HD), F32),
            pltpu.VMEM((TILE, HD), F32),
            pltpu.VMEM((TILE, 2 * HD), F32),
            pltpu.VMEM((TP, ROWS, COLS), BF16),
            pltpu.VMEM((TP, ROWS, COLS), BF16),
            pltpu.VMEM((2, 8, HD), F32),
            dma((2 + TP,)),
            dma((5,)),
            dma((5,)),
            dma((SLOTS,)),
            dma((SLOTS,)),
            dma((SLOTS,)),
            dma((SLOTS,)),
            dma((SLOTS,)),
            dma((SLOTS,)),
            dma((TP,)),
            dma((TP,)),
        ],
        compiler_params=pltpu.CompilerParams(
            collective_id=0, has_side_effects=True, vmem_limit_bytes=58 * 1024 * 1024
        ),
    )(
        positions.reshape(ROWS),
        lengths,
        queries[0].transpose(1, 0, 2).reshape(BLOCK, HD),
        new_keys.reshape(ROWS, HD),
        new_values.reshape(ROWS, HD),
        cache_keys.reshape(CACHE, HD),
        cache_values.reshape(CACHE, HD),
        out_weight,
    )
    return out[None]


def solution(mesh):
    in_specs = (
        P("work", None, "tp", None),
        P("work", None, "tp", None),
        P("work", None, "tp", None),
        P("work", None, "tp", None),
        P("work", None, "tp", None),
        P("work"),
        P("work", None),
        P("tp", None),
    )
    out_specs = P("work", None, "tp")
    return jax.shard_map(
        per_device, mesh=mesh, in_specs=in_specs, out_specs=out_specs, check_vma=False
    )
```

```python
import math

import jax
import jax.numpy as jnp
from jax import lax
from jax.experimental import pallas as pl
from jax.experimental.pallas import tpu as pltpu
from jax.sharding import PartitionSpec as P

MESH = pl.DeviceIdType.MESH
F32 = jnp.float32
BF16 = jnp.bfloat16

HEADS = 5
ROWS = 16
HD = 128
CACHE = 4096
BLOCK = HEADS * ROWS
NEWPAD = 128
CHUNK = 1024
CHUNKS = CACHE // CHUNK
TILE = 4 * BLOCK
SLOTS = 16
TP = 8
COLS = 640
PLANES = 8
ORDER = (0, 1, 3, 5, 4, 2, 6, 7)
TILES = PLANES + 1
DIRECT = 2
LEAST = 1024
STEP = 512

SCALE2 = HD**-0.5 * math.log2(math.e)
LOG_BASE = math.log(1000000.0)
NT = (((1,), (1,)), ((), ()))


def cos_sin(angle):
    turn = jnp.floor(angle * (2.0 / math.pi) + 0.5)
    rest = angle - turn * 1.5703125
    rest = rest - turn * 4.837512969970703125e-4
    rest = rest - turn * 7.54978995489188e-8
    z = rest * rest
    sine = rest + rest * z * ((-1.9515295891e-4 * z + 8.3321608736e-3) * z - 1.6666654611e-1)
    cosine = 1.0 - 0.5 * z + z * z * (
        (2.443315711809948e-5 * z - 1.388731625493765e-3) * z + 4.166664568298827e-2
    )
    quarter = turn.astype(jnp.int32) & 3
    odd = (quarter & 1) == 1
    c = jnp.where(odd, sine, cosine)
    s = jnp.where(odd, cosine, sine)
    c = jnp.where((quarter == 1) | (quarter == 2), -c, c)
    s = jnp.where(quarter >= 2, -s, s)
    return c, s


def kernel(
    pos_ref, len_ref, q_ref, nk_ref, nv_ref, ck_ref, cv_ref, w_ref, out_ref,
    kall, vaug, wv, qbuf, nsend, nrecv, lsend, lrecv, s0, s1, t0, t1, mx0, mx1, acc,
    nkeep, lkeep, xn_out, xn_in, xl_out, xl_in, psend, precv,
    loc_sem, q_send, q_recv, c_send, c_recv, f_send, f_recv, n_send, n_recv, l_send, l_recv,
    xn_send, xn_recv, xl_send, xl_recv, p_send, p_recv,
):
    me = lax.axis_index("work")
    t = lax.axis_index("tp")
    z = me // 4
    yh = (me // 2) % 2
    c = me % 2
    slot_me = me // 2

    def device(slot, core):
        return {"work": 2 * slot + core, "tp": t}

    def remote(src, dst, send, recv, to):
        return pltpu.make_async_remote_copy(
            src, dst, send, recv, device_id=to, device_id_type=MESH
        )

    sibling = device(slot_me, 1 - c)
    beside = 2 * z + 1 - yh

    def plane(i):
        return (z + ORDER[i]) % PLANES

    def source(i):
        return (z + PLANES - ORDER[i]) % PLANES

    copy_k = pltpu.make_async_copy(ck_ref, kall.at[pl.ds(0, CACHE)], loc_sem.at[0])
    copy_v = pltpu.make_async_copy(
        cv_ref, vaug.at[pl.ds(0, CACHE), pl.ds(0, HD)], loc_sem.at[1]
    )
    copy_k.start()
    copy_v.start()

    barrier = pltpu.get_barrier_semaphore()

    def signal(to):
        pl.semaphore_signal(barrier, inc=1, device_id=to, device_id_type=MESH)

    def greet(i, _):
        signal(device((slot_me + i) % SLOTS, c))
        return 0

    lax.fori_loop(1, SLOTS, greet, 0)
    cross = [sibling, device(beside, 1 - c)]
    for d in (1, PLANES - 1):
        for b in range(2):
            cross.append(device(2 * ((z + d) % PLANES) + b, 1 - c))
    for to in cross:
        signal(to)

    def greet_tp(i, _):
        signal({"work": me, "tp": (t + i) % TP})
        return 0

    lax.fori_loop(1, TP, greet_tp, 0)

    copy_w = [
        pltpu.make_async_copy(w_ref.at[:, pl.ds(k * COLS, COLS)], wv.at[k], loc_sem.at[2 + k])
        for k in range(TP)
    ]
    for k in range(TP):
        copy_w[k].start()

    lane = lax.broadcasted_iota(jnp.int32, (ROWS, HD), 1)
    place = pos_ref[0] + lax.broadcasted_iota(jnp.int32, (ROWS, HD), 0)
    ladder = (lane % (HD // 2)).astype(F32) * (2.0 / HD)
    angle = place.astype(F32) * jnp.exp(ladder * -LOG_BASE)
    cosine, sine = cos_sin(angle)
    sine = jnp.where(lane < HD // 2, -sine, sine)

    def rotated(x):
        x = x.astype(F32)
        return (x * cosine + pltpu.roll(x, HD // 2, 1) * sine).astype(BF16)

    for g in range(HEADS):
        qbuf[z, yh, g * ROWS : (g + 1) * ROWS, :] = rotated(q_ref[g * ROWS : (g + 1) * ROWS, :])
    kall[CACHE : CACHE + ROWS, :] = rotated(nk_ref[...])
    kall[CACHE + ROWS :, :] = jnp.zeros((NEWPAD - ROWS, HD), BF16)
    vaug[CACHE : CACHE + ROWS, 0:HD] = nv_ref[...]
    vaug[CACHE + ROWS :, 0:HD] = jnp.zeros((NEWPAD - ROWS, HD), BF16)
    vaug[CACHE:, HD:] = jnp.ones((NEWPAD, HD), BF16)

    pl.semaphore_wait(barrier, SLOTS - 1 + len(cross) + TP - 1)

    mine = qbuf.at[z, yh]
    sends = []

    def send_cross(k, to):
        copy = remote(mine, qbuf.at[z, 2 + yh], c_send.at[k], c_recv.at[slot_me], to)
        copy.start()
        sends.append(copy)

    def send_same(k, slot):
        copy = remote(mine, mine, q_send.at[k], q_recv.at[slot_me], device(slot, c))
        copy.start()
        sends.append(copy)

    send_cross(0, sibling)
    for i in range(1, PLANES):
        for b in range(2):
            send_same(2 * i + b, 2 * source(i) + b)
            if i < DIRECT:
                send_cross(2 * i + b, device(2 * source(i) + b, 1 - c))
        if i == 1:
            send_same(1, beside)
            send_cross(1, device(beside, 1 - c))

    copy_k.wait()
    length = jnp.full((1, HD), len_ref[0], jnp.int32)
    head_key = jnp.broadcast_to(kall[0:16, :].astype(F32)[0:1, :], (STEP, HD)).astype(BF16)

    def live_rows(j):
        rows = lax.broadcasted_iota(jnp.int32, (STEP, HD), 0) + j * STEP
        return jnp.where(rows < length, 1.0, 0.0).astype(BF16)

    def mask_keys(j, _):
        live = live_rows(j)
        rows = pl.ds(pl.multiple_of(j * STEP, STEP), STEP)
        kall[rows, :] = kall[rows, :] * live + head_key * (1.0 - live)
        return 0

    def mask_values(j, _):
        live = live_rows(j)
        rows = pl.ds(pl.multiple_of(j * STEP, STEP), STEP)
        vaug[rows, 0:HD] = vaug[rows, 0:HD] * live
        vaug[rows, HD:] = live
        return 0

    lax.fori_loop(LEAST // STEP, CACHE // STEP, mask_keys, 0)
    vaug[0:LEAST, HD:] = jnp.ones((LEAST, HD), BF16)

    def wait_cross(slot):
        buf = qbuf.at[slot // 2, 2 + slot % 2]
        remote(mine, buf, c_send.at[0], c_recv.at[slot], sibling).wait_recv()

    def wait_same(slot):
        buf = qbuf.at[slot // 2, slot % 2]
        remote(mine, buf, q_send.at[0], q_recv.at[slot], sibling).wait_recv()

    def forward(i):
        p = plane(i)
        return remote(
            qbuf.at[p, pl.ds(0, 2)], qbuf.at[p, pl.ds(2, 2)], f_send.at[i], f_recv.at[i], sibling
        )

    def pass_on(i):
        for b in range(2):
            wait_same(2 * plane(i) + b)
        if i >= DIRECT:
            forward(i).start()

    def queries_of(i):
        if i == 0 or i == PLANES:
            slot = slot_me if i == 0 else beside
            if i:
                wait_same(slot)
            wait_cross(slot)
            b = slot % 2
            return jnp.concatenate([qbuf[z, b], qbuf[z, 2 + b]], axis=0)
        if i < DIRECT:
            for b in range(2):
                wait_cross(2 * plane(i) + b)
        else:
            forward(i).wait_recv()
        return qbuf[plane(i)].reshape(TILE, HD)

    def scores(q, j, s_ref, mx):
        rows = q.shape[0]
        s = lax.dot_general(
            q, kall[j * CHUNK : (j + 1) * CHUNK, :], NT, preferred_element_type=F32
        )
        s_ref[j, 0:rows, :] = s
        top = mx[0:rows, :]
        for u in range(CHUNK // HD):
            top = jnp.maximum(top, s[:, u * HD : (u + 1) * HD])
        mx[0:rows, :] = top

    def new_scores(i, q, t_ref, mx):
        rows = q.shape[0]
        row = lax.broadcasted_iota(jnp.int32, (rows, HD), 0)
        col = lax.broadcasted_iota(jnp.int32, (rows, HD), 1)
        r = row & 15
        seen = (col >> 2) < (r >> 2)
        if i == 0:
            seen = seen | ((row < BLOCK) & ((col >> 2) == (r >> 2)) & (col <= r))
        s = lax.dot_general(q, kall[CACHE:, :], NT, preferred_element_type=F32)
        s = jnp.where(seen, s, -1e30)
        t_ref[0:rows, :] = s
        mx[0:rows, :] = s

    def close_max(rows, mx):
        mx[0:rows, :] = jnp.broadcast_to(
            jnp.max(mx[0:rows, :], axis=1, keepdims=True), (rows, HD)
        )

    def weights(s, top):
        return jnp.exp2((s - top) * SCALE2).astype(BF16)

    def values(rows, j, s_ref, mx):
        top = mx[0:rows, :]
        p = jnp.concatenate(
            [
                weights(s_ref[j, 0:rows, u * HD : (u + 1) * HD], top)
                for u in range(CHUNK // HD)
            ],
            axis=1,
        )
        v = vaug[j * CHUNK : (j + 1) * CHUNK, :]
        acc[0:rows, :] += jnp.dot(p, v, preferred_element_type=F32)

    def new_values(rows, t_ref, mx):
        p = weights(t_ref[0:rows, :], mx[0:rows, :])
        acc[0:rows, :] = jnp.dot(p, vaug[CACHE:, :], preferred_element_type=F32)

    def as_row(level):
        flat = jnp.concatenate([level, jnp.zeros((HD - BLOCK, HD), F32)], axis=0)
        return jnp.transpose(flat)[0:8, :]

    def send_result(k, n, level, slot, to):
        nsend[k] = n
        lsend[k] = as_row(level)
        for src, dst, send, recv in (
            (nsend, nrecv, n_send, n_recv), (lsend, lrecv, l_send, l_recv)
        ):
            copy = remote(src.at[k], dst.at[slot], send.at[k], recv.at[slot], to)
            copy.start()
            sends.append(copy)

    def exchange(i):
        return [
            remote(xn_out.at[i], xn_in.at[i], xn_send.at[i], xn_recv.at[i], sibling),
            remote(xl_out.at[i], xl_in.at[i], xl_send.at[i], xl_recv.at[i], sibling),
        ]

    def finish(i, rows, mx):
        total = acc[0:rows, HD:]
        n = acc[0:rows, :HD] / total
        level = mx[0:rows, :] * SCALE2 + jnp.log(total) * math.log2(math.e)
        half = rows // 2
        if i == 0:
            nrecv[slot_me] = n[:half].astype(BF16)
            lrecv[slot_me] = as_row(level[:half])
            send_result(0, n[half:].astype(BF16), level[half:], SLOTS + yh, sibling)
        elif i == PLANES:
            send_result(1, n[:half].astype(BF16), level[:half], slot_me, device(beside, c))
            send_result(
                2 * PLANES, n[half:].astype(BF16), level[half:], SLOTS + yh,
                device(beside, 1 - c),
            )
        else:
            nkeep[i % 2] = n[:half]
            lkeep[i % 2] = level[:half]
            xn_out[i] = n[half:].astype(BF16)
            xl_out[i] = level[half:]
            for copy in exchange(i):
                copy.start()
                sends.append(copy)

    def merge(i):
        for copy in exchange(i):
            copy.wait_recv()
        level, other = lkeep[i % 2], xl_in[i]
        top = jnp.maximum(level, other)
        a, b = jnp.exp2(level - top), jnp.exp2(other - top)
        total = a + b
        n = ((nkeep[i % 2] * a + xn_in[i].astype(F32) * b) / total).astype(BF16)
        level = top + jnp.log(total) * math.log2(math.e)
        for k in range(2):
            part = slice(k * BLOCK, (k + 1) * BLOCK)
            send_result(
                2 * i + k, n[part], level[part], slot_me, device(2 * plane(i) + k, c)
            )

    s_refs, t_refs, mx_refs = (s0, s1), (t0, t1), (mx0, mx1)

    def rows_of(i):
        return 2 * BLOCK if i in (0, PLANES) else TILE

    q = queries_of(0)
    new_scores(0, q, t0, mx0)
    for j in range(CHUNKS):
        scores(q, j, s0, mx0)
    close_max(rows_of(0), mx0)
    copy_v.wait()
    lax.fori_loop(LEAST // STEP, CACHE // STEP, mask_values, 0)
    pass_on(1)

    for i in range(TILES):
        now, later = i % 2, (i + 1) % 2
        rows = rows_of(i)
        if i + 2 < PLANES:
            pass_on(i + 2)
        if i + 1 < TILES:
            q = queries_of(i + 1)
            new_scores(i + 1, q, t_refs[later], mx_refs[later])
        new_values(rows, t_refs[now], mx_refs[now])
        for j in range(CHUNKS):
            if i + 1 < TILES:
                scores(q, j, s_refs[later], mx_refs[later])
            values(rows, j, s_refs[now], mx_refs[now])
        if i + 1 < TILES:
            close_max(rows_of(i + 1), mx_refs[later])
        finish(i, rows, mx_refs[now])
        if 2 <= i:
            merge(i - 1)

    def wait_result(slot):
        remote(nsend.at[0], nrecv.at[slot], n_send.at[0], n_recv.at[slot], sibling).wait_recv()
        remote(lsend.at[0], lrecv.at[slot], l_send.at[0], l_recv.at[slot], sibling).wait_recv()

    def wait_other(i, _):
        wait_result((slot_me + i) % SLOTS)
        return 0

    lax.fori_loop(1, SLOTS, wait_other, 0)
    wait_result(SLOTS)
    wait_result(SLOTS + 1)
    parts = SLOTS + 2
    levels = [lrecv[v] for v in range(parts)]
    summit = levels[0]
    for v in range(1, parts):
        summit = jnp.maximum(summit, levels[v])
    shares = [jnp.exp2(level - summit) for level in levels]
    denom = shares[0]
    for v in range(1, parts):
        denom = denom + shares[v]
    row = lax.broadcasted_iota(jnp.int32, (8, HD), 0)
    packed = []
    for first in range(0, parts, 8):
        rows = jnp.zeros((8, HD), F32)
        for v in range(first, min(first + 8, parts)):
            rows = jnp.where(row == v - first, shares[v], rows)
        packed.append(rows / denom)
    packed.append(jnp.zeros((HD - 8 * len(packed), HD), F32))
    share = jnp.transpose(jnp.concatenate(packed, axis=0))[0:BLOCK, :]
    attention = jnp.zeros((BLOCK, HD), F32)
    for v in range(parts):
        attention = attention + nrecv[v].astype(F32) * share[:, v : v + 1]
    attention = attention.astype(BF16)
    flat = jnp.concatenate(
        [attention[g * ROWS : (g + 1) * ROWS, :] for g in range(HEADS)], axis=1
    )

    for k in range(TP):
        copy_w[k].wait()
    for i in (4, 5, 3, 2, 6, 7, 1):
        peer = (t + i) % TP
        psend[i] = jnp.dot(flat, wv[peer], preferred_element_type=F32).astype(BF16)
        copy = remote(
            psend.at[i], precv.at[t], p_send.at[i], p_recv.at[t], {"work": me, "tp": peer}
        )
        copy.start()
        sends.append(copy)
    total = jnp.dot(flat, wv[t], preferred_element_type=F32)
    for i in (1, 7, 2, 6, 3, 5, 4):
        peer = (t + i) % TP
        remote(
            psend.at[i], precv.at[peer], p_send.at[i], p_recv.at[peer], {"work": me, "tp": peer}
        ).wait_recv()
        total = total + precv[peer].astype(F32)
    out_ref[...] = total.astype(BF16)

    for copy in sends:
        copy.wait_send()
    for i in range(DIRECT, PLANES):
        forward(i).wait_send()


def per_device(
    queries, new_keys, new_values, cache_keys, cache_values, lengths, positions, out_weight
):
    vmem = pl.BlockSpec(memory_space=pltpu.VMEM)
    smem = pl.BlockSpec(memory_space=pltpu.SMEM)
    anywhere = pl.BlockSpec(memory_space=pl.ANY)
    dma = pltpu.SemaphoreType.DMA
    out = pl.pallas_call(
        kernel,
        out_shape=jax.ShapeDtypeStruct((ROWS, COLS), BF16),
        in_specs=[smem, smem, vmem, vmem, vmem, anywhere, anywhere, anywhere],
        out_specs=vmem,
        scratch_shapes=[
            pltpu.VMEM((CACHE + NEWPAD, HD), BF16),
            pltpu.VMEM((CACHE + NEWPAD, 2 * HD), BF16),
            pltpu.VMEM((TP, COLS, COLS), BF16),
            pltpu.VMEM((PLANES, 4, BLOCK, HD), BF16),
            pltpu.VMEM((SLOTS + 1, BLOCK, HD), BF16),
            pltpu.VMEM((SLOTS + 2, BLOCK, HD), BF16),
            pltpu.VMEM((SLOTS + 1, 8, HD), F32),
            pltpu.VMEM((SLOTS + 2, 8, HD), F32),
            pltpu.VMEM((CHUNKS, TILE, CHUNK), F32),
            pltpu.VMEM((CHUNKS, TILE, CHUNK), F32),
            pltpu.VMEM((TILE, HD), F32),
            pltpu.VMEM((TILE, HD), F32),
            pltpu.VMEM((TILE, HD), F32),
            pltpu.VMEM((TILE, HD), F32),
            pltpu.VMEM((TILE, 2 * HD), F32),
            pltpu.VMEM((2, 2 * BLOCK, HD), F32),
            pltpu.VMEM((2, 2 * BLOCK, HD), F32),
            pltpu.VMEM((PLANES, 2 * BLOCK, HD), BF16),
            pltpu.VMEM((PLANES, 2 * BLOCK, HD), BF16),
            pltpu.VMEM((PLANES, 2 * BLOCK, HD), F32),
            pltpu.VMEM((PLANES, 2 * BLOCK, HD), F32),
            pltpu.VMEM((TP, ROWS, COLS), BF16),
            pltpu.VMEM((TP, ROWS, COLS), BF16),
            dma((2 + TP,)),
            dma((SLOTS,)),
            dma((SLOTS,)),
            dma((2 * DIRECT,)),
            dma((SLOTS,)),
            dma((PLANES,)),
            dma((PLANES,)),
            dma((SLOTS + 1,)),
            dma((SLOTS + 2,)),
            dma((SLOTS + 1,)),
            dma((SLOTS + 2,)),
            dma((PLANES,)),
            dma((PLANES,)),
            dma((PLANES,)),
            dma((PLANES,)),
            dma((TP,)),
            dma((TP,)),
        ],
        compiler_params=pltpu.CompilerParams(
            collective_id=0, has_side_effects=True, vmem_limit_bytes=58 * 1024 * 1024
        ),
    )(
        positions.reshape(ROWS),
        lengths,
        queries[0].transpose(1, 0, 2).reshape(BLOCK, HD),
        new_keys.reshape(ROWS, HD),
        new_values.reshape(ROWS, HD),
        cache_keys.reshape(CACHE, HD),
        cache_values.reshape(CACHE, HD),
        out_weight,
    )
    return out[None]


def solution(mesh):
    in_specs = (
        P("work", None, "tp", None),
        P("work", None, "tp", None),
        P("work", None, "tp", None),
        P("work", None, "tp", None),
        P("work", None, "tp", None),
        P("work"),
        P("work", None),
        P("tp", None),
    )
    out_specs = P("work", None, "tp")
    return jax.shard_map(
        per_device, mesh=mesh, in_specs=in_specs, out_specs=out_specs, check_vma=False
    )
```

```python
import math

import jax
import jax.numpy as jnp
from jax import lax
from jax.experimental import pallas as pl
from jax.experimental.pallas import tpu as pltpu
from jax.sharding import PartitionSpec as P

MESH = pl.DeviceIdType.MESH
F32 = jnp.float32
BF16 = jnp.bfloat16

HEADS = 5
ROWS = 16
HD = 128
CACHE = 4096
PAIR = 2 * CACHE
NEWPAD = 128
BLOCK = HEADS * ROWS
TILE = 2 * BLOCK
CHUNK = 1024
CHUNKS = PAIR // CHUNK
TP = 8
COLS = 640
PLANES = 8
ORDER = (0, 2, 6, 3, 5, 4, 1, 7)
EARLY = 2
LATE = 6
SLOTS = PLANES + 1 + PLANES - LATE
LEAST = 1024
STEP = 512

SCALE2 = HD**-0.5 * math.log2(math.e)
LOG_BASE = math.log(1000000.0)
NT = (((1,), (1,)), ((), ()))


def cos_sin(angle):
    turn = jnp.floor(angle * (2.0 / math.pi) + 0.5)
    rest = angle - turn * 1.5703125
    rest = rest - turn * 4.837512969970703125e-4
    rest = rest - turn * 7.54978995489188e-8
    z = rest * rest
    sine = rest + rest * z * ((-1.9515295891e-4 * z + 8.3321608736e-3) * z - 1.6666654611e-1)
    cosine = 1.0 - 0.5 * z + z * z * (
        (2.443315711809948e-5 * z - 1.388731625493765e-3) * z + 4.166664568298827e-2
    )
    quarter = turn.astype(jnp.int32) & 3
    odd = (quarter & 1) == 1
    c = jnp.where(odd, sine, cosine)
    s = jnp.where(odd, cosine, sine)
    c = jnp.where((quarter == 1) | (quarter == 2), -c, c)
    s = jnp.where(quarter >= 2, -s, s)
    return c, s


def kernel(
    pos_ref, len_ref, q_ref, nk_ref, nv_ref, ck_ref, cv_ref, w_ref, out_ref,
    kall, vaug, wv, qbuf, nsend, nrecv, lsend, lrecv, s0, s1, t0, t1, mx0, mx1, acc,
    nkeep, lkeep, xn_out, xn_in, xl_out, xl_in, psend, precv, lens,
    loc_sem, pair_send, pair_recv, q_send, q_recv, n_send, n_recv, l_send, l_recv,
    xn_send, xn_recv, xl_send, xl_recv, p_send, p_recv,
):
    me = lax.axis_index("work")
    t = lax.axis_index("tp")
    z = me // 4
    yh = (me // 2) % 2
    c = me % 2

    def device(d, hi, core):
        return {"work": 4 * ((z + d + PLANES) % PLANES) + 2 * hi + core, "tp": t}

    def remote(src, dst, send, recv, to):
        return pltpu.make_async_remote_copy(
            src, dst, send, recv, device_id=to, device_id_type=MESH
        )

    sibling = device(0, yh, 1 - c)
    partner = device(0, 1 - yh, c)

    copy_k = pltpu.make_async_copy(ck_ref, kall.at[pl.ds(0, CACHE)], loc_sem.at[0])
    copy_v = pltpu.make_async_copy(
        cv_ref, vaug.at[pl.ds(0, CACHE), pl.ds(0, HD)], loc_sem.at[1]
    )
    copy_k.start()
    copy_v.start()

    barrier = pltpu.get_barrier_semaphore()
    others = [sibling, partner]
    others += [device(d, yh, c) for d in range(1, PLANES)]
    direct = {ORDER[1], PLANES - ORDER[1]}
    for d in ORDER[LATE:]:
        direct |= {d, PLANES - d}
    others += [device(d, 1 - yh, c) for d in sorted(direct)]
    others += [{"work": me, "tp": (t + i) % TP} for i in range(1, TP)]
    for to in others:
        pl.semaphore_signal(barrier, inc=1, device_id=to, device_id_type=MESH)

    lane = lax.broadcasted_iota(jnp.int32, (ROWS, HD), 1)
    place = pos_ref[0] + lax.broadcasted_iota(jnp.int32, (ROWS, HD), 0)
    ladder = (lane % (HD // 2)).astype(F32) * (2.0 / HD)
    angle = place.astype(F32) * jnp.exp(ladder * -LOG_BASE)
    cosine, sine = cos_sin(angle)
    sine = jnp.where(lane < HD // 2, -sine, sine)

    def rotated(x):
        x = x.astype(F32)
        return (x * cosine + pltpu.roll(x, HD // 2, 1) * sine).astype(BF16)

    for g in range(HEADS):
        qbuf[0, 0, g * ROWS : (g + 1) * ROWS, :] = rotated(q_ref[g * ROWS : (g + 1) * ROWS, :])
    kall[PAIR : PAIR + ROWS, :] = rotated(nk_ref[...])
    lens[0] = jnp.full((8, HD), len_ref[0], jnp.int32).astype(F32)

    pl.semaphore_wait(barrier, len(others))

    sends = []

    def start(copy):
        copy.start()
        sends.append(copy)

    def send_q(i, rel):
        k = 2 * i + rel
        to = device(-ORDER[i], yh if rel == 0 else 1 - yh, c)
        start(remote(qbuf.at[0, 0], qbuf.at[i, rel], q_send.at[k], q_recv.at[k], to))

    pair = [
        remote(src, dst, pair_send.at[k], pair_recv.at[k], sibling)
        for k, (src, dst) in enumerate(
            (
                (lens.at[0], lens.at[1]),
                (kall.at[pl.ds(PAIR, ROWS)], kall.at[pl.ds(PAIR + ROWS, ROWS)]),
                (nv_ref, vaug.at[pl.ds(PAIR + ROWS, ROWS), pl.ds(0, HD)]),
                (ck_ref, kall.at[pl.ds(CACHE, CACHE)]),
                (cv_ref, vaug.at[pl.ds(CACHE, CACHE), pl.ds(0, HD)]),
            )
        )
    ]
    send_q(0, 1)
    for copy in pair[:4]:
        start(copy)
    for i in range(1, PLANES):
        for rel in range(2 if i < EARLY else 1):
            send_q(i, rel)
    start(pair[4])

    copy_w = [
        pltpu.make_async_copy(w_ref.at[:, pl.ds(k * COLS, COLS)], wv.at[k], loc_sem.at[2 + k])
        for k in range(TP)
    ]
    for k in range(TP):
        copy_w[k].start()

    kall[PAIR + 2 * ROWS :, :] = jnp.zeros((NEWPAD - 2 * ROWS, HD), BF16)
    vaug[PAIR : PAIR + ROWS, 0:HD] = nv_ref[...]
    vaug[PAIR + 2 * ROWS :, 0:HD] = jnp.zeros((NEWPAD - 2 * ROWS, HD), BF16)
    vaug[PAIR:, HD:] = jnp.ones((NEWPAD, HD), BF16)

    def live_rows(base, j):
        rows = lax.broadcasted_iota(jnp.int32, (STEP, HD), 0) + j * STEP
        return jnp.where(rows.astype(F32) < lens[base // CACHE, 0:1, :], 1.0, 0.0).astype(BF16)

    def mask_keys(base):
        first = kall[base : base + 16, :].astype(F32)[0:1, :]
        first = jnp.broadcast_to(first, (STEP, HD)).astype(BF16)

        def body(j, _):
            live = live_rows(base, j)
            rows = pl.ds(base + pl.multiple_of(j * STEP, STEP), STEP)
            kall[rows, :] = kall[rows, :] * live + first * (1.0 - live)
            return 0

        lax.fori_loop(LEAST // STEP, CACHE // STEP, body, 0)

    def mask_values(base):
        vaug[base : base + LEAST, HD:] = jnp.ones((LEAST, HD), BF16)

        def body(j, _):
            live = live_rows(base, j)
            rows = pl.ds(base + pl.multiple_of(j * STEP, STEP), STEP)
            vaug[rows, 0:HD] = vaug[rows, 0:HD] * live
            vaug[rows, HD:] = live
            return 0

        lax.fori_loop(LEAST // STEP, CACHE // STEP, body, 0)

    def wait_q(i, rel):
        k = 2 * i + rel
        remote(qbuf.at[0, 0], qbuf.at[i, rel], q_send.at[k], q_recv.at[k], partner).wait_recv()

    def pass_on(i):
        wait_q(i, 0)
        if i >= EARLY:
            k = 2 * i + 1
            start(remote(qbuf.at[i, 0], qbuf.at[i, 1], q_send.at[k], q_recv.at[k], partner))

    def queries_of(i):
        wait_q(i, 1)
        return qbuf[i].reshape(TILE, HD)

    def scores(q, j, s_ref, mx):
        s = lax.dot_general(
            q, kall[j * CHUNK : (j + 1) * CHUNK, :], NT, preferred_element_type=F32
        )
        s_ref[j] = s
        top = mx[...]
        for u in range(CHUNK // HD):
            top = jnp.maximum(top, s[:, u * HD : (u + 1) * HD])
        mx[...] = top

    def new_scores(i, q, t_ref, mx):
        row = lax.broadcasted_iota(jnp.int32, (TILE, HD), 0)
        col = lax.broadcasted_iota(jnp.int32, (TILE, HD), 1)
        r, r2 = row & 15, col & 15
        seen = (r2 >> 2) < (r >> 2)
        if i == 0:
            own = (row < BLOCK) & (col < ROWS)
            seen = seen | (own & ((r2 >> 2) == (r >> 2)) & (r2 <= r))
        s = lax.dot_general(q, kall[PAIR:, :], NT, preferred_element_type=F32)
        s = jnp.where(seen & (col < 2 * ROWS), s, -1e30)
        t_ref[...] = s
        mx[...] = s

    def close_max(mx):
        mx[...] = jnp.broadcast_to(jnp.max(mx[...], axis=1, keepdims=True), (TILE, HD))

    def weights(s, top):
        return jnp.exp2((s - top) * SCALE2).astype(BF16)

    def values(j, s_ref, mx):
        top = mx[...]
        p = jnp.concatenate(
            [weights(s_ref[j, :, u * HD : (u + 1) * HD], top) for u in range(CHUNK // HD)], axis=1
        )
        v = vaug[j * CHUNK : (j + 1) * CHUNK, :]
        acc[...] += jnp.dot(p, v, preferred_element_type=F32)

    def new_values(t_ref, mx):
        p = weights(t_ref[...], mx[...])
        acc[...] = jnp.dot(p, vaug[PAIR:, :], preferred_element_type=F32)

    def as_row(level):
        flat = jnp.concatenate([level, jnp.zeros((HD - BLOCK, HD), F32)], axis=0)
        return jnp.transpose(flat)[0:8, :]

    def as_columns(row):
        return jnp.transpose(jnp.concatenate([row] * (HD // 8), axis=0))[0:BLOCK, :]

    def send_result(slot, n, level, to):
        nsend[slot] = n.astype(BF16)
        lsend[slot] = as_row(level)
        for src, dst, send, recv in (
            (nsend, nrecv, n_send, n_recv), (lsend, lrecv, l_send, l_recv)
        ):
            start(remote(src.at[slot], dst.at[slot], send.at[slot], recv.at[slot], to))

    def exchange(i):
        return [
            remote(xn_out.at[i], xn_in.at[i], xn_send.at[i], xn_recv.at[i], partner),
            remote(xl_out.at[i], xl_in.at[i], xl_send.at[i], xl_recv.at[i], partner),
        ]

    def finish(i, mx):
        total = acc[:, HD:]
        n = acc[:, :HD] / total
        level = mx[...] * SCALE2 + jnp.log(total) * math.log2(math.e)
        if i == 0:
            nrecv[0] = n[:BLOCK].astype(BF16)
            lrecv[0] = as_row(level[:BLOCK])
            send_result(PLANES, n[BLOCK:], level[BLOCK:], partner)
        elif i >= LATE:
            send_result(i, n[:BLOCK], level[:BLOCK], device(ORDER[i], yh, c))
            send_result(
                PLANES + 1 + i - LATE, n[BLOCK:], level[BLOCK:], device(ORDER[i], 1 - yh, c)
            )
        else:
            xn_out[i] = n[BLOCK:].astype(BF16)
            xl_out[i] = as_row(level[BLOCK:])
            for copy in exchange(i):
                start(copy)
            nkeep[i % 2] = n[:BLOCK]
            lkeep[i % 2] = level[:BLOCK]

    def merge(i):
        for copy in exchange(i):
            copy.wait_recv()
        level, other = lkeep[i % 2], as_columns(xl_in[i])
        top = jnp.maximum(level, other)
        a, b = jnp.exp2(level - top), jnp.exp2(other - top)
        total = a + b
        n = (nkeep[i % 2] * a + xn_in[i].astype(F32) * b) / total
        level = top + jnp.log(total) * math.log2(math.e)
        send_result(i, n, level, device(ORDER[i], yh, c))

    s_refs, t_refs, mx_refs = (s0, s1), (t0, t1), (mx0, mx1)

    copy_k.wait()
    mask_keys(0)
    for copy in pair[:3]:
        copy.wait_recv()
    q = queries_of(0)
    new_scores(0, q, t0, mx0)
    for j in range(CHUNKS // 2):
        scores(q, j, s0, mx0)
    copy_v.wait()
    mask_values(0)
    pass_on(1)
    pair[3].wait_recv()
    mask_keys(CACHE)
    for j in range(CHUNKS // 2, CHUNKS):
        scores(q, j, s0, mx0)
    close_max(mx0)

    for i in range(PLANES):
        now, later = i % 2, (i + 1) % 2
        more = i + 1 < PLANES
        if i + 2 < PLANES:
            pass_on(i + 2)
        if more:
            q = queries_of(i + 1)
            new_scores(i + 1, q, t_refs[later], mx_refs[later])
        new_values(t_refs[now], mx_refs[now])
        for j in range(CHUNKS):
            if i == 0 and j == CHUNKS // 2:
                pair[4].wait_recv()
                mask_values(CACHE)
            if more:
                scores(q, j, s_refs[later], mx_refs[later])
            values(j, s_refs[now], mx_refs[now])
        if more:
            close_max(mx_refs[later])
        finish(i, mx_refs[now])
        if 1 <= i - 1 < LATE:
            merge(i - 1)

    for slot in range(1, SLOTS):
        for src, dst, send, recv in (
            (nsend, nrecv, n_send, n_recv), (lsend, lrecv, l_send, l_recv)
        ):
            remote(
                src.at[slot], dst.at[slot], send.at[slot], recv.at[slot], partner
            ).wait_recv()
    levels = [lrecv[v] for v in range(SLOTS)]
    summit = levels[0]
    for v in range(1, SLOTS):
        summit = jnp.maximum(summit, levels[v])
    shares = [jnp.exp2(level - summit) for level in levels]
    denom = shares[0]
    for v in range(1, SLOTS):
        denom = denom + shares[v]
    row = lax.broadcasted_iota(jnp.int32, (8, HD), 0)
    packed = []
    for first in range(0, SLOTS, 8):
        rows = jnp.zeros((8, HD), F32)
        for v in range(first, min(first + 8, SLOTS)):
            rows = jnp.where(row == v - first, shares[v], rows)
        packed.append(rows / denom)
    packed.append(jnp.zeros((HD - 8 * len(packed), HD), F32))
    share = jnp.transpose(jnp.concatenate(packed, axis=0))[0:BLOCK, :]
    attention = jnp.zeros((BLOCK, HD), F32)
    for v in range(SLOTS):
        attention = attention + nrecv[v].astype(F32) * share[:, v : v + 1]
    attention = attention.astype(BF16)
    flat = jnp.concatenate(
        [attention[g * ROWS : (g + 1) * ROWS, :] for g in range(HEADS)], axis=1
    )

    for k in range(TP):
        copy_w[k].wait()

    def columns(i):
        peer = (t + i) % TP
        return remote(
            psend.at[i], precv.at[i], p_send.at[i], p_recv.at[i], {"work": me, "tp": peer}
        )

    for i in (4, 5, 3, 2, 6, 7, 1):
        psend[i] = jnp.dot(flat, wv[(t + i) % TP], preferred_element_type=F32).astype(BF16)
        start(columns(i))
    total = jnp.dot(flat, wv[t], preferred_element_type=F32)
    for i in (4, 5, 3, 2, 6, 7, 1):
        columns(i).wait_recv()
        total = total + precv[i].astype(F32)
    out_ref[...] = total.astype(BF16)

    for copy in sends:
        copy.wait_send()


def per_device(
    queries, new_keys, new_values, cache_keys, cache_values, lengths, positions, out_weight
):
    vmem = pl.BlockSpec(memory_space=pltpu.VMEM)
    smem = pl.BlockSpec(memory_space=pltpu.SMEM)
    anywhere = pl.BlockSpec(memory_space=pl.ANY)
    dma = pltpu.SemaphoreType.DMA
    out = pl.pallas_call(
        kernel,
        out_shape=jax.ShapeDtypeStruct((ROWS, COLS), BF16),
        in_specs=[smem, smem, vmem, vmem, vmem, anywhere, anywhere, anywhere],
        out_specs=vmem,
        scratch_shapes=[
            pltpu.VMEM((PAIR + NEWPAD, HD), BF16),
            pltpu.VMEM((PAIR + NEWPAD, 2 * HD), BF16),
            pltpu.VMEM((TP, COLS, COLS), BF16),
            pltpu.VMEM((PLANES, 2, BLOCK, HD), BF16),
            pltpu.VMEM((SLOTS, BLOCK, HD), BF16),
            pltpu.VMEM((SLOTS, BLOCK, HD), BF16),
            pltpu.VMEM((SLOTS, 8, HD), F32),
            pltpu.VMEM((SLOTS, 8, HD), F32),
            pltpu.VMEM((CHUNKS, TILE, CHUNK), F32),
            pltpu.VMEM((CHUNKS, TILE, CHUNK), F32),
            pltpu.VMEM((TILE, HD), F32),
            pltpu.VMEM((TILE, HD), F32),
            pltpu.VMEM((TILE, HD), F32),
            pltpu.VMEM((TILE, HD), F32),
            pltpu.VMEM((TILE, 2 * HD), F32),
            pltpu.VMEM((2, BLOCK, HD), F32),
            pltpu.VMEM((2, BLOCK, HD), F32),
            pltpu.VMEM((LATE, BLOCK, HD), BF16),
            pltpu.VMEM((LATE, BLOCK, HD), BF16),
            pltpu.VMEM((LATE, 8, HD), F32),
            pltpu.VMEM((LATE, 8, HD), F32),
            pltpu.VMEM((TP, ROWS, COLS), BF16),
            pltpu.VMEM((TP, ROWS, COLS), BF16),
            pltpu.VMEM((2, 8, HD), F32),
            dma((2 + TP,)),
            dma((5,)),
            dma((5,)),
            dma((2 * PLANES,)),
            dma((2 * PLANES,)),
            dma((SLOTS,)),
            dma((SLOTS,)),
            dma((SLOTS,)),
            dma((SLOTS,)),
            dma((LATE,)),
            dma((LATE,)),
            dma((LATE,)),
            dma((LATE,)),
            dma((TP,)),
            dma((TP,)),
        ],
        compiler_params=pltpu.CompilerParams(
            collective_id=0, has_side_effects=True, vmem_limit_bytes=58 * 1024 * 1024
        ),
    )(
        positions.reshape(ROWS),
        lengths,
        queries[0].transpose(1, 0, 2).reshape(BLOCK, HD),
        new_keys.reshape(ROWS, HD),
        new_values.reshape(ROWS, HD),
        cache_keys.reshape(CACHE, HD),
        cache_values.reshape(CACHE, HD),
        out_weight,
    )
    return out[None]


def solution(mesh):
    in_specs = (
        P("work", None, "tp", None),
        P("work", None, "tp", None),
        P("work", None, "tp", None),
        P("work", None, "tp", None),
        P("work", None, "tp", None),
        P("work"),
        P("work", None),
        P("tp", None),
    )
    out_specs = P("work", None, "tp")
    return jax.shard_map(
        per_device, mesh=mesh, in_specs=in_specs, out_specs=out_specs, check_vma=False
    )
```

```python
import math

import jax
import jax.numpy as jnp
from jax import lax
from jax.experimental import pallas as pl
from jax.experimental.pallas import tpu as pltpu
from jax.sharding import PartitionSpec as P

MESH = pl.DeviceIdType.MESH
F32 = jnp.float32
BF16 = jnp.bfloat16

HEADS = 5
ROWS = 16
HD = 128
CACHE = 4096
PAIR = 2 * CACHE
NEWPAD = 128
BLOCK = HEADS * ROWS
TILE = 2 * BLOCK
CHUNK = 2048
CHUNKS = PAIR // CHUNK
TP = 8
COLS = 640
PLANES = 8
ORDER = (0, 2, 6, 3, 5, 4, 1, 7)
CODE = sum(d * PLANES**i for i, d in enumerate(ORDER))
SLOTS = 2 * PLANES
LEAST = 1024
STEP = 512

SCALE2 = HD**-0.5 * math.log2(math.e)
LOG_BASE = math.log(1000000.0)
NT = (((1,), (1,)), ((), ()))


def cos_sin(angle):
    turn = jnp.floor(angle * (2.0 / math.pi) + 0.5)
    rest = angle - turn * 1.5703125
    rest = rest - turn * 4.837512969970703125e-4
    rest = rest - turn * 7.54978995489188e-8
    z = rest * rest
    sine = rest + rest * z * ((-1.9515295891e-4 * z + 8.3321608736e-3) * z - 1.6666654611e-1)
    cosine = 1.0 - 0.5 * z + z * z * (
        (2.443315711809948e-5 * z - 1.388731625493765e-3) * z + 4.166664568298827e-2
    )
    quarter = turn.astype(jnp.int32) & 3
    odd = (quarter & 1) == 1
    c = jnp.where(odd, sine, cosine)
    s = jnp.where(odd, cosine, sine)
    c = jnp.where((quarter == 1) | (quarter == 2), -c, c)
    s = jnp.where(quarter >= 2, -s, s)
    return c, s


def kernel(
    pos_ref, len_ref, q_ref, nk_ref, nv_ref, ck_ref, cv_ref, w_ref, out_ref,
    kall, vaug, wv, qbuf, nsend, nrecv, lsend, lrecv, s0, s1, t0, t1, mx0, mx1, acc,
    flat, psend, precv, lens,
    loc_sem, pair_send, pair_recv, q_send, q_recv, n_send, n_recv, l_send, l_recv,
    p_send, p_recv,
):
    me = lax.axis_index("work")
    t = lax.axis_index("tp")
    z = me // 4
    yh = (me // 2) % 2
    c = me % 2

    def device(d, rel, core):
        hi = (yh + rel) % 2
        return {"work": 4 * ((z + d + PLANES) % PLANES) + 2 * hi + core, "tp": t}

    def remote(src, dst, send, recv, to):
        return pltpu.make_async_remote_copy(
            src, dst, send, recv, device_id=to, device_id_type=MESH
        )

    sibling = device(0, 0, 1 - c)
    partner = device(0, 1, c)

    copy_k = pltpu.make_async_copy(ck_ref, kall.at[pl.ds(0, CACHE)], loc_sem.at[0])
    copy_v = pltpu.make_async_copy(
        cv_ref, vaug.at[pl.ds(0, CACHE), pl.ds(0, HD)], loc_sem.at[1]
    )
    copy_k.start()
    copy_v.start()

    barrier = pltpu.get_barrier_semaphore()

    def signal(to):
        pl.semaphore_signal(barrier, inc=1, device_id=to, device_id_type=MESH)

    def greet(i, _):
        signal(device(i // 2, i % 2, c))
        return 0

    lax.fori_loop(1, SLOTS, greet, 0)
    signal(sibling)

    def greet_tp(i, _):
        signal({"work": me, "tp": (t + i) % TP})
        return 0

    lax.fori_loop(1, TP, greet_tp, 0)

    lane = lax.broadcasted_iota(jnp.int32, (ROWS, HD), 1)
    place = pos_ref[0] + lax.broadcasted_iota(jnp.int32, (ROWS, HD), 0)
    ladder = (lane % (HD // 2)).astype(F32) * (2.0 / HD)
    angle = place.astype(F32) * jnp.exp(ladder * -LOG_BASE)
    cosine, sine = cos_sin(angle)
    sine = jnp.where(lane < HD // 2, -sine, sine)

    def rotated(x):
        x = x.astype(F32)
        return (x * cosine + pltpu.roll(x, HD // 2, 1) * sine).astype(BF16)

    for g in range(HEADS):
        qbuf[0, g * ROWS : (g + 1) * ROWS, :] = rotated(q_ref[g * ROWS : (g + 1) * ROWS, :])
    kall[PAIR : PAIR + ROWS, :] = rotated(nk_ref[...])
    lens[0] = jnp.full((8, HD), len_ref[0], jnp.int32).astype(F32)

    pl.semaphore_wait(barrier, SLOTS - 1 + 1 + TP - 1)

    def query_copy(k, d, rel):
        return remote(qbuf.at[0], qbuf.at[k], q_send.at[k], q_recv.at[k], device(-d, rel, c))

    pair = [
        remote(src, dst, pair_send.at[k], pair_recv.at[k], sibling)
        for k, (src, dst) in enumerate(
            (
                (lens.at[0], lens.at[1]),
                (kall.at[pl.ds(PAIR, ROWS)], kall.at[pl.ds(PAIR + ROWS, ROWS)]),
                (nv_ref, vaug.at[pl.ds(PAIR + ROWS, ROWS), pl.ds(0, HD)]),
                (ck_ref, kall.at[pl.ds(CACHE, CACHE)]),
                (cv_ref, vaug.at[pl.ds(CACHE, CACHE), pl.ds(0, HD)]),
            )
        )
    ]
    query_copy(1, 0, 1).start()
    for copy in pair[:4]:
        copy.start()

    def send_queries(i, code):
        for rel in range(2):
            query_copy(2 * i + rel, code % PLANES, rel).start()
        return code // PLANES

    lax.fori_loop(1, PLANES, send_queries, CODE // PLANES)
    pair[4].start()

    def weight_copy(k):
        return pltpu.make_async_copy(
            w_ref.at[:, pl.ds(pl.multiple_of(k * COLS, HD), COLS)], wv.at[k], loc_sem.at[2 + k]
        )

    def start_weights(k, _):
        weight_copy(k).start()
        return 0

    lax.fori_loop(0, TP, start_weights, 0)

    kall[PAIR + 2 * ROWS :, :] = jnp.zeros((NEWPAD - 2 * ROWS, HD), BF16)
    vaug[PAIR : PAIR + ROWS, 0:HD] = nv_ref[...]
    vaug[PAIR + 2 * ROWS :, 0:HD] = jnp.zeros((NEWPAD - 2 * ROWS, HD), BF16)
    vaug[PAIR:, HD:] = jnp.ones((NEWPAD, HD), BF16)

    def live_rows(base, j):
        rows = lax.broadcasted_iota(jnp.int32, (STEP, HD), 0) + j * STEP
        return jnp.where(rows.astype(F32) < lens[base // CACHE, 0:1, :], 1.0, 0.0).astype(BF16)

    def mask_keys(base):
        first = kall[base : base + 16, :].astype(F32)[0:1, :]
        first = jnp.broadcast_to(first, (STEP, HD)).astype(BF16)

        def body(j, _):
            live = live_rows(base, j)
            rows = pl.ds(base + pl.multiple_of(j * STEP, STEP), STEP)
            kall[rows, :] = kall[rows, :] * live + first * (1.0 - live)
            return 0

        lax.fori_loop(LEAST // STEP, CACHE // STEP, body, 0)

    def mask_values(base):
        def ones(j, _):
            rows = pl.ds(base + pl.multiple_of(j * STEP, STEP), STEP)
            vaug[rows, HD:] = jnp.ones((STEP, HD), BF16)
            return 0

        lax.fori_loop(0, LEAST // STEP, ones, 0)

        def body(j, _):
            live = live_rows(base, j)
            rows = pl.ds(base + pl.multiple_of(j * STEP, STEP), STEP)
            vaug[rows, 0:HD] = vaug[rows, 0:HD] * live
            vaug[rows, HD:] = live
            return 0

        lax.fori_loop(LEAST // STEP, CACHE // STEP, body, 0)

    def wait_queries(i):
        for rel in range(2):
            query_copy(2 * i + rel, 0, 1).wait_recv()

    def queries_of(i):
        return qbuf[pl.ds(2 * i, 2)].reshape(TILE, HD)

    def chunk(j):
        return pl.ds(pl.multiple_of(j * CHUNK, CHUNK), CHUNK)

    def scores(q, j, s_ref, mx):
        s = lax.dot_general(q, kall[chunk(j), :], NT, preferred_element_type=F32)
        s_ref[j] = s
        top = mx[...]
        for u in range(CHUNK // HD):
            top = jnp.maximum(top, s[:, u * HD : (u + 1) * HD])
        mx[...] = top

    def new_scores(first, q, t_ref, mx):
        row = lax.broadcasted_iota(jnp.int32, (TILE, HD), 0)
        col = lax.broadcasted_iota(jnp.int32, (TILE, HD), 1)
        r, r2 = row & 15, col & 15
        seen = (r2 >> 2) < (r >> 2)
        if first:
            own = (row < BLOCK) & (col < ROWS)
            seen = seen | (own & ((r2 >> 2) == (r >> 2)) & (r2 <= r))
        s = lax.dot_general(q, kall[PAIR:, :], NT, preferred_element_type=F32)
        s = jnp.where(seen & (col < 2 * ROWS), s, -1e30)
        t_ref[...] = s
        mx[...] = s

    def close_max(mx):
        mx[...] = jnp.broadcast_to(jnp.max(mx[...], axis=1, keepdims=True), (TILE, HD))

    def weights(s, top):
        return jnp.exp2((s - top) * SCALE2).astype(BF16)

    def chunk_weights(j, s_ref, mx):
        top = mx[...]
        return jnp.concatenate(
            [weights(s_ref[j, :, u * HD : (u + 1) * HD], top) for u in range(CHUNK // HD)], axis=1
        )

    def add_values(j, p):
        acc[...] += jnp.dot(p, vaug[chunk(j), :], preferred_element_type=F32)

    def new_values(t_ref, mx):
        p = weights(t_ref[...], mx[...])
        acc[...] = jnp.dot(p, vaug[PAIR:, :], preferred_element_type=F32)

    def as_row(level):
        padded = jnp.concatenate([level, jnp.zeros((HD - BLOCK, HD), F32)], axis=0)
        return jnp.transpose(padded)[0:8, :]

    def result_copies(k, d, rel):
        to = device(d, rel, c)
        return [
            remote(src.at[k], dst.at[k], send.at[k], recv.at[k], to)
            for src, dst, send, recv in (
                (nsend, nrecv, n_send, n_recv), (lsend, lrecv, l_send, l_recv)
            )
        ]

    def finish(i, d, mx, maybe_first):
        total = acc[:, HD:]
        n = (acc[:, :HD] / total).astype(BF16)
        level = mx[...] * SCALE2 + jnp.log(total) * math.log2(math.e)
        for rel in range(2):
            part = slice(rel * BLOCK, (rel + 1) * BLOCK)
            k = 2 * i + rel
            nsend[k] = n[part]
            lsend[k] = as_row(level[part])
            copies = result_copies(k, d, rel)
            if maybe_first and rel == 0:
                @pl.when(i > 0)
                def _():
                    for copy in copies:
                        copy.start()

                @pl.when(i == 0)
                def _():
                    nrecv[0] = n[:BLOCK]
                    lrecv[0] = lsend[0]
            else:
                for copy in copies:
                    copy.start()

    copy_k.wait()
    mask_keys(0)
    for copy in pair[:3]:
        copy.wait_recv()
    query_copy(1, 0, 1).wait_recv()
    q = queries_of(0)
    new_scores(True, q, t0, mx0)

    def first_scores(j, _):
        @pl.when(j == CHUNKS // 2)
        def _():
            pair[3].wait_recv()
            mask_keys(CACHE)

        scores(q, j, s0, mx0)
        return 0

    lax.fori_loop(0, CHUNKS, first_scores, 0)
    close_max(mx0)
    copy_v.wait()
    mask_values(0)

    def both(i, s_now, t_now, mx_now, s_later, t_later, mx_later, maybe_first):
        wait_queries(i + 1)
        q = queries_of(i + 1)
        new_scores(False, q, t_later, mx_later)
        new_values(t_now, mx_now)

        def body(j, _):
            if maybe_first:
                @pl.when((i == 0) & (j == CHUNKS // 2))
                def _():
                    pair[4].wait_recv()
                    mask_values(CACHE)

            p = chunk_weights(j, s_now, mx_now)
            scores(q, j, s_later, mx_later)
            add_values(j, p)
            return 0

        lax.fori_loop(0, CHUNKS, body, 0)
        close_max(mx_later)

    def two_tiles(k, code):
        i = 2 * k
        both(i, s0, t0, mx0, s1, t1, mx1, True)
        finish(i, code % PLANES, mx0, True)
        code = code // PLANES

        @pl.when(i + 2 < PLANES)
        def _():
            both(i + 1, s1, t1, mx1, s0, t0, mx0, False)

        @pl.when(i + 2 == PLANES)
        def _():
            new_values(t1, mx1)

            def body(j, _):
                add_values(j, chunk_weights(j, s1, mx1))
                return 0

            lax.fori_loop(0, CHUNKS, body, 0)

        finish(i + 1, code % PLANES, mx1, False)
        return code // PLANES

    lax.fori_loop(0, PLANES // 2, two_tiles, CODE)

    def wait_result(k, _):
        for copy in result_copies(k, 0, 1):
            copy.wait_recv()
        return 0

    lax.fori_loop(1, SLOTS, wait_result, 0)
    levels = [lrecv[v] for v in range(SLOTS)]
    summit = levels[0]
    for v in range(1, SLOTS):
        summit = jnp.maximum(summit, levels[v])
    shares = [jnp.exp2(level - summit) for level in levels]
    denom = shares[0]
    for v in range(1, SLOTS):
        denom = denom + shares[v]
    row = lax.broadcasted_iota(jnp.int32, (8, HD), 0)
    packed = []
    for first in range(0, SLOTS, 8):
        rows = jnp.zeros((8, HD), F32)
        for v in range(first, first + 8):
            rows = jnp.where(row == v - first, shares[v], rows)
        packed.append(rows / denom)
    packed.append(jnp.zeros((HD - SLOTS, HD), F32))
    share = jnp.transpose(jnp.concatenate(packed, axis=0))[0:BLOCK, :]
    attention = jnp.zeros((BLOCK, HD), F32)
    for v in range(SLOTS):
        attention = attention + nrecv[v].astype(F32) * share[:, v : v + 1]
    attention = attention.astype(BF16)
    for g in range(HEADS):
        flat[:, g * HD : (g + 1) * HD] = attention[g * ROWS : (g + 1) * ROWS, :]

    def wait_weights(k, _):
        weight_copy(k).wait()
        return 0

    lax.fori_loop(0, TP, wait_weights, 0)

    def columns(i):
        return remote(
            psend.at[i], precv.at[i], p_send.at[i], p_recv.at[i],
            {"work": me, "tp": (t + i) % TP},
        )

    def project(k, _):
        i = 1 + (k + 2) % (TP - 1)
        psend[i] = jnp.dot(
            flat[...], wv[(t + i) % TP], preferred_element_type=F32
        ).astype(BF16)
        columns(i).start()
        return 0

    lax.fori_loop(0, TP - 1, project, 0)
    total = jnp.dot(flat[...], wv[t], preferred_element_type=F32)

    def gather(i, total):
        columns(i).wait_recv()
        return total + precv[i].astype(F32)

    out_ref[...] = lax.fori_loop(1, TP, gather, total).astype(BF16)

    for copy in pair:
        copy.wait_send()

    def sent(k, _):
        query_copy(k, 0, 1).wait_send()
        for copy in result_copies(k, 0, 1):
            copy.wait_send()
        return 0

    lax.fori_loop(1, SLOTS, sent, 0)

    def sent_columns(i, _):
        columns(i).wait_send()
        return 0

    lax.fori_loop(1, TP, sent_columns, 0)


def per_device(
    queries, new_keys, new_values, cache_keys, cache_values, lengths, positions, out_weight
):
    vmem = pl.BlockSpec(memory_space=pltpu.VMEM)
    smem = pl.BlockSpec(memory_space=pltpu.SMEM)
    anywhere = pl.BlockSpec(memory_space=pl.ANY)
    dma = pltpu.SemaphoreType.DMA
    out = pl.pallas_call(
        kernel,
        out_shape=jax.ShapeDtypeStruct((ROWS, COLS), BF16),
        in_specs=[smem, smem, vmem, vmem, vmem, anywhere, anywhere, anywhere],
        out_specs=vmem,
        scratch_shapes=[
            pltpu.VMEM((PAIR + NEWPAD, HD), BF16),
            pltpu.VMEM((PAIR + NEWPAD, 2 * HD), BF16),
            pltpu.VMEM((TP, COLS, COLS), BF16),
            pltpu.VMEM((SLOTS, BLOCK, HD), BF16),
            pltpu.VMEM((SLOTS, BLOCK, HD), BF16),
            pltpu.VMEM((SLOTS, BLOCK, HD), BF16),
            pltpu.VMEM((SLOTS, 8, HD), F32),
            pltpu.VMEM((SLOTS, 8, HD), F32),
            pltpu.VMEM((CHUNKS, TILE, CHUNK), F32),
            pltpu.VMEM((CHUNKS, TILE, CHUNK), F32),
            pltpu.VMEM((TILE, HD), F32),
            pltpu.VMEM((TILE, HD), F32),
            pltpu.VMEM((TILE, HD), F32),
            pltpu.VMEM((TILE, HD), F32),
            pltpu.VMEM((TILE, 2 * HD), F32),
            pltpu.VMEM((ROWS, HEADS * HD), BF16),
            pltpu.VMEM((TP, ROWS, COLS), BF16),
            pltpu.VMEM((TP, ROWS, COLS), BF16),
            pltpu.VMEM((2, 8, HD), F32),
            dma((2 + TP,)),
            dma((5,)),
            dma((5,)),
            dma((SLOTS,)),
            dma((SLOTS,)),
            dma((SLOTS,)),
            dma((SLOTS,)),
            dma((SLOTS,)),
            dma((SLOTS,)),
            dma((TP,)),
            dma((TP,)),
        ],
        compiler_params=pltpu.CompilerParams(
            collective_id=0, has_side_effects=True, vmem_limit_bytes=58 * 1024 * 1024
        ),
    )(
        positions.reshape(ROWS),
        lengths,
        queries[0].transpose(1, 0, 2).reshape(BLOCK, HD),
        new_keys.reshape(ROWS, HD),
        new_values.reshape(ROWS, HD),
        cache_keys.reshape(CACHE, HD),
        cache_values.reshape(CACHE, HD),
        out_weight,
    )
    return out[None]


def solution(mesh):
    in_specs = (
        P("work", None, "tp", None),
        P("work", None, "tp", None),
        P("work", None, "tp", None),
        P("work", None, "tp", None),
        P("work", None, "tp", None),
        P("work"),
        P("work", None),
        P("tp", None),
    )
    out_specs = P("work", None, "tp")
    return jax.shard_map(
        per_device, mesh=mesh, in_specs=in_specs, out_specs=out_specs, check_vma=False
    )
```

```python
import math

import jax
import jax.numpy as jnp
from jax import lax
from jax.experimental import pallas as pl
from jax.experimental.pallas import tpu as pltpu
from jax.sharding import PartitionSpec as P

MESH = pl.DeviceIdType.MESH
F32 = jnp.float32
BF16 = jnp.bfloat16

HEADS = 5
ROWS = 16
HD = 128
CACHE = 4096
PAIR = 2 * CACHE
NEWPAD = 128
BLOCK = HEADS * ROWS
TILE = 2 * BLOCK
CHUNK = 2048
CHUNKS = PAIR // CHUNK
TP = 8
COLS = 640
PLANES = 8
ORDER = (0, 2, 6, 3, 5, 4, 1, 7)
CODE = sum(d * PLANES**i for i, d in enumerate(ORDER))
SLOTS = 2 * PLANES
LEAST = 1024
STEP = 512

SCALE2 = HD**-0.5 * math.log2(math.e)
LOG_BASE = math.log(1000000.0)
NT = (((1,), (1,)), ((), ()))


def cos_sin(angle):
    turn = jnp.floor(angle * (2.0 / math.pi) + 0.5)
    rest = angle - turn * 1.5703125
    rest = rest - turn * 4.837512969970703125e-4
    rest = rest - turn * 7.54978995489188e-8
    z = rest * rest
    sine = rest + rest * z * ((-1.9515295891e-4 * z + 8.3321608736e-3) * z - 1.6666654611e-1)
    cosine = 1.0 - 0.5 * z + z * z * (
        (2.443315711809948e-5 * z - 1.388731625493765e-3) * z + 4.166664568298827e-2
    )
    quarter = turn.astype(jnp.int32) & 3
    odd = (quarter & 1) == 1
    c = jnp.where(odd, sine, cosine)
    s = jnp.where(odd, cosine, sine)
    c = jnp.where((quarter == 1) | (quarter == 2), -c, c)
    s = jnp.where(quarter >= 2, -s, s)
    return c, s


def kernel(
    pos_ref, len_ref, q_ref, nk_ref, nv_ref, ck_ref, cv_ref, w_ref, out_ref,
    kall, vaug, wv, qbuf, nsend, nrecv, lsend, lrecv, s0, s1, t0, t1, mx0, mx1, acc,
    flat, psend, precv, lens,
    loc_sem, pair_send, pair_recv, q_send, q_recv, n_send, n_recv, l_send, l_recv,
    p_send, p_recv,
):
    me = lax.axis_index("work")
    t = lax.axis_index("tp")
    z = me // 4
    yh = (me // 2) % 2
    c = me % 2

    def device(d, rel, core):
        hi = (yh + rel) % 2
        return {"work": 4 * ((z + d + PLANES) % PLANES) + 2 * hi + core, "tp": t}

    def remote(src, dst, send, recv, to):
        return pltpu.make_async_remote_copy(
            src, dst, send, recv, device_id=to, device_id_type=MESH
        )

    sibling = device(0, 0, 1 - c)
    partner = device(0, 1, c)

    copy_k = pltpu.make_async_copy(ck_ref, kall.at[pl.ds(0, CACHE)], loc_sem.at[0])
    copy_v = pltpu.make_async_copy(
        cv_ref, vaug.at[pl.ds(0, CACHE), pl.ds(0, HD)], loc_sem.at[1]
    )
    copy_k.start()
    copy_v.start()

    barrier = pltpu.get_barrier_semaphore()

    def signal(to):
        pl.semaphore_signal(barrier, inc=1, device_id=to, device_id_type=MESH)

    def greet(i, _):
        signal(device(i // 2, i % 2, c))
        return 0

    lax.fori_loop(1, SLOTS, greet, 0)
    signal(sibling)

    def greet_tp(i, _):
        signal({"work": me, "tp": (t + i) % TP})
        return 0

    lax.fori_loop(1, TP, greet_tp, 0)

    lane = lax.broadcasted_iota(jnp.int32, (ROWS, HD), 1)
    place = pos_ref[0] + lax.broadcasted_iota(jnp.int32, (ROWS, HD), 0)
    ladder = (lane % (HD // 2)).astype(F32) * (2.0 / HD)
    angle = place.astype(F32) * jnp.exp(ladder * -LOG_BASE)
    cosine, sine = cos_sin(angle)
    sine = jnp.where(lane < HD // 2, -sine, sine)

    def rotated(x):
        x = x.astype(F32)
        return (x * cosine + pltpu.roll(x, HD // 2, 1) * sine).astype(BF16)

    for g in range(HEADS):
        qbuf[0, g * ROWS : (g + 1) * ROWS, :] = rotated(q_ref[g * ROWS : (g + 1) * ROWS, :])
    kall[PAIR : PAIR + ROWS, :] = rotated(nk_ref[...])
    lens[0] = jnp.full((8, HD), len_ref[0], jnp.int32).astype(F32)

    pl.semaphore_wait(barrier, SLOTS - 1 + 1 + TP - 1)

    def query_copy(k, d, rel):
        return remote(qbuf.at[0], qbuf.at[k], q_send.at[k], q_recv.at[k], device(-d, rel, c))

    pair = [
        remote(src, dst, pair_send.at[k], pair_recv.at[k], sibling)
        for k, (src, dst) in enumerate(
            (
                (lens.at[0], lens.at[1]),
                (kall.at[pl.ds(PAIR, ROWS)], kall.at[pl.ds(PAIR + ROWS, ROWS)]),
                (nv_ref, vaug.at[pl.ds(PAIR + ROWS, ROWS), pl.ds(0, HD)]),
                (ck_ref, kall.at[pl.ds(CACHE, CACHE)]),
                (cv_ref, vaug.at[pl.ds(CACHE, CACHE), pl.ds(0, HD)]),
            )
        )
    ]
    query_copy(1, 0, 1).start()
    for copy in pair[:4]:
        copy.start()

    def send_queries(i, code):
        for rel in range(2):
            query_copy(2 * i + rel, code % PLANES, rel).start()
        return code // PLANES

    lax.fori_loop(1, PLANES, send_queries, CODE // PLANES)
    pair[4].start()

    def weight_copy(k):
        return pltpu.make_async_copy(
            w_ref.at[:, pl.ds(pl.multiple_of(k * COLS, HD), COLS)], wv.at[k], loc_sem.at[2 + k]
        )

    def start_weights(k, _):
        weight_copy(k).start()
        return 0

    lax.fori_loop(0, TP, start_weights, 0)

    kall[PAIR + 2 * ROWS :, :] = jnp.zeros((NEWPAD - 2 * ROWS, HD), BF16)
    vaug[PAIR : PAIR + ROWS, 0:HD] = nv_ref[...]
    vaug[PAIR + 2 * ROWS :, 0:HD] = jnp.zeros((NEWPAD - 2 * ROWS, HD), BF16)
    vaug[PAIR:, HD:] = jnp.ones((NEWPAD, HD), BF16)

    def live_rows(base, j):
        rows = lax.broadcasted_iota(jnp.int32, (STEP, HD), 0) + j * STEP
        return jnp.where(rows.astype(F32) < lens[base // CACHE, 0:1, :], 1.0, 0.0).astype(BF16)

    def mask_keys(base):
        first = kall[base : base + 16, :].astype(F32)[0:1, :]
        first = jnp.broadcast_to(first, (STEP, HD)).astype(BF16)

        def body(j, _):
            live = live_rows(base, j)
            rows = pl.ds(base + pl.multiple_of(j * STEP, STEP), STEP)
            kall[rows, :] = kall[rows, :] * live + first * (1.0 - live)
            return 0

        lax.fori_loop(LEAST // STEP, CACHE // STEP, body, 0)

    def mask_values(base):
        def ones(j, _):
            rows = pl.ds(base + pl.multiple_of(j * STEP, STEP), STEP)
            vaug[rows, HD:] = jnp.ones((STEP, HD), BF16)
            return 0

        lax.fori_loop(0, LEAST // STEP, ones, 0)

        def body(j, _):
            live = live_rows(base, j)
            rows = pl.ds(base + pl.multiple_of(j * STEP, STEP), STEP)
            vaug[rows, 0:HD] = vaug[rows, 0:HD] * live
            vaug[rows, HD:] = live
            return 0

        lax.fori_loop(LEAST // STEP, CACHE // STEP, body, 0)

    def wait_queries(i):
        for rel in range(2):
            query_copy(2 * i + rel, 0, 1).wait_recv()

    def queries_of(i):
        return qbuf[pl.ds(2 * i, 2)].reshape(TILE, HD)

    def chunk(j):
        return pl.ds(pl.multiple_of(j * CHUNK, CHUNK), CHUNK)

    def scores(q, j, s_ref, mx):
        s = lax.dot_general(q, kall[chunk(j), :], NT, preferred_element_type=F32)
        s_ref[j] = s
        top = mx[...]
        for u in range(CHUNK // HD):
            top = jnp.maximum(top, s[:, u * HD : (u + 1) * HD])
        mx[...] = top

    def new_scores(first, q, t_ref, mx):
        row = lax.broadcasted_iota(jnp.int32, (TILE, HD), 0)
        col = lax.broadcasted_iota(jnp.int32, (TILE, HD), 1)
        r, r2 = row & 15, col & 15
        seen = (r2 >> 2) < (r >> 2)
        if first:
            own = (row < BLOCK) & (col < ROWS)
            seen = seen | (own & ((r2 >> 2) == (r >> 2)) & (r2 <= r))
        s = lax.dot_general(q, kall[PAIR:, :], NT, preferred_element_type=F32)
        s = jnp.where(seen & (col < 2 * ROWS), s, -1e30)
        t_ref[...] = s
        mx[...] = s

    def close_max(mx):
        mx[...] = jnp.broadcast_to(jnp.max(mx[...], axis=1, keepdims=True), (TILE, HD))

    def weights(s, top):
        return jnp.exp2(((s - top) * SCALE2).astype(BF16))

    def chunk_weights(j, s_ref, mx):
        top = mx[...]
        return jnp.concatenate(
            [weights(s_ref[j, :, u * HD : (u + 1) * HD], top) for u in range(CHUNK // HD)], axis=1
        )

    def add_values(j, p):
        acc[...] += jnp.dot(p, vaug[chunk(j), :], preferred_element_type=F32)

    def new_values(t_ref, mx):
        p = weights(t_ref[...], mx[...])
        acc[...] = jnp.dot(p, vaug[PAIR:, :], preferred_element_type=F32)

    def as_row(level):
        padded = jnp.concatenate([level, jnp.zeros((HD - BLOCK, HD), F32)], axis=0)
        return jnp.transpose(padded)[0:8, :]

    def result_copies(k, d, rel):
        to = device(d, rel, c)
        return [
            remote(src.at[k], dst.at[k], send.at[k], recv.at[k], to)
            for src, dst, send, recv in (
                (nsend, nrecv, n_send, n_recv), (lsend, lrecv, l_send, l_recv)
            )
        ]

    def finish(i, d, mx, maybe_first):
        total = acc[:, HD:]
        n = (acc[:, :HD] / total).astype(BF16)
        level = mx[...] * SCALE2 + jnp.log(total) * math.log2(math.e)
        for rel in range(2):
            part = slice(rel * BLOCK, (rel + 1) * BLOCK)
            k = 2 * i + rel
            nsend[k] = n[part]
            lsend[k] = as_row(level[part])
            copies = result_copies(k, d, rel)
            if maybe_first and rel == 0:
                @pl.when(i > 0)
                def _():
                    for copy in copies:
                        copy.start()

                @pl.when(i == 0)
                def _():
                    nrecv[0] = n[:BLOCK]
                    lrecv[0] = lsend[0]
            else:
                for copy in copies:
                    copy.start()

    copy_k.wait()
    mask_keys(0)
    for copy in pair[:3]:
        copy.wait_recv()
    query_copy(1, 0, 1).wait_recv()
    q = queries_of(0)
    new_scores(True, q, t0, mx0)

    def first_scores(j, _):
        @pl.when(j == CHUNKS // 2)
        def _():
            pair[3].wait_recv()
            mask_keys(CACHE)

        scores(q, j, s0, mx0)
        return 0

    lax.fori_loop(0, CHUNKS, first_scores, 0)
    close_max(mx0)
    copy_v.wait()
    mask_values(0)

    def both(i, s_now, t_now, mx_now, s_later, t_later, mx_later, maybe_first):
        wait_queries(i + 1)
        q = queries_of(i + 1)
        new_scores(False, q, t_later, mx_later)
        new_values(t_now, mx_now)

        def body(j, _):
            if maybe_first:
                @pl.when((i == 0) & (j == CHUNKS // 2))
                def _():
                    pair[4].wait_recv()
                    mask_values(CACHE)

            p = chunk_weights(j, s_now, mx_now)
            scores(q, j, s_later, mx_later)
            add_values(j, p)
            return 0

        lax.fori_loop(0, CHUNKS, body, 0)
        close_max(mx_later)

    def two_tiles(k, code):
        i = 2 * k
        both(i, s0, t0, mx0, s1, t1, mx1, True)
        finish(i, code % PLANES, mx0, True)
        code = code // PLANES

        @pl.when(i + 2 < PLANES)
        def _():
            both(i + 1, s1, t1, mx1, s0, t0, mx0, False)

        @pl.when(i + 2 == PLANES)
        def _():
            new_values(t1, mx1)

            def body(j, _):
                add_values(j, chunk_weights(j, s1, mx1))
                return 0

            lax.fori_loop(0, CHUNKS, body, 0)

        finish(i + 1, code % PLANES, mx1, False)
        return code // PLANES

    lax.fori_loop(0, PLANES // 2, two_tiles, CODE)

    def wait_result(k, _):
        for copy in result_copies(k, 0, 1):
            copy.wait_recv()
        return 0

    lax.fori_loop(1, SLOTS, wait_result, 0)
    levels = [lrecv[v] for v in range(SLOTS)]
    summit = levels[0]
    for v in range(1, SLOTS):
        summit = jnp.maximum(summit, levels[v])
    shares = [jnp.exp2(level - summit) for level in levels]
    denom = shares[0]
    for v in range(1, SLOTS):
        denom = denom + shares[v]
    row = lax.broadcasted_iota(jnp.int32, (8, HD), 0)
    packed = []
    for first in range(0, SLOTS, 8):
        rows = jnp.zeros((8, HD), F32)
        for v in range(first, first + 8):
            rows = jnp.where(row == v - first, shares[v], rows)
        packed.append(rows / denom)
    packed.append(jnp.zeros((HD - SLOTS, HD), F32))
    share = jnp.transpose(jnp.concatenate(packed, axis=0))[0:BLOCK, :]
    attention = jnp.zeros((BLOCK, HD), F32)
    for v in range(SLOTS):
        attention = attention + nrecv[v].astype(F32) * share[:, v : v + 1]
    attention = attention.astype(BF16)
    for g in range(HEADS):
        flat[:, g * HD : (g + 1) * HD] = attention[g * ROWS : (g + 1) * ROWS, :]

    def wait_weights(k, _):
        weight_copy(k).wait()
        return 0

    lax.fori_loop(0, TP, wait_weights, 0)

    def columns(i):
        return remote(
            psend.at[i], precv.at[i], p_send.at[i], p_recv.at[i],
            {"work": me, "tp": (t + i) % TP},
        )

    def project(k, _):
        i = 1 + (k + 2) % (TP - 1)
        psend[i] = jnp.dot(
            flat[...], wv[(t + i) % TP], preferred_element_type=F32
        ).astype(BF16)
        columns(i).start()
        return 0

    lax.fori_loop(0, TP - 1, project, 0)
    total = jnp.dot(flat[...], wv[t], preferred_element_type=F32)

    def gather(i, total):
        columns(i).wait_recv()
        return total + precv[i].astype(F32)

    out_ref[...] = lax.fori_loop(1, TP, gather, total).astype(BF16)

    for copy in pair:
        copy.wait_send()

    def sent(k, _):
        query_copy(k, 0, 1).wait_send()
        for copy in result_copies(k, 0, 1):
            copy.wait_send()
        return 0

    lax.fori_loop(1, SLOTS, sent, 0)

    def sent_columns(i, _):
        columns(i).wait_send()
        return 0

    lax.fori_loop(1, TP, sent_columns, 0)


def per_device(
    queries, new_keys, new_values, cache_keys, cache_values, lengths, positions, out_weight
):
    vmem = pl.BlockSpec(memory_space=pltpu.VMEM)
    smem = pl.BlockSpec(memory_space=pltpu.SMEM)
    anywhere = pl.BlockSpec(memory_space=pl.ANY)
    dma = pltpu.SemaphoreType.DMA
    out = pl.pallas_call(
        kernel,
        out_shape=jax.ShapeDtypeStruct((ROWS, COLS), BF16),
        in_specs=[smem, smem, vmem, vmem, vmem, anywhere, anywhere, anywhere],
        out_specs=vmem,
        scratch_shapes=[
            pltpu.VMEM((PAIR + NEWPAD, HD), BF16),
            pltpu.VMEM((PAIR + NEWPAD, 2 * HD), BF16),
            pltpu.VMEM((TP, COLS, COLS), BF16),
            pltpu.VMEM((SLOTS, BLOCK, HD), BF16),
            pltpu.VMEM((SLOTS, BLOCK, HD), BF16),
            pltpu.VMEM((SLOTS, BLOCK, HD), BF16),
            pltpu.VMEM((SLOTS, 8, HD), F32),
            pltpu.VMEM((SLOTS, 8, HD), F32),
            pltpu.VMEM((CHUNKS, TILE, CHUNK), F32),
            pltpu.VMEM((CHUNKS, TILE, CHUNK), F32),
            pltpu.VMEM((TILE, HD), F32),
            pltpu.VMEM((TILE, HD), F32),
            pltpu.VMEM((TILE, HD), F32),
            pltpu.VMEM((TILE, HD), F32),
            pltpu.VMEM((TILE, 2 * HD), F32),
            pltpu.VMEM((ROWS, HEADS * HD), BF16),
            pltpu.VMEM((TP, ROWS, COLS), BF16),
            pltpu.VMEM((TP, ROWS, COLS), BF16),
            pltpu.VMEM((2, 8, HD), F32),
            dma((2 + TP,)),
            dma((5,)),
            dma((5,)),
            dma((SLOTS,)),
            dma((SLOTS,)),
            dma((SLOTS,)),
            dma((SLOTS,)),
            dma((SLOTS,)),
            dma((SLOTS,)),
            dma((TP,)),
            dma((TP,)),
        ],
        compiler_params=pltpu.CompilerParams(
            collective_id=0, has_side_effects=True, vmem_limit_bytes=58 * 1024 * 1024
        ),
    )(
        positions.reshape(ROWS),
        lengths,
        queries[0].transpose(1, 0, 2).reshape(BLOCK, HD),
        new_keys.reshape(ROWS, HD),
        new_values.reshape(ROWS, HD),
        cache_keys.reshape(CACHE, HD),
        cache_values.reshape(CACHE, HD),
        out_weight,
    )
    return out[None]


def solution(mesh):
    in_specs = (
        P("work", None, "tp", None),
        P("work", None, "tp", None),
        P("work", None, "tp", None),
        P("work", None, "tp", None),
        P("work", None, "tp", None),
        P("work"),
        P("work", None),
        P("tp", None),
    )
    out_specs = P("work", None, "tp")
    return jax.shard_map(
        per_device, mesh=mesh, in_specs=in_specs, out_specs=out_specs, check_vma=False
    )
```

```python
import math

import jax
import jax.numpy as jnp
from jax import lax
from jax.experimental import pallas as pl
from jax.experimental.pallas import tpu as pltpu
from jax.sharding import PartitionSpec as P

MESH = pl.DeviceIdType.MESH
F32 = jnp.float32
BF16 = jnp.bfloat16

HEADS = 5
ROWS = 16
HD = 128
CACHE = 4096
PAIR = 2 * CACHE
NEWPAD = 128
BLOCK = HEADS * ROWS
TILE = 2 * BLOCK
CHUNK = 2048
CHUNKS = PAIR // CHUNK
TP = 8
COLS = 640
PLANES = 8
ORDER = (0, 2, 6, 3, 5, 4, 1, 7)
CODE = sum(d * PLANES**i for i, d in enumerate(ORDER))
SLOTS = 2 * PLANES
LEAST = 1024
STEP = 512

SCALE2 = HD**-0.5 * math.log2(math.e)
LOG_BASE = math.log(1000000.0)
NT = (((1,), (1,)), ((), ()))


def cos_sin(angle):
    turn = jnp.floor(angle * (2.0 / math.pi) + 0.5)
    rest = angle - turn * 1.5703125
    rest = rest - turn * 4.837512969970703125e-4
    rest = rest - turn * 7.54978995489188e-8
    z = rest * rest
    sine = rest + rest * z * ((-1.9515295891e-4 * z + 8.3321608736e-3) * z - 1.6666654611e-1)
    cosine = 1.0 - 0.5 * z + z * z * (
        (2.443315711809948e-5 * z - 1.388731625493765e-3) * z + 4.166664568298827e-2
    )
    quarter = turn.astype(jnp.int32) & 3
    odd = (quarter & 1) == 1
    c = jnp.where(odd, sine, cosine)
    s = jnp.where(odd, cosine, sine)
    c = jnp.where((quarter == 1) | (quarter == 2), -c, c)
    s = jnp.where(quarter >= 2, -s, s)
    return c, s


def exchange_kernel(
    pos_ref, len_ref, q_ref, nk_ref, nv_ref, ck_ref, cv_ref,
    qbuf, newk, newv, lens, ksib, vsib,
    pair_send, pair_recv, q_send, q_recv,
):
    me = lax.axis_index("work")
    t = lax.axis_index("tp")
    z = me // 4
    yh = (me // 2) % 2
    c = me % 2

    def device(d, rel, core):
        hi = (yh + rel) % 2
        return {"work": 4 * ((z + d + PLANES) % PLANES) + 2 * hi + core, "tp": t}

    def remote(src, dst, send, recv, to):
        return pltpu.make_async_remote_copy(
            src, dst, send, recv, device_id=to, device_id_type=MESH
        )

    sibling = device(0, 0, 1 - c)

    barrier = pltpu.get_barrier_semaphore()

    def signal(to):
        pl.semaphore_signal(barrier, inc=1, device_id=to, device_id_type=MESH)

    def greet(i, _):
        signal(device(i // 2, i % 2, c))
        return 0

    lax.fori_loop(1, SLOTS, greet, 0)
    signal(sibling)

    lane = lax.broadcasted_iota(jnp.int32, (ROWS, HD), 1)
    place = pos_ref[0] + lax.broadcasted_iota(jnp.int32, (ROWS, HD), 0)
    ladder = (lane % (HD // 2)).astype(F32) * (2.0 / HD)
    angle = place.astype(F32) * jnp.exp(ladder * -LOG_BASE)
    cosine, sine = cos_sin(angle)
    sine = jnp.where(lane < HD // 2, -sine, sine)

    def rotated(x):
        x = x.astype(F32)
        return (x * cosine + pltpu.roll(x, HD // 2, 1) * sine).astype(BF16)

    for g in range(HEADS):
        qbuf[0, g * ROWS : (g + 1) * ROWS, :] = rotated(q_ref[g * ROWS : (g + 1) * ROWS, :])
    newk[0:ROWS, :] = rotated(nk_ref[...])
    newv[0:ROWS, :] = nv_ref[...]
    lens[0] = jnp.full((8, HD), len_ref[0], jnp.int32).astype(F32)

    pl.semaphore_wait(barrier, SLOTS - 1 + 1)

    def query_copy(k, d, rel):
        return remote(qbuf.at[0], qbuf.at[k], q_send.at[k], q_recv.at[k], device(-d, rel, c))

    pair = [
        remote(src, dst, pair_send.at[k], pair_recv.at[k], sibling)
        for k, (src, dst) in enumerate(
            (
                (lens.at[0], lens.at[1]),
                (newk.at[pl.ds(0, ROWS)], newk.at[pl.ds(ROWS, ROWS)]),
                (nv_ref, newv.at[pl.ds(ROWS, ROWS)]),
                (ck_ref, ksib),
                (cv_ref, vsib),
            )
        )
    ]
    query_copy(1, 0, 1).start()
    for copy in pair[:4]:
        copy.start()

    def send_queries(i, code):
        for rel in range(2):
            query_copy(2 * i + rel, code % PLANES, rel).start()
        return code // PLANES

    lax.fori_loop(1, PLANES, send_queries, CODE // PLANES)
    pair[4].start()
    for copy in pair:
        copy.wait()

    def wait_queries(k, _):
        query_copy(k, 0, 1).wait()
        return 0

    lax.fori_loop(1, SLOTS, wait_queries, 0)


def attention_kernel(
    qbuf, newk, newv, lens, ck_ref, cv_ref, ksib, vsib, nsend, lsend,
    kall, vaug, s0, s1, t0, t1, mx0, mx1, acc, loc_sem,
):
    copies = [
        pltpu.make_async_copy(src, dst, loc_sem.at[k])
        for k, (src, dst) in enumerate(
            (
                (ck_ref, kall.at[pl.ds(0, CACHE)]),
                (ksib, kall.at[pl.ds(CACHE, CACHE)]),
                (cv_ref, vaug.at[pl.ds(0, CACHE), pl.ds(0, HD)]),
                (vsib, vaug.at[pl.ds(CACHE, CACHE), pl.ds(0, HD)]),
            )
        )
    ]
    for copy in copies:
        copy.start()
    kall[PAIR : PAIR + 2 * ROWS, :] = newk[...]
    kall[PAIR + 2 * ROWS :, :] = jnp.zeros((NEWPAD - 2 * ROWS, HD), BF16)
    vaug[PAIR : PAIR + 2 * ROWS, 0:HD] = newv[...]
    vaug[PAIR + 2 * ROWS :, 0:HD] = jnp.zeros((NEWPAD - 2 * ROWS, HD), BF16)
    vaug[PAIR:, HD:] = jnp.ones((NEWPAD, HD), BF16)

    def live_rows(base, j):
        rows = lax.broadcasted_iota(jnp.int32, (STEP, HD), 0) + j * STEP
        return jnp.where(rows.astype(F32) < lens[base // CACHE, 0:1, :], 1.0, 0.0).astype(BF16)

    def mask_keys(base):
        first = kall[base : base + 16, :].astype(F32)[0:1, :]
        first = jnp.broadcast_to(first, (STEP, HD)).astype(BF16)

        def body(j, _):
            live = live_rows(base, j)
            rows = pl.ds(base + pl.multiple_of(j * STEP, STEP), STEP)
            kall[rows, :] = kall[rows, :] * live + first * (1.0 - live)
            return 0

        lax.fori_loop(LEAST // STEP, CACHE // STEP, body, 0)

    def mask_values(base):
        def ones(j, _):
            rows = pl.ds(base + pl.multiple_of(j * STEP, STEP), STEP)
            vaug[rows, HD:] = jnp.ones((STEP, HD), BF16)
            return 0

        lax.fori_loop(0, LEAST // STEP, ones, 0)

        def body(j, _):
            live = live_rows(base, j)
            rows = pl.ds(base + pl.multiple_of(j * STEP, STEP), STEP)
            vaug[rows, 0:HD] = vaug[rows, 0:HD] * live
            vaug[rows, HD:] = live
            return 0

        lax.fori_loop(LEAST // STEP, CACHE // STEP, body, 0)

    def queries_of(i):
        return qbuf[pl.ds(2 * i, 2)].reshape(TILE, HD)

    def chunk(j):
        return pl.ds(pl.multiple_of(j * CHUNK, CHUNK), CHUNK)

    def scores(q, j, s_ref, mx):
        s = lax.dot_general(q, kall[chunk(j), :], NT, preferred_element_type=F32)
        s_ref[j] = s
        top = mx[...]
        for u in range(CHUNK // HD):
            top = jnp.maximum(top, s[:, u * HD : (u + 1) * HD])
        mx[...] = top

    def new_scores(first, q, t_ref, mx):
        row = lax.broadcasted_iota(jnp.int32, (TILE, HD), 0)
        col = lax.broadcasted_iota(jnp.int32, (TILE, HD), 1)
        r, r2 = row & 15, col & 15
        seen = (r2 >> 2) < (r >> 2)
        if first:
            own = (row < BLOCK) & (col < ROWS)
            seen = seen | (own & ((r2 >> 2) == (r >> 2)) & (r2 <= r))
        s = lax.dot_general(q, kall[PAIR:, :], NT, preferred_element_type=F32)
        s = jnp.where(seen & (col < 2 * ROWS), s, -1e30)
        t_ref[...] = s
        mx[...] = s

    def close_max(mx):
        mx[...] = jnp.broadcast_to(jnp.max(mx[...], axis=1, keepdims=True), (TILE, HD))

    def weights(s, top):
        return jnp.exp2((s - top) * SCALE2).astype(BF16)

    def chunk_weights(j, s_ref, mx):
        top = mx[...]
        return jnp.concatenate(
            [weights(s_ref[j, :, u * HD : (u + 1) * HD], top) for u in range(CHUNK // HD)], axis=1
        )

    def add_values(j, p):
        acc[...] += jnp.dot(p, vaug[chunk(j), :], preferred_element_type=F32)

    def new_values(t_ref, mx):
        p = weights(t_ref[...], mx[...])
        acc[...] = jnp.dot(p, vaug[PAIR:, :], preferred_element_type=F32)

    def as_row(level):
        padded = jnp.concatenate([level, jnp.zeros((HD - BLOCK, HD), F32)], axis=0)
        return jnp.transpose(padded)[0:8, :]

    def finish(i, mx):
        total = acc[:, HD:]
        n = (acc[:, :HD] / total).astype(BF16)
        level = mx[...] * SCALE2 + jnp.log(total) * math.log2(math.e)
        for rel in range(2):
            part = slice(rel * BLOCK, (rel + 1) * BLOCK)
            k = 2 * i + rel
            nsend[k] = n[part]
            lsend[k] = as_row(level[part])

    copies[0].wait()
    mask_keys(0)
    copies[1].wait()
    mask_keys(CACHE)
    q = queries_of(0)
    new_scores(True, q, t0, mx0)

    def first_scores(j, _):
        scores(q, j, s0, mx0)
        return 0

    lax.fori_loop(0, CHUNKS, first_scores, 0)
    close_max(mx0)
    copies[2].wait()
    mask_values(0)
    copies[3].wait()
    mask_values(CACHE)

    def both(i, s_now, t_now, mx_now, s_later, t_later, mx_later):
        q = queries_of(i + 1)
        new_scores(False, q, t_later, mx_later)
        new_values(t_now, mx_now)

        def body(j, _):
            p = chunk_weights(j, s_now, mx_now)
            scores(q, j, s_later, mx_later)
            add_values(j, p)
            return 0

        lax.fori_loop(0, CHUNKS, body, 0)
        close_max(mx_later)

    def two_tiles(k, _):
        i = 2 * k
        both(i, s0, t0, mx0, s1, t1, mx1)
        finish(i, mx0)

        @pl.when(i + 2 < PLANES)
        def _():
            both(i + 1, s1, t1, mx1, s0, t0, mx0)

        @pl.when(i + 2 == PLANES)
        def _():
            new_values(t1, mx1)

            def body(j, _):
                add_values(j, chunk_weights(j, s1, mx1))
                return 0

            lax.fori_loop(0, CHUNKS, body, 0)

        finish(i + 1, mx1)
        return 0

    lax.fori_loop(0, PLANES // 2, two_tiles, 0)


def combine_kernel(
    nsend, lsend, w_ref, out_ref,
    nrecv, lrecv, wv, flat, psend, precv,
    loc_sem, n_send, n_recv, l_send, l_recv, p_send, p_recv,
):
    me = lax.axis_index("work")
    t = lax.axis_index("tp")
    z = me // 4
    yh = (me // 2) % 2
    c = me % 2

    def device(d, rel, core):
        hi = (yh + rel) % 2
        return {"work": 4 * ((z + d + PLANES) % PLANES) + 2 * hi + core, "tp": t}

    def remote(src, dst, send, recv, to):
        return pltpu.make_async_remote_copy(
            src, dst, send, recv, device_id=to, device_id_type=MESH
        )

    sibling = device(0, 0, 1 - c)

    barrier = pltpu.get_barrier_semaphore()

    def signal(to):
        pl.semaphore_signal(barrier, inc=1, device_id=to, device_id_type=MESH)

    def greet(i, _):
        signal(device(i // 2, i % 2, c))
        return 0

    lax.fori_loop(1, SLOTS, greet, 0)

    def greet_tp(i, _):
        signal({"work": me, "tp": (t + i) % TP})
        return 0

    lax.fori_loop(1, TP, greet_tp, 0)

    def weight_copy(k):
        return pltpu.make_async_copy(
            w_ref.at[:, pl.ds(pl.multiple_of(k * COLS, HD), COLS)], wv.at[k], loc_sem.at[k]
        )

    def start_weights(k, _):
        weight_copy(k).start()
        return 0

    lax.fori_loop(0, TP, start_weights, 0)
    pl.semaphore_wait(barrier, SLOTS - 1 + TP - 1)

    def result_copies(k, d, rel):
        to = device(d, rel, c)
        return [
            remote(src.at[k], dst.at[k], send.at[k], recv.at[k], to)
            for src, dst, send, recv in (
                (nsend, nrecv, n_send, n_recv), (lsend, lrecv, l_send, l_recv)
            )
        ]

    def send_results(i, code):
        for rel in range(2):
            for copy in result_copies(2 * i + rel, code % PLANES, rel):
                copy.start()
        return code // PLANES

    for copy in result_copies(1, 0, 1):
        copy.start()
    lax.fori_loop(1, PLANES, send_results, CODE // PLANES)
    nrecv[0] = nsend[0]
    lrecv[0] = lsend[0]

    def wait_result(k, _):
        for copy in result_copies(k, 0, 1):
            copy.wait_recv()
        return 0

    lax.fori_loop(1, SLOTS, wait_result, 0)
    levels = [lrecv[v] for v in range(SLOTS)]
    summit = levels[0]
    for v in range(1, SLOTS):
        summit = jnp.maximum(summit, levels[v])
    shares = [jnp.exp2(level - summit) for level in levels]
    denom = shares[0]
    for v in range(1, SLOTS):
        denom = denom + shares[v]
    row = lax.broadcasted_iota(jnp.int32, (8, HD), 0)
    packed = []
    for first in range(0, SLOTS, 8):
        rows = jnp.zeros((8, HD), F32)
        for v in range(first, first + 8):
            rows = jnp.where(row == v - first, shares[v], rows)
        packed.append(rows / denom)
    packed.append(jnp.zeros((HD - SLOTS, HD), F32))
    share = jnp.transpose(jnp.concatenate(packed, axis=0))[0:BLOCK, :]
    attention = jnp.zeros((BLOCK, HD), F32)
    for v in range(SLOTS):
        attention = attention + nrecv[v].astype(F32) * share[:, v : v + 1]
    attention = attention.astype(BF16)
    for g in range(HEADS):
        flat[:, g * HD : (g + 1) * HD] = attention[g * ROWS : (g + 1) * ROWS, :]

    def wait_weights(k, _):
        weight_copy(k).wait()
        return 0

    lax.fori_loop(0, TP, wait_weights, 0)

    def columns(i):
        return remote(
            psend.at[i], precv.at[i], p_send.at[i], p_recv.at[i],
            {"work": me, "tp": (t + i) % TP},
        )

    def project(k, _):
        i = 1 + (k + 2) % (TP - 1)
        psend[i] = jnp.dot(
            flat[...], wv[(t + i) % TP], preferred_element_type=F32
        ).astype(BF16)
        columns(i).start()
        return 0

    lax.fori_loop(0, TP - 1, project, 0)
    total = jnp.dot(flat[...], wv[t], preferred_element_type=F32)

    def gather(i, total):
        columns(i).wait_recv()
        return total + precv[i].astype(F32)

    out_ref[...] = lax.fori_loop(1, TP, gather, total).astype(BF16)

    def sent(k, _):
        for copy in result_copies(k, 0, 1):
            copy.wait_send()
        return 0

    lax.fori_loop(1, SLOTS, sent, 0)

    def sent_columns(i, _):
        columns(i).wait_send()
        return 0

    lax.fori_loop(1, TP, sent_columns, 0)


def per_device(
    queries, new_keys, new_values, cache_keys, cache_values, lengths, positions, out_weight
):
    vmem = pl.BlockSpec(memory_space=pltpu.VMEM)
    smem = pl.BlockSpec(memory_space=pltpu.SMEM)
    anywhere = pl.BlockSpec(memory_space=pl.ANY)
    dma = pltpu.SemaphoreType.DMA
    ck = cache_keys.reshape(CACHE, HD)
    cv = cache_values.reshape(CACHE, HD)
    cache = jax.ShapeDtypeStruct((CACHE, HD), BF16)
    qall, newk, newv, lens, ksib, vsib = pl.pallas_call(
        exchange_kernel,
        out_shape=[
            jax.ShapeDtypeStruct((SLOTS, BLOCK, HD), BF16),
            jax.ShapeDtypeStruct((2 * ROWS, HD), BF16),
            jax.ShapeDtypeStruct((2 * ROWS, HD), BF16),
            jax.ShapeDtypeStruct((2, 8, HD), F32),
            cache,
            cache,
        ],
        in_specs=[smem, smem, vmem, vmem, vmem, anywhere, anywhere],
        out_specs=[vmem, vmem, vmem, vmem, anywhere, anywhere],
        scratch_shapes=[dma((5,)), dma((5,)), dma((SLOTS,)), dma((SLOTS,))],
        compiler_params=pltpu.CompilerParams(
            collective_id=0, has_side_effects=True, vmem_limit_bytes=58 * 1024 * 1024
        ),
    )(
        positions.reshape(ROWS),
        lengths,
        queries[0].transpose(1, 0, 2).reshape(BLOCK, HD),
        new_keys.reshape(ROWS, HD),
        new_values.reshape(ROWS, HD),
        ck,
        cv,
    )
    n, level = pl.pallas_call(
        attention_kernel,
        out_shape=[
            jax.ShapeDtypeStruct((SLOTS, BLOCK, HD), BF16),
            jax.ShapeDtypeStruct((SLOTS, 8, HD), F32),
        ],
        in_specs=[vmem, vmem, vmem, vmem, anywhere, anywhere, anywhere, anywhere],
        out_specs=[vmem, vmem],
        scratch_shapes=[
            pltpu.VMEM((PAIR + NEWPAD, HD), BF16),
            pltpu.VMEM((PAIR + NEWPAD, 2 * HD), BF16),
            pltpu.VMEM((CHUNKS, TILE, CHUNK), F32),
            pltpu.VMEM((CHUNKS, TILE, CHUNK), F32),
            pltpu.VMEM((TILE, HD), F32),
            pltpu.VMEM((TILE, HD), F32),
            pltpu.VMEM((TILE, HD), F32),
            pltpu.VMEM((TILE, HD), F32),
            pltpu.VMEM((TILE, 2 * HD), F32),
            dma((4,)),
        ],
        compiler_params=pltpu.CompilerParams(vmem_limit_bytes=58 * 1024 * 1024),
    )(qall, newk, newv, lens, ck, cv, ksib, vsib)
    out = pl.pallas_call(
        combine_kernel,
        out_shape=jax.ShapeDtypeStruct((ROWS, COLS), BF16),
        in_specs=[vmem, vmem, anywhere],
        out_specs=vmem,
        scratch_shapes=[
            pltpu.VMEM((SLOTS, BLOCK, HD), BF16),
            pltpu.VMEM((SLOTS, 8, HD), F32),
            pltpu.VMEM((TP, COLS, COLS), BF16),
            pltpu.VMEM((ROWS, HEADS * HD), BF16),
            pltpu.VMEM((TP, ROWS, COLS), BF16),
            pltpu.VMEM((TP, ROWS, COLS), BF16),
            dma((TP,)),
            dma((SLOTS,)),
            dma((SLOTS,)),
            dma((SLOTS,)),
            dma((SLOTS,)),
            dma((TP,)),
            dma((TP,)),
        ],
        compiler_params=pltpu.CompilerParams(
            collective_id=1, has_side_effects=True, vmem_limit_bytes=58 * 1024 * 1024
        ),
    )(n, level, out_weight)
    return out[None]


def solution(mesh):
    in_specs = (
        P("work", None, "tp", None),
        P("work", None, "tp", None),
        P("work", None, "tp", None),
        P("work", None, "tp", None),
        P("work", None, "tp", None),
        P("work"),
        P("work", None),
        P("tp", None),
    )
    out_specs = P("work", None, "tp")
    return jax.shard_map(
        per_device, mesh=mesh, in_specs=in_specs, out_specs=out_specs, check_vma=False
    )
```

```python
import math

import jax
import jax.numpy as jnp
from jax import lax
from jax.experimental import pallas as pl
from jax.experimental.pallas import tpu as pltpu
from jax.sharding import PartitionSpec as P

MESH = pl.DeviceIdType.MESH
F32 = jnp.float32
BF16 = jnp.bfloat16

HEADS = 5
ROWS = 16
HD = 128
CACHE = 4096
PAIR = 2 * CACHE
NEWPAD = 128
BLOCK = HEADS * ROWS
GROUP = 2
PARTS = 2 * GROUP
TILE = PARTS * BLOCK
CHUNK = 2048
CHUNKS = PAIR // CHUNK
TP = 8
COLS = 640
PLANES = 8
TILES = PLANES // GROUP
ORDER = (0, 1, 3, 5, 4, 2, 6, 7)
CODE = sum(d * PLANES**i for i, d in enumerate(ORDER))
SLOTS = 2 * PLANES
LEAST = 1024
STEP = 512

SCALE2 = HD**-0.5 * math.log2(math.e)
LOG_BASE = math.log(1000000.0)
NT = (((1,), (1,)), ((), ()))


def cos_sin(angle):
    turn = jnp.floor(angle * (2.0 / math.pi) + 0.5)
    rest = angle - turn * 1.5703125
    rest = rest - turn * 4.837512969970703125e-4
    rest = rest - turn * 7.54978995489188e-8
    z = rest * rest
    sine = rest + rest * z * ((-1.9515295891e-4 * z + 8.3321608736e-3) * z - 1.6666654611e-1)
    cosine = 1.0 - 0.5 * z + z * z * (
        (2.443315711809948e-5 * z - 1.388731625493765e-3) * z + 4.166664568298827e-2
    )
    quarter = turn.astype(jnp.int32) & 3
    odd = (quarter & 1) == 1
    c = jnp.where(odd, sine, cosine)
    s = jnp.where(odd, cosine, sine)
    c = jnp.where((quarter == 1) | (quarter == 2), -c, c)
    s = jnp.where(quarter >= 2, -s, s)
    return c, s


def kernel(
    pos_ref, len_ref, q_ref, nk_ref, nv_ref, ck_ref, cv_ref, w_ref, out_ref,
    kall, vaug, wv, qbuf, nsend, nrecv, lsend, lrecv, s0, s1, t0, t1, mx0, mx1, acc,
    flat, psend, precv, lens,
    loc_sem, pair_send, pair_recv, q_send, q_recv, n_send, n_recv, l_send, l_recv,
    p_send, p_recv,
):
    me = lax.axis_index("work")
    t = lax.axis_index("tp")
    z = me // 4
    yh = (me // 2) % 2
    c = me % 2

    def device(d, rel, core):
        hi = (yh + rel) % 2
        return {"work": 4 * ((z + d + PLANES) % PLANES) + 2 * hi + core, "tp": t}

    def remote(src, dst, send, recv, to):
        return pltpu.make_async_remote_copy(
            src, dst, send, recv, device_id=to, device_id_type=MESH
        )

    sibling = device(0, 0, 1 - c)
    partner = device(0, 1, c)

    copy_k = pltpu.make_async_copy(ck_ref, kall.at[pl.ds(0, CACHE)], loc_sem.at[0])
    copy_v = pltpu.make_async_copy(
        cv_ref, vaug.at[pl.ds(0, CACHE), pl.ds(0, HD)], loc_sem.at[1]
    )
    copy_k.start()
    copy_v.start()

    barrier = pltpu.get_barrier_semaphore()

    def signal(to):
        pl.semaphore_signal(barrier, inc=1, device_id=to, device_id_type=MESH)

    def greet(i, _):
        signal(device(i // 2, i % 2, c))
        return 0

    lax.fori_loop(1, SLOTS, greet, 0)
    signal(sibling)

    def greet_tp(i, _):
        signal({"work": me, "tp": (t + i) % TP})
        return 0

    lax.fori_loop(1, TP, greet_tp, 0)

    lane = lax.broadcasted_iota(jnp.int32, (ROWS, HD), 1)
    place = pos_ref[0] + lax.broadcasted_iota(jnp.int32, (ROWS, HD), 0)
    ladder = (lane % (HD // 2)).astype(F32) * (2.0 / HD)
    angle = place.astype(F32) * jnp.exp(ladder * -LOG_BASE)
    cosine, sine = cos_sin(angle)
    sine = jnp.where(lane < HD // 2, -sine, sine)

    def rotated(x):
        x = x.astype(F32)
        return (x * cosine + pltpu.roll(x, HD // 2, 1) * sine).astype(BF16)

    for g in range(HEADS):
        qbuf[0, g * ROWS : (g + 1) * ROWS, :] = rotated(q_ref[g * ROWS : (g + 1) * ROWS, :])
    kall[PAIR : PAIR + ROWS, :] = rotated(nk_ref[...])
    lens[0] = jnp.full((8, HD), len_ref[0], jnp.int32).astype(F32)

    pl.semaphore_wait(barrier, SLOTS - 1 + 1 + TP - 1)

    def query_copy(k, d, rel):
        return remote(qbuf.at[0], qbuf.at[k], q_send.at[k], q_recv.at[k], device(-d, rel, c))

    pair = [
        remote(src, dst, pair_send.at[k], pair_recv.at[k], sibling)
        for k, (src, dst) in enumerate(
            (
                (lens.at[0], lens.at[1]),
                (kall.at[pl.ds(PAIR, ROWS)], kall.at[pl.ds(PAIR + ROWS, ROWS)]),
                (nv_ref, vaug.at[pl.ds(PAIR + ROWS, ROWS), pl.ds(0, HD)]),
                (ck_ref, kall.at[pl.ds(CACHE, CACHE)]),
                (cv_ref, vaug.at[pl.ds(CACHE, CACHE), pl.ds(0, HD)]),
            )
        )
    ]
    query_copy(1, 0, 1).start()
    for copy in pair[:4]:
        copy.start()

    def send_queries(i, code):
        for rel in range(2):
            query_copy(2 * i + rel, code % PLANES, rel).start()
        return code // PLANES

    lax.fori_loop(1, PLANES, send_queries, CODE // PLANES)
    pair[4].start()

    def weight_copy(k):
        return pltpu.make_async_copy(
            w_ref.at[:, pl.ds(pl.multiple_of(k * COLS, HD), COLS)], wv.at[k], loc_sem.at[2 + k]
        )

    def start_weights(k, _):
        weight_copy(k).start()
        return 0

    lax.fori_loop(0, TP, start_weights, 0)

    kall[PAIR + 2 * ROWS :, :] = jnp.zeros((NEWPAD - 2 * ROWS, HD), BF16)
    vaug[PAIR : PAIR + ROWS, 0:HD] = nv_ref[...]
    vaug[PAIR + 2 * ROWS :, 0:HD] = jnp.zeros((NEWPAD - 2 * ROWS, HD), BF16)
    vaug[PAIR:, HD:] = jnp.ones((NEWPAD, HD), BF16)

    def live_rows(base, j):
        rows = lax.broadcasted_iota(jnp.int32, (STEP, HD), 0) + j * STEP
        return jnp.where(rows.astype(F32) < lens[base // CACHE, 0:1, :], 1.0, 0.0).astype(BF16)

    def mask_keys(base):
        first = kall[base : base + 16, :].astype(F32)[0:1, :]
        first = jnp.broadcast_to(first, (STEP, HD)).astype(BF16)

        def body(j, _):
            live = live_rows(base, j)
            rows = pl.ds(base + pl.multiple_of(j * STEP, STEP), STEP)
            kall[rows, :] = kall[rows, :] * live + first * (1.0 - live)
            return 0

        lax.fori_loop(LEAST // STEP, CACHE // STEP, body, 0)

    def mask_values(base):
        def ones(j, _):
            rows = pl.ds(base + pl.multiple_of(j * STEP, STEP), STEP)
            vaug[rows, HD:] = jnp.ones((STEP, HD), BF16)
            return 0

        lax.fori_loop(0, LEAST // STEP, ones, 0)

        def body(j, _):
            live = live_rows(base, j)
            rows = pl.ds(base + pl.multiple_of(j * STEP, STEP), STEP)
            vaug[rows, 0:HD] = vaug[rows, 0:HD] * live
            vaug[rows, HD:] = live
            return 0

        lax.fori_loop(LEAST // STEP, CACHE // STEP, body, 0)

    def wait_queries(i):
        for part in range(PARTS):
            query_copy(PARTS * i + part, 0, 1).wait_recv()

    def queries_of(i):
        return qbuf[pl.ds(PARTS * i, PARTS)].reshape(TILE, HD)

    def chunk(j):
        return pl.ds(pl.multiple_of(j * CHUNK, CHUNK), CHUNK)

    def scores(q, j, s_ref, mx):
        s = lax.dot_general(q, kall[chunk(j), :], NT, preferred_element_type=F32)
        s_ref[j] = s
        top = mx[...]
        for u in range(CHUNK // HD):
            top = jnp.maximum(top, s[:, u * HD : (u + 1) * HD])
        mx[...] = top

    def new_scores(first, q, t_ref, mx):
        row = lax.broadcasted_iota(jnp.int32, (TILE, HD), 0)
        col = lax.broadcasted_iota(jnp.int32, (TILE, HD), 1)
        r, r2 = row & 15, col & 15
        seen = (r2 >> 2) < (r >> 2)
        if first:
            own = (row < BLOCK) & (col < ROWS)
            seen = seen | (own & ((r2 >> 2) == (r >> 2)) & (r2 <= r))
        s = lax.dot_general(q, kall[PAIR:, :], NT, preferred_element_type=F32)
        s = jnp.where(seen & (col < 2 * ROWS), s, -1e30)
        t_ref[...] = s
        mx[...] = s

    def close_max(mx):
        mx[...] = jnp.broadcast_to(jnp.max(mx[...], axis=1, keepdims=True), (TILE, HD))

    def weights(s, top):
        return jnp.exp2((s - top) * SCALE2).astype(BF16)

    def chunk_weights(j, s_ref, mx):
        top = mx[...]
        return jnp.concatenate(
            [weights(s_ref[j, :, u * HD : (u + 1) * HD], top) for u in range(CHUNK // HD)], axis=1
        )

    def add_values(j, p):
        acc[...] += jnp.dot(p, vaug[chunk(j), :], preferred_element_type=F32)

    def new_values(t_ref, mx):
        p = weights(t_ref[...], mx[...])
        acc[...] = jnp.dot(p, vaug[PAIR:, :], preferred_element_type=F32)

    def as_row(level):
        padded = jnp.concatenate([level, jnp.zeros((HD - BLOCK, HD), F32)], axis=0)
        return jnp.transpose(padded)[0:8, :]

    def result_copies(k, d, rel):
        to = device(d, rel, c)
        return [
            remote(src.at[k], dst.at[k], send.at[k], recv.at[k], to)
            for src, dst, send, recv in (
                (nsend, nrecv, n_send, n_recv), (lsend, lrecv, l_send, l_recv)
            )
        ]

    def finish(i, code, mx, maybe_first):
        total = acc[:, HD:]
        n = (acc[:, :HD] / total).astype(BF16)
        level = mx[...] * SCALE2 + jnp.log(total) * math.log2(math.e)
        for part in range(PARTS):
            rows = slice(part * BLOCK, (part + 1) * BLOCK)
            k = PARTS * i + part
            nsend[k] = n[rows]
            lsend[k] = as_row(level[rows])
            copies = result_copies(k, (code // PLANES ** (part // 2)) % PLANES, part % 2)
            if maybe_first and part == 0:
                @pl.when(i > 0)
                def _():
                    for copy in copies:
                        copy.start()

                @pl.when(i == 0)
                def _():
                    nrecv[0] = n[:BLOCK]
                    lrecv[0] = lsend[0]
            else:
                for copy in copies:
                    copy.start()
        return code // PLANES**GROUP

    copy_k.wait()
    mask_keys(0)
    for copy in pair[:3]:
        copy.wait_recv()
    for part in range(1, PARTS):
        query_copy(part, 0, 1).wait_recv()
    q = queries_of(0)
    new_scores(True, q, t0, mx0)

    def first_scores(j, _):
        @pl.when(j == CHUNKS // 2)
        def _():
            pair[3].wait_recv()
            mask_keys(CACHE)

        scores(q, j, s0, mx0)
        return 0

    lax.fori_loop(0, CHUNKS, first_scores, 0)
    close_max(mx0)
    copy_v.wait()
    mask_values(0)

    def both(i, s_now, t_now, mx_now, s_later, t_later, mx_later, maybe_first):
        wait_queries(i + 1)
        q = queries_of(i + 1)
        new_scores(False, q, t_later, mx_later)
        new_values(t_now, mx_now)

        def body(j, _):
            if maybe_first:
                @pl.when((i == 0) & (j == CHUNKS // 2))
                def _():
                    pair[4].wait_recv()
                    mask_values(CACHE)

            p = chunk_weights(j, s_now, mx_now)
            scores(q, j, s_later, mx_later)
            add_values(j, p)
            return 0

        lax.fori_loop(0, CHUNKS, body, 0)
        close_max(mx_later)

    def two_tiles(k, code):
        i = 2 * k
        both(i, s0, t0, mx0, s1, t1, mx1, True)
        code = finish(i, code, mx0, True)

        @pl.when(i + 2 < TILES)
        def _():
            both(i + 1, s1, t1, mx1, s0, t0, mx0, False)

        @pl.when(i + 2 == TILES)
        def _():
            new_values(t1, mx1)

            def body(j, _):
                add_values(j, chunk_weights(j, s1, mx1))
                return 0

            lax.fori_loop(0, CHUNKS, body, 0)

        return finish(i + 1, code, mx1, False)

    lax.fori_loop(0, TILES // 2, two_tiles, CODE)

    def wait_result(k, _):
        for copy in result_copies(k, 0, 1):
            copy.wait_recv()
        return 0

    lax.fori_loop(1, SLOTS, wait_result, 0)
    levels = [lrecv[v] for v in range(SLOTS)]
    summit = levels[0]
    for v in range(1, SLOTS):
        summit = jnp.maximum(summit, levels[v])
    shares = [jnp.exp2(level - summit) for level in levels]
    denom = shares[0]
    for v in range(1, SLOTS):
        denom = denom + shares[v]
    row = lax.broadcasted_iota(jnp.int32, (8, HD), 0)
    packed = []
    for first in range(0, SLOTS, 8):
        rows = jnp.zeros((8, HD), F32)
        for v in range(first, first + 8):
            rows = jnp.where(row == v - first, shares[v], rows)
        packed.append(rows / denom)
    packed.append(jnp.zeros((HD - SLOTS, HD), F32))
    share = jnp.transpose(jnp.concatenate(packed, axis=0))[0:BLOCK, :]
    attention = jnp.zeros((BLOCK, HD), F32)
    for v in range(SLOTS):
        attention = attention + nrecv[v].astype(F32) * share[:, v : v + 1]
    attention = attention.astype(BF16)
    for g in range(HEADS):
        flat[:, g * HD : (g + 1) * HD] = attention[g * ROWS : (g + 1) * ROWS, :]

    def wait_weights(k, _):
        weight_copy(k).wait()
        return 0

    lax.fori_loop(0, TP, wait_weights, 0)

    def columns(i):
        return remote(
            psend.at[i], precv.at[i], p_send.at[i], p_recv.at[i],
            {"work": me, "tp": (t + i) % TP},
        )

    def project(k, _):
        i = 1 + (k + 2) % (TP - 1)
        psend[i] = jnp.dot(
            flat[...], wv[(t + i) % TP], preferred_element_type=F32
        ).astype(BF16)
        columns(i).start()
        return 0

    lax.fori_loop(0, TP - 1, project, 0)
    total = jnp.dot(flat[...], wv[t], preferred_element_type=F32)

    def gather(i, total):
        columns(i).wait_recv()
        return total + precv[i].astype(F32)

    out_ref[...] = lax.fori_loop(1, TP, gather, total).astype(BF16)

    for copy in pair:
        copy.wait_send()

    def sent(k, _):
        query_copy(k, 0, 1).wait_send()
        for copy in result_copies(k, 0, 1):
            copy.wait_send()
        return 0

    lax.fori_loop(1, SLOTS, sent, 0)

    def sent_columns(i, _):
        columns(i).wait_send()
        return 0

    lax.fori_loop(1, TP, sent_columns, 0)


def per_device(
    queries, new_keys, new_values, cache_keys, cache_values, lengths, positions, out_weight
):
    vmem = pl.BlockSpec(memory_space=pltpu.VMEM)
    smem = pl.BlockSpec(memory_space=pltpu.SMEM)
    anywhere = pl.BlockSpec(memory_space=pl.ANY)
    dma = pltpu.SemaphoreType.DMA
    out = pl.pallas_call(
        kernel,
        out_shape=jax.ShapeDtypeStruct((ROWS, COLS), BF16),
        in_specs=[smem, smem, vmem, vmem, vmem, anywhere, anywhere, anywhere],
        out_specs=vmem,
        scratch_shapes=[
            pltpu.VMEM((PAIR + NEWPAD, HD), BF16),
            pltpu.VMEM((PAIR + NEWPAD, 2 * HD), BF16),
            pltpu.VMEM((TP, COLS, COLS), BF16),
            pltpu.VMEM((SLOTS, BLOCK, HD), BF16),
            pltpu.VMEM((SLOTS, BLOCK, HD), BF16),
            pltpu.VMEM((SLOTS, BLOCK, HD), BF16),
            pltpu.VMEM((SLOTS, 8, HD), F32),
            pltpu.VMEM((SLOTS, 8, HD), F32),
            pltpu.VMEM((CHUNKS, TILE, CHUNK), F32),
            pltpu.VMEM((CHUNKS, TILE, CHUNK), F32),
            pltpu.VMEM((TILE, HD), F32),
            pltpu.VMEM((TILE, HD), F32),
            pltpu.VMEM((TILE, HD), F32),
            pltpu.VMEM((TILE, HD), F32),
            pltpu.VMEM((TILE, 2 * HD), F32),
            pltpu.VMEM((ROWS, HEADS * HD), BF16),
            pltpu.VMEM((TP, ROWS, COLS), BF16),
            pltpu.VMEM((TP, ROWS, COLS), BF16),
            pltpu.VMEM((2, 8, HD), F32),
            dma((2 + TP,)),
            dma((5,)),
            dma((5,)),
            dma((SLOTS,)),
            dma((SLOTS,)),
            dma((SLOTS,)),
            dma((SLOTS,)),
            dma((SLOTS,)),
            dma((SLOTS,)),
            dma((TP,)),
            dma((TP,)),
        ],
        compiler_params=pltpu.CompilerParams(
            collective_id=0, has_side_effects=True, vmem_limit_bytes=58 * 1024 * 1024
        ),
    )(
        positions.reshape(ROWS),
        lengths,
        queries[0].transpose(1, 0, 2).reshape(BLOCK, HD),
        new_keys.reshape(ROWS, HD),
        new_values.reshape(ROWS, HD),
        cache_keys.reshape(CACHE, HD),
        cache_values.reshape(CACHE, HD),
        out_weight,
    )
    return out[None]


def solution(mesh):
    in_specs = (
        P("work", None, "tp", None),
        P("work", None, "tp", None),
        P("work", None, "tp", None),
        P("work", None, "tp", None),
        P("work", None, "tp", None),
        P("work"),
        P("work", None),
        P("tp", None),
    )
    out_specs = P("work", None, "tp")
    return jax.shard_map(
        per_device, mesh=mesh, in_specs=in_specs, out_specs=out_specs, check_vma=False
    )
```

```python
import math

import jax
import jax.numpy as jnp
from jax import lax
from jax.experimental import pallas as pl
from jax.experimental.pallas import tpu as pltpu
from jax.sharding import PartitionSpec as P

MESH = pl.DeviceIdType.MESH
F32 = jnp.float32
BF16 = jnp.bfloat16

HEADS = 5
ROWS = 16
HD = 128
CACHE = 4096
PAIR = 2 * CACHE
NEWPAD = 128
BLOCK = HEADS * ROWS
GROUP = 2
PARTS = 2 * GROUP
TILE = PARTS * BLOCK
CHUNK = 2048
CHUNKS = PAIR // CHUNK
TP = 8
COLS = 640
PLANES = 8
TILES = PLANES // GROUP
ORDER = (0, 2, 3, 5, 4, 6, 1, 7)
CODE = sum(d * PLANES**i for i, d in enumerate(ORDER))
SLOTS = 2 * PLANES
LEAST = 1024
STEP = 512

SCALE2 = HD**-0.5 * math.log2(math.e)
LOG_BASE = math.log(1000000.0)
NT = (((1,), (1,)), ((), ()))


def cos_sin(angle):
    turn = jnp.floor(angle * (2.0 / math.pi) + 0.5)
    rest = angle - turn * 1.5703125
    rest = rest - turn * 4.837512969970703125e-4
    rest = rest - turn * 7.54978995489188e-8
    z = rest * rest
    sine = rest + rest * z * ((-1.9515295891e-4 * z + 8.3321608736e-3) * z - 1.6666654611e-1)
    cosine = 1.0 - 0.5 * z + z * z * (
        (2.443315711809948e-5 * z - 1.388731625493765e-3) * z + 4.166664568298827e-2
    )
    quarter = turn.astype(jnp.int32) & 3
    odd = (quarter & 1) == 1
    c = jnp.where(odd, sine, cosine)
    s = jnp.where(odd, cosine, sine)
    c = jnp.where((quarter == 1) | (quarter == 2), -c, c)
    s = jnp.where(quarter >= 2, -s, s)
    return c, s


def kernel(
    pos_ref, len_ref, q_ref, nk_ref, nv_ref, ck_ref, cv_ref, w_ref, out_ref,
    kall, vaug, wv, qbuf, nsend, nrecv, lsend, lrecv, s0, s1, t0, t1, mx0, mx1, acc,
    flat, psend, precv, lens,
    loc_sem, pair_send, pair_recv, q_send, q_recv, n_send, n_recv, l_send, l_recv,
    p_send, p_recv,
):
    me = lax.axis_index("work")
    t = lax.axis_index("tp")
    z = me // 4
    yh = (me // 2) % 2
    c = me % 2

    def device(d, rel, core):
        hi = (yh + rel) % 2
        return {"work": 4 * ((z + d + PLANES) % PLANES) + 2 * hi + core, "tp": t}

    def remote(src, dst, send, recv, to):
        return pltpu.make_async_remote_copy(
            src, dst, send, recv, device_id=to, device_id_type=MESH
        )

    sibling = device(0, 0, 1 - c)
    partner = device(0, 1, c)

    copy_k = pltpu.make_async_copy(ck_ref, kall.at[pl.ds(0, CACHE)], loc_sem.at[0])
    copy_v = pltpu.make_async_copy(
        cv_ref, vaug.at[pl.ds(0, CACHE), pl.ds(0, HD)], loc_sem.at[1]
    )
    copy_k.start()
    copy_v.start()

    barrier = pltpu.get_barrier_semaphore()

    def signal(to):
        pl.semaphore_signal(barrier, inc=1, device_id=to, device_id_type=MESH)

    def greet(i, _):
        signal(device(i // 2, i % 2, c))
        return 0

    lax.fori_loop(1, SLOTS, greet, 0)
    signal(sibling)

    def greet_tp(i, _):
        signal({"work": me, "tp": (t + i) % TP})
        return 0

    lax.fori_loop(1, TP, greet_tp, 0)

    lane = lax.broadcasted_iota(jnp.int32, (ROWS, HD), 1)
    place = pos_ref[0] + lax.broadcasted_iota(jnp.int32, (ROWS, HD), 0)
    ladder = (lane % (HD // 2)).astype(F32) * (2.0 / HD)
    angle = place.astype(F32) * jnp.exp(ladder * -LOG_BASE)
    cosine, sine = cos_sin(angle)
    sine = jnp.where(lane < HD // 2, -sine, sine)

    def rotated(x):
        x = x.astype(F32)
        return (x * cosine + pltpu.roll(x, HD // 2, 1) * sine).astype(BF16)

    for g in range(HEADS):
        qbuf[0, g * ROWS : (g + 1) * ROWS, :] = rotated(q_ref[g * ROWS : (g + 1) * ROWS, :])
    kall[PAIR : PAIR + ROWS, :] = rotated(nk_ref[...])
    lens[0] = jnp.full((8, HD), len_ref[0], jnp.int32).astype(F32)

    pl.semaphore_wait(barrier, SLOTS - 1 + 1 + TP - 1)

    def query_copy(k, d, rel):
        return remote(qbuf.at[0], qbuf.at[k], q_send.at[k], q_recv.at[k], device(-d, rel, c))

    pair = [
        remote(src, dst, pair_send.at[k], pair_recv.at[k], sibling)
        for k, (src, dst) in enumerate(
            (
                (lens.at[0], lens.at[1]),
                (kall.at[pl.ds(PAIR, ROWS)], kall.at[pl.ds(PAIR + ROWS, ROWS)]),
                (nv_ref, vaug.at[pl.ds(PAIR + ROWS, ROWS), pl.ds(0, HD)]),
                (ck_ref, kall.at[pl.ds(CACHE, CACHE)]),
                (cv_ref, vaug.at[pl.ds(CACHE, CACHE), pl.ds(0, HD)]),
            )
        )
    ]
    def relay_copy(i, d):
        k = 2 * i
        return remote(
            qbuf.at[pl.ds(0, 2)], qbuf.at[pl.ds(k, 2)], q_send.at[k], q_recv.at[k],
            device(-d, 0, c),
        )

    def relay(tile, code):
        for g in range(GROUP):
            relay_copy(GROUP * tile + g, code // PLANES**g % PLANES).start()

    query_copy(1, 0, 1).start()
    for copy in pair[:4]:
        copy.start()
    for rel in range(2):
        query_copy(2 + rel, ORDER[1], rel).start()

    def weight_copy(k):
        return pltpu.make_async_copy(
            w_ref.at[:, pl.ds(pl.multiple_of(k * COLS, HD), COLS)], wv.at[k], loc_sem.at[2 + k]
        )

    def start_weights(k, _):
        weight_copy(k).start()
        return 0

    lax.fori_loop(0, TP, start_weights, 0)

    kall[PAIR + 2 * ROWS :, :] = jnp.zeros((NEWPAD - 2 * ROWS, HD), BF16)
    vaug[PAIR : PAIR + ROWS, 0:HD] = nv_ref[...]
    vaug[PAIR + 2 * ROWS :, 0:HD] = jnp.zeros((NEWPAD - 2 * ROWS, HD), BF16)
    vaug[PAIR:, HD:] = jnp.ones((NEWPAD, HD), BF16)

    def live_rows(base, j):
        rows = lax.broadcasted_iota(jnp.int32, (STEP, HD), 0) + j * STEP
        return jnp.where(rows.astype(F32) < lens[base // CACHE, 0:1, :], 1.0, 0.0).astype(BF16)

    def mask_keys(base):
        first = kall[base : base + 16, :].astype(F32)[0:1, :]
        first = jnp.broadcast_to(first, (STEP, HD)).astype(BF16)

        def body(j, _):
            live = live_rows(base, j)
            rows = pl.ds(base + pl.multiple_of(j * STEP, STEP), STEP)
            kall[rows, :] = kall[rows, :] * live + first * (1.0 - live)
            return 0

        lax.fori_loop(LEAST // STEP, CACHE // STEP, body, 0)

    def mask_values(base):
        def ones(j, _):
            rows = pl.ds(base + pl.multiple_of(j * STEP, STEP), STEP)
            vaug[rows, HD:] = jnp.ones((STEP, HD), BF16)
            return 0

        lax.fori_loop(0, LEAST // STEP, ones, 0)

        def body(j, _):
            live = live_rows(base, j)
            rows = pl.ds(base + pl.multiple_of(j * STEP, STEP), STEP)
            vaug[rows, 0:HD] = vaug[rows, 0:HD] * live
            vaug[rows, HD:] = live
            return 0

        lax.fori_loop(LEAST // STEP, CACHE // STEP, body, 0)

    def wait_queries(i):
        for g in range(GROUP):
            relay_copy(GROUP * i + g, 1).wait_recv()

    def queries_of(i):
        return qbuf[pl.ds(PARTS * i, PARTS)].reshape(TILE, HD)

    def chunk(j):
        return pl.ds(pl.multiple_of(j * CHUNK, CHUNK), CHUNK)

    def scores(q, j, s_ref, mx):
        s = lax.dot_general(q, kall[chunk(j), :], NT, preferred_element_type=F32)
        s_ref[j] = s
        top = mx[...]
        for u in range(CHUNK // HD):
            top = jnp.maximum(top, s[:, u * HD : (u + 1) * HD])
        mx[...] = top

    def new_scores(first, q, t_ref, mx):
        row = lax.broadcasted_iota(jnp.int32, (TILE, HD), 0)
        col = lax.broadcasted_iota(jnp.int32, (TILE, HD), 1)
        r, r2 = row & 15, col & 15
        seen = (r2 >> 2) < (r >> 2)
        if first:
            own = (row < BLOCK) & (col < ROWS)
            seen = seen | (own & ((r2 >> 2) == (r >> 2)) & (r2 <= r))
        s = lax.dot_general(q, kall[PAIR:, :], NT, preferred_element_type=F32)
        s = jnp.where(seen & (col < 2 * ROWS), s, -1e30)
        t_ref[...] = s
        mx[...] = s

    def close_max(mx):
        mx[...] = jnp.broadcast_to(jnp.max(mx[...], axis=1, keepdims=True), (TILE, HD))

    def weights(s, top):
        return jnp.exp2((s - top) * SCALE2).astype(BF16)

    def chunk_weights(j, s_ref, mx):
        top = mx[...]
        return jnp.concatenate(
            [weights(s_ref[j, :, u * HD : (u + 1) * HD], top) for u in range(CHUNK // HD)], axis=1
        )

    def add_values(j, p):
        acc[...] += jnp.dot(p, vaug[chunk(j), :], preferred_element_type=F32)

    def new_values(t_ref, mx):
        p = weights(t_ref[...], mx[...])
        acc[...] = jnp.dot(p, vaug[PAIR:, :], preferred_element_type=F32)

    def as_row(level):
        padded = jnp.concatenate([level, jnp.zeros((HD - BLOCK, HD), F32)], axis=0)
        return jnp.transpose(padded)[0:8, :]

    def result_copies(k, d, rel):
        to = device(d, rel, c)
        return [
            remote(src.at[k], dst.at[k], send.at[k], recv.at[k], to)
            for src, dst, send, recv in (
                (nsend, nrecv, n_send, n_recv), (lsend, lrecv, l_send, l_recv)
            )
        ]

    def finish(i, code, mx, maybe_first):
        total = acc[:, HD:]
        n = (acc[:, :HD] / total).astype(BF16)
        level = mx[...] * SCALE2 + jnp.log(total) * math.log2(math.e)
        for part in range(PARTS):
            rows = slice(part * BLOCK, (part + 1) * BLOCK)
            k = PARTS * i + part
            nsend[k] = n[rows]
            lsend[k] = as_row(level[rows])
            copies = result_copies(k, (code // PLANES ** (part // 2)) % PLANES, part % 2)
            if maybe_first and part == 0:
                @pl.when(i > 0)
                def _():
                    for copy in copies:
                        copy.start()

                @pl.when(i == 0)
                def _():
                    nrecv[0] = n[:BLOCK]
                    lrecv[0] = lsend[0]
            else:
                for copy in copies:
                    copy.start()
        return code // PLANES**GROUP

    copy_k.wait()
    mask_keys(0)
    for copy in pair[:3]:
        copy.wait_recv()
    for part in range(1, PARTS):
        query_copy(part, 0, 1).wait_recv()
    pair[4].start()
    relay(1, CODE // PLANES**GROUP)
    q = queries_of(0)
    new_scores(True, q, t0, mx0)

    def first_scores(j, _):
        @pl.when(j == CHUNKS // 2)
        def _():
            pair[3].wait_recv()
            mask_keys(CACHE)

        scores(q, j, s0, mx0)
        return 0

    lax.fori_loop(0, CHUNKS, first_scores, 0)
    close_max(mx0)
    copy_v.wait()
    mask_values(0)

    def both(i, code, s_now, t_now, mx_now, s_later, t_later, mx_later, maybe_first):
        wait_queries(i + 1)

        @pl.when(i + 2 < TILES)
        def _():
            relay(i + 2, code // PLANES ** (2 * GROUP))

        q = queries_of(i + 1)
        new_scores(False, q, t_later, mx_later)
        new_values(t_now, mx_now)

        def body(j, _):
            if maybe_first:
                @pl.when((i == 0) & (j == CHUNKS // 2))
                def _():
                    pair[4].wait_recv()
                    mask_values(CACHE)

            p = chunk_weights(j, s_now, mx_now)
            scores(q, j, s_later, mx_later)
            add_values(j, p)
            return 0

        lax.fori_loop(0, CHUNKS, body, 0)
        close_max(mx_later)

    def two_tiles(k, code):
        i = 2 * k
        both(i, code, s0, t0, mx0, s1, t1, mx1, True)
        code = finish(i, code, mx0, True)

        @pl.when(i + 2 < TILES)
        def _():
            both(i + 1, code, s1, t1, mx1, s0, t0, mx0, False)

        @pl.when(i + 2 == TILES)
        def _():
            new_values(t1, mx1)

            def body(j, _):
                add_values(j, chunk_weights(j, s1, mx1))
                return 0

            lax.fori_loop(0, CHUNKS, body, 0)

        return finish(i + 1, code, mx1, False)

    lax.fori_loop(0, TILES // 2, two_tiles, CODE)

    def wait_result(k, _):
        for copy in result_copies(k, 0, 1):
            copy.wait_recv()
        return 0

    lax.fori_loop(1, SLOTS, wait_result, 0)
    levels = [lrecv[v] for v in range(SLOTS)]
    summit = levels[0]
    for v in range(1, SLOTS):
        summit = jnp.maximum(summit, levels[v])
    shares = [jnp.exp2(level - summit) for level in levels]
    denom = shares[0]
    for v in range(1, SLOTS):
        denom = denom + shares[v]
    row = lax.broadcasted_iota(jnp.int32, (8, HD), 0)
    packed = []
    for first in range(0, SLOTS, 8):
        rows = jnp.zeros((8, HD), F32)
        for v in range(first, first + 8):
            rows = jnp.where(row == v - first, shares[v], rows)
        packed.append(rows / denom)
    packed.append(jnp.zeros((HD - SLOTS, HD), F32))
    share = jnp.transpose(jnp.concatenate(packed, axis=0))[0:BLOCK, :]
    attention = jnp.zeros((BLOCK, HD), F32)
    for v in range(SLOTS):
        attention = attention + nrecv[v].astype(F32) * share[:, v : v + 1]
    attention = attention.astype(BF16)
    for g in range(HEADS):
        flat[:, g * HD : (g + 1) * HD] = attention[g * ROWS : (g + 1) * ROWS, :]

    def wait_weights(k, _):
        weight_copy(k).wait()
        return 0

    lax.fori_loop(0, TP, wait_weights, 0)

    def columns(i):
        return remote(
            psend.at[i], precv.at[i], p_send.at[i], p_recv.at[i],
            {"work": me, "tp": (t + i) % TP},
        )

    def project(k, _):
        i = 1 + (k + 2) % (TP - 1)
        psend[i] = jnp.dot(
            flat[...], wv[(t + i) % TP], preferred_element_type=F32
        ).astype(BF16)
        columns(i).start()
        return 0

    lax.fori_loop(0, TP - 1, project, 0)
    total = jnp.dot(flat[...], wv[t], preferred_element_type=F32)

    def gather(i, total):
        columns(i).wait_recv()
        return total + precv[i].astype(F32)

    out_ref[...] = lax.fori_loop(1, TP, gather, total).astype(BF16)

    for copy in pair:
        copy.wait_send()

    def sent(k, _):
        for copy in result_copies(k, 0, 1):
            copy.wait_send()
        return 0

    lax.fori_loop(1, SLOTS, sent, 0)
    for part in range(1, PARTS):
        query_copy(part, 0, 1).wait_send()

    def relayed(i, _):
        relay_copy(i, 1).wait_send()
        return 0

    lax.fori_loop(GROUP, PLANES, relayed, 0)

    def sent_columns(i, _):
        columns(i).wait_send()
        return 0

    lax.fori_loop(1, TP, sent_columns, 0)


def per_device(
    queries, new_keys, new_values, cache_keys, cache_values, lengths, positions, out_weight
):
    vmem = pl.BlockSpec(memory_space=pltpu.VMEM)
    smem = pl.BlockSpec(memory_space=pltpu.SMEM)
    anywhere = pl.BlockSpec(memory_space=pl.ANY)
    dma = pltpu.SemaphoreType.DMA
    out = pl.pallas_call(
        kernel,
        out_shape=jax.ShapeDtypeStruct((ROWS, COLS), BF16),
        in_specs=[smem, smem, vmem, vmem, vmem, anywhere, anywhere, anywhere],
        out_specs=vmem,
        scratch_shapes=[
            pltpu.VMEM((PAIR + NEWPAD, HD), BF16),
            pltpu.VMEM((PAIR + NEWPAD, 2 * HD), BF16),
            pltpu.VMEM((TP, COLS, COLS), BF16),
            pltpu.VMEM((SLOTS, BLOCK, HD), BF16),
            pltpu.VMEM((SLOTS, BLOCK, HD), BF16),
            pltpu.VMEM((SLOTS, BLOCK, HD), BF16),
            pltpu.VMEM((SLOTS, 8, HD), F32),
            pltpu.VMEM((SLOTS, 8, HD), F32),
            pltpu.VMEM((CHUNKS, TILE, CHUNK), F32),
            pltpu.VMEM((CHUNKS, TILE, CHUNK), F32),
            pltpu.VMEM((TILE, HD), F32),
            pltpu.VMEM((TILE, HD), F32),
            pltpu.VMEM((TILE, HD), F32),
            pltpu.VMEM((TILE, HD), F32),
            pltpu.VMEM((TILE, 2 * HD), F32),
            pltpu.VMEM((ROWS, HEADS * HD), BF16),
            pltpu.VMEM((TP, ROWS, COLS), BF16),
            pltpu.VMEM((TP, ROWS, COLS), BF16),
            pltpu.VMEM((2, 8, HD), F32),
            dma((2 + TP,)),
            dma((5,)),
            dma((5,)),
            dma((SLOTS,)),
            dma((SLOTS,)),
            dma((SLOTS,)),
            dma((SLOTS,)),
            dma((SLOTS,)),
            dma((SLOTS,)),
            dma((TP,)),
            dma((TP,)),
        ],
        compiler_params=pltpu.CompilerParams(
            collective_id=0, has_side_effects=True, vmem_limit_bytes=58 * 1024 * 1024
        ),
    )(
        positions.reshape(ROWS),
        lengths,
        queries[0].transpose(1, 0, 2).reshape(BLOCK, HD),
        new_keys.reshape(ROWS, HD),
        new_values.reshape(ROWS, HD),
        cache_keys.reshape(CACHE, HD),
        cache_values.reshape(CACHE, HD),
        out_weight,
    )
    return out[None]


def solution(mesh):
    in_specs = (
        P("work", None, "tp", None),
        P("work", None, "tp", None),
        P("work", None, "tp", None),
        P("work", None, "tp", None),
        P("work", None, "tp", None),
        P("work"),
        P("work", None),
        P("tp", None),
    )
    out_specs = P("work", None, "tp")
    return jax.shard_map(
        per_device, mesh=mesh, in_specs=in_specs, out_specs=out_specs, check_vma=False
    )
```

```python
import math

import jax
import jax.numpy as jnp
from jax import lax
from jax.experimental import pallas as pl
from jax.experimental.pallas import tpu as pltpu
from jax.sharding import PartitionSpec as P

MESH = pl.DeviceIdType.MESH
F32 = jnp.float32
BF16 = jnp.bfloat16

HEADS = 5
ROWS = 16
HD = 128
CACHE = 4096
PAIR = 2 * CACHE
NEWPAD = 128
BLOCK = HEADS * ROWS
GROUP = 2
PARTS = 2 * GROUP
TILE = PARTS * BLOCK
CHUNK = 2048
CHUNKS = PAIR // CHUNK
TP = 8
COLS = 640
PLANES = 8
TILES = PLANES // GROUP
ORDER = (0, 7, 3, 5, 4, 2, 6, 1)
CODE = sum(d * PLANES**i for i, d in enumerate(ORDER))
SLOTS = 2 * PLANES
MESSAGE = BLOCK + 16
LEAST = 1024
STEP = 1024

SCALE2 = HD**-0.5 * math.log2(math.e)
LOG_BASE = math.log(1000000.0)
NT = (((1,), (1,)), ((), ()))


def cos_sin(angle):
    turn = jnp.floor(angle * (2.0 / math.pi) + 0.5)
    rest = angle - turn * 1.5703125
    rest = rest - turn * 4.837512969970703125e-4
    rest = rest - turn * 7.54978995489188e-8
    z = rest * rest
    sine = rest + rest * z * ((-1.9515295891e-4 * z + 8.3321608736e-3) * z - 1.6666654611e-1)
    cosine = 1.0 - 0.5 * z + z * z * (
        (2.443315711809948e-5 * z - 1.388731625493765e-3) * z + 4.166664568298827e-2
    )
    quarter = turn.astype(jnp.int32) & 3
    odd = (quarter & 1) == 1
    c = jnp.where(odd, sine, cosine)
    s = jnp.where(odd, cosine, sine)
    c = jnp.where((quarter == 1) | (quarter == 2), -c, c)
    s = jnp.where(quarter >= 2, -s, s)
    return c, s


def kernel(
    pos_ref, len_ref, q_ref, nk_ref, nv_ref, ck_ref, cv_ref, w_ref, out_ref,
    kall, vaug, wv, qbuf, nsend, nrecv, s0, s1, t0, t1, mx0, mx1, acc,
    flat, psend, precv, lens,
    loc_sem, pair_send, pair_recv, q_send, q_recv, n_send, n_recv,
    p_send, p_recv,
):
    me = lax.axis_index("work")
    t = lax.axis_index("tp")
    z = me // 4
    yh = (me // 2) % 2
    c = me % 2

    def device(d, rel, core):
        hi = (yh + rel) % 2
        return {"work": 4 * ((z + d + PLANES) % PLANES) + 2 * hi + core, "tp": t}

    def remote(src, dst, send, recv, to):
        return pltpu.make_async_remote_copy(
            src, dst, send, recv, device_id=to, device_id_type=MESH
        )

    sibling = device(0, 0, 1 - c)
    partner = device(0, 1, c)

    copy_k = pltpu.make_async_copy(ck_ref, kall.at[pl.ds(0, CACHE)], loc_sem.at[0])
    copy_v = pltpu.make_async_copy(
        cv_ref, vaug.at[pl.ds(0, CACHE), pl.ds(0, HD)], loc_sem.at[1]
    )
    copy_k.start()
    copy_v.start()

    barrier = pltpu.get_barrier_semaphore()

    def signal(to):
        pl.semaphore_signal(barrier, inc=1, device_id=to, device_id_type=MESH)

    def greet(i, _):
        signal(device(i // 2, i % 2, c))
        return 0

    lax.fori_loop(1, SLOTS, greet, 0)
    signal(sibling)

    def greet_tp(i, _):
        signal({"work": me, "tp": (t + i) % TP})
        return 0

    lax.fori_loop(1, TP, greet_tp, 0)

    lane = lax.broadcasted_iota(jnp.int32, (ROWS, HD), 1)
    place = pos_ref[0] + lax.broadcasted_iota(jnp.int32, (ROWS, HD), 0)
    ladder = (lane % (HD // 2)).astype(F32) * (2.0 / HD)
    angle = place.astype(F32) * jnp.exp(ladder * -LOG_BASE)
    cosine, sine = cos_sin(angle)
    sine = jnp.where(lane < HD // 2, -sine, sine)

    def rotated(x):
        x = x.astype(F32)
        return (x * cosine + pltpu.roll(x, HD // 2, 1) * sine).astype(BF16)

    for g in range(HEADS):
        qbuf[0, g * ROWS : (g + 1) * ROWS, :] = rotated(q_ref[g * ROWS : (g + 1) * ROWS, :])
    kall[PAIR : PAIR + ROWS, :] = rotated(nk_ref[...])
    lens[0] = jnp.full((8, HD), len_ref[0], jnp.int32).astype(F32)

    pl.semaphore_wait(barrier, SLOTS - 1 + 1 + TP - 1)

    def query_copy(k, d, rel):
        return remote(qbuf.at[0], qbuf.at[k], q_send.at[k], q_recv.at[k], device(-d, rel, c))

    pair = [
        remote(src, dst, pair_send.at[k], pair_recv.at[k], sibling)
        for k, (src, dst) in enumerate(
            (
                (lens.at[0], lens.at[1]),
                (kall.at[pl.ds(PAIR, ROWS)], kall.at[pl.ds(PAIR + ROWS, ROWS)]),
                (nv_ref, vaug.at[pl.ds(PAIR + ROWS, ROWS), pl.ds(0, HD)]),
                (ck_ref, kall.at[pl.ds(CACHE, CACHE)]),
                (cv_ref, vaug.at[pl.ds(CACHE, CACHE), pl.ds(0, HD)]),
            )
        )
    ]
    query_copy(1, 0, 1).start()
    for copy in pair[:4]:
        copy.start()

    def send_queries(i, code):
        for rel in range(2):
            query_copy(2 * i + rel, code % PLANES, rel).start()
        return code // PLANES

    lax.fori_loop(1, PLANES, send_queries, CODE // PLANES)
    pair[4].start()

    def weight_copy(k):
        return pltpu.make_async_copy(
            w_ref.at[:, pl.ds(pl.multiple_of(k * COLS, HD), COLS)], wv.at[k], loc_sem.at[2 + k]
        )

    def start_weights(k, _):
        weight_copy(k).start()
        return 0

    lax.fori_loop(0, TP, start_weights, 0)

    kall[PAIR + 2 * ROWS :, :] = jnp.zeros((NEWPAD - 2 * ROWS, HD), BF16)
    vaug[PAIR : PAIR + ROWS, 0:HD] = nv_ref[...]
    vaug[PAIR + 2 * ROWS :, 0:HD] = jnp.zeros((NEWPAD - 2 * ROWS, HD), BF16)
    vaug[PAIR:, HD:] = jnp.ones((NEWPAD, HD), BF16)

    def live_rows(base, j):
        rows = lax.broadcasted_iota(jnp.int32, (STEP, HD), 0) + j * STEP
        return jnp.where(rows.astype(F32) < lens[base // CACHE, 0:1, :], 1.0, 0.0).astype(BF16)

    def mask_keys(base):
        first = kall[base : base + 16, :].astype(F32)[0:1, :]
        first = jnp.broadcast_to(first, (STEP, HD)).astype(BF16)

        def body(j, _):
            live = live_rows(base, j)
            rows = pl.ds(base + pl.multiple_of(j * STEP, STEP), STEP)
            kall[rows, :] = kall[rows, :] * live + first * (1.0 - live)
            return 0

        lax.fori_loop(LEAST // STEP, CACHE // STEP, body, 0)

    def mask_values(base):
        def ones(j, _):
            rows = pl.ds(base + pl.multiple_of(j * STEP, STEP), STEP)
            vaug[rows, HD:] = jnp.ones((STEP, HD), BF16)
            return 0

        lax.fori_loop(0, LEAST // STEP, ones, 0)

        def body(j, _):
            live = live_rows(base, j)
            rows = pl.ds(base + pl.multiple_of(j * STEP, STEP), STEP)
            vaug[rows, 0:HD] = vaug[rows, 0:HD] * live
            vaug[rows, HD:] = live
            return 0

        lax.fori_loop(LEAST // STEP, CACHE // STEP, body, 0)

    def wait_queries(i):
        for part in range(PARTS):
            query_copy(PARTS * i + part, 0, 1).wait_recv()

    def queries_of(i):
        return qbuf[pl.ds(PARTS * i, PARTS)].reshape(TILE, HD)

    def chunk(j):
        return pl.ds(pl.multiple_of(j * CHUNK, CHUNK), CHUNK)

    def scores(q, j, s_ref, mx):
        s = lax.dot_general(q, kall[chunk(j), :], NT, preferred_element_type=F32)
        s_ref[j] = s
        top = mx[...]
        for u in range(CHUNK // HD):
            top = jnp.maximum(top, s[:, u * HD : (u + 1) * HD])
        mx[...] = top

    def new_scores(first, q, t_ref, mx):
        row = lax.broadcasted_iota(jnp.int32, (TILE, HD), 0)
        col = lax.broadcasted_iota(jnp.int32, (TILE, HD), 1)
        r, r2 = row & 15, col & 15
        seen = (r2 >> 2) < (r >> 2)
        if first:
            own = (row < BLOCK) & (col < ROWS)
            seen = seen | (own & ((r2 >> 2) == (r >> 2)) & (r2 <= r))
        s = lax.dot_general(q, kall[PAIR:, :], NT, preferred_element_type=F32)
        s = jnp.where(seen & (col < 2 * ROWS), s, -1e30)
        t_ref[...] = s
        mx[...] = s

    def close_max(mx):
        mx[...] = jnp.broadcast_to(jnp.max(mx[...], axis=1, keepdims=True), (TILE, HD))

    def weights(s, top):
        return jnp.exp2((s - top) * SCALE2).astype(BF16)

    def chunk_weights(j, s_ref, mx):
        top = mx[...]
        return jnp.concatenate(
            [weights(s_ref[j, :, u * HD : (u + 1) * HD], top) for u in range(CHUNK // HD)], axis=1
        )

    def add_values(j, p):
        acc[...] += jnp.dot(p, vaug[chunk(j), :], preferred_element_type=F32)

    def new_values(t_ref, mx):
        p = weights(t_ref[...], mx[...])
        acc[...] = jnp.dot(p, vaug[PAIR:, :], preferred_element_type=F32)

    def as_rows(level):
        padded = jnp.concatenate([level, jnp.zeros((HD - BLOCK, HD), F32)], axis=0)
        row = jnp.transpose(padded)[0:8, :]
        high = row.astype(BF16).astype(F32)
        middle = (row - high).astype(BF16).astype(F32)
        low = row - high - middle
        place = lax.broadcasted_iota(jnp.int32, (8, HD), 0)
        terms = jnp.where(
            place == 0, high, jnp.where(place == 1, middle, jnp.where(place == 2, low, 0.0))
        )
        return jnp.concatenate([terms, jnp.zeros((8, HD), F32)], axis=0).astype(BF16)

    def result_copy(k, d, rel):
        return remote(nsend.at[k], nrecv.at[k], n_send.at[k], n_recv.at[k], device(d, rel, c))

    def finish(i, code, mx, maybe_first):
        total = acc[:, HD:]
        n = (acc[:, :HD] / total).astype(BF16)
        level = mx[...] * SCALE2 + jnp.log(total) * math.log2(math.e)
        for part in range(PARTS):
            rows = slice(part * BLOCK, (part + 1) * BLOCK)
            k = PARTS * i + part
            nsend[k, 0:BLOCK, :] = n[rows]
            nsend[k, BLOCK:, :] = as_rows(level[rows])
            copy = result_copy(k, (code // PLANES ** (part // 2)) % PLANES, part % 2)
            if maybe_first and part == 0:
                @pl.when(i > 0)
                def _():
                    copy.start()

                @pl.when(i == 0)
                def _():
                    nrecv[0] = nsend[0]
            else:
                copy.start()
        return code // PLANES**GROUP

    copy_k.wait()
    mask_keys(0)
    for copy in pair[:3]:
        copy.wait_recv()
    for part in range(1, PARTS):
        query_copy(part, 0, 1).wait_recv()
    q = queries_of(0)
    new_scores(True, q, t0, mx0)

    def first_scores(j, _):
        @pl.when(j == CHUNKS // 2)
        def _():
            pair[3].wait_recv()
            mask_keys(CACHE)

        scores(q, j, s0, mx0)
        return 0

    lax.fori_loop(0, CHUNKS, first_scores, 0)
    close_max(mx0)
    copy_v.wait()
    mask_values(0)

    def both(i, s_now, t_now, mx_now, s_later, t_later, mx_later, maybe_first):
        wait_queries(i + 1)
        q = queries_of(i + 1)
        new_scores(False, q, t_later, mx_later)
        new_values(t_now, mx_now)

        def body(j, _):
            if maybe_first:
                @pl.when((i == 0) & (j == CHUNKS // 2))
                def _():
                    pair[4].wait_recv()
                    mask_values(CACHE)

            p = chunk_weights(j, s_now, mx_now)
            scores(q, j, s_later, mx_later)
            add_values(j, p)
            return 0

        lax.fori_loop(0, CHUNKS, body, 0)
        close_max(mx_later)

    def two_tiles(k, code):
        i = 2 * k
        both(i, s0, t0, mx0, s1, t1, mx1, True)
        code = finish(i, code, mx0, True)

        @pl.when(i + 2 < TILES)
        def _():
            both(i + 1, s1, t1, mx1, s0, t0, mx0, False)

        @pl.when(i + 2 == TILES)
        def _():
            new_values(t1, mx1)

            def body(j, _):
                add_values(j, chunk_weights(j, s1, mx1))
                return 0

            lax.fori_loop(0, CHUNKS, body, 0)

        return finish(i + 1, code, mx1, False)

    lax.fori_loop(0, TILES // 2, two_tiles, CODE)

    def wait_result(k, _):
        result_copy(k, 0, 1).wait_recv()
        return 0

    def level_of(v):
        terms = nrecv[v, BLOCK:, :].astype(F32)
        return jnp.broadcast_to(jnp.sum(terms, axis=0, keepdims=True), (8, HD))

    def as_columns(rows):
        place = lax.broadcasted_iota(jnp.int32, (8, HD), 0)
        packed = []
        for first in range(0, len(rows), 8):
            block = jnp.zeros((8, HD), F32)
            for v in range(first, min(first + 8, len(rows))):
                block = jnp.where(place == v - first, rows[v], block)
            packed.append(block)
        packed.append(jnp.zeros((HD - 8 * len(packed), HD), F32))
        return jnp.transpose(jnp.concatenate(packed, axis=0))[0:BLOCK, :]

    def largest(levels):
        top = levels[0]
        for level in levels[1:]:
            top = jnp.maximum(top, level)
        return top

    early = SLOTS - PARTS
    lax.fori_loop(1, early, wait_result, 0)
    levels = [level_of(v) for v in range(early)]
    early_top = largest(levels)
    shares = [jnp.exp2(level - early_top) for level in levels]
    early_sum = sum(shares[1:], shares[0])
    share = as_columns(shares)
    early_total = jnp.zeros((BLOCK, HD), F32)
    for v in range(early):
        early_total = early_total + nrecv[v, 0:BLOCK, :].astype(F32) * share[:, v : v + 1]

    lax.fori_loop(early, SLOTS, wait_result, 0)
    levels = [early_top] + [level_of(v) for v in range(early, SLOTS)]
    summit = largest(levels)
    shares = [jnp.exp2(level - summit) for level in levels]
    denom = sum(shares[1:], shares[0] * early_sum)
    share = as_columns([part / denom for part in shares])
    attention = early_total * share[:, 0:1]
    for k in range(PARTS):
        part = nrecv[early + k, 0:BLOCK, :].astype(F32)
        attention = attention + part * share[:, k + 1 : k + 2]
    attention = attention.astype(BF16)
    for g in range(HEADS):
        flat[:, g * HD : (g + 1) * HD] = attention[g * ROWS : (g + 1) * ROWS, :]

    def wait_weights(k, _):
        weight_copy(k).wait()
        return 0

    lax.fori_loop(0, TP, wait_weights, 0)

    def columns(i):
        return remote(
            psend.at[i], precv.at[i], p_send.at[i], p_recv.at[i],
            {"work": me, "tp": (t + i) % TP},
        )

    joined = flat[...]
    for i in (4, 5, 3, 2, 6, 7, 1):
        psend[i] = jnp.dot(joined, wv[(t + i) % TP], preferred_element_type=F32).astype(BF16)
        columns(i).start()
    total = jnp.dot(joined, wv[t], preferred_element_type=F32)

    def gather(i, total):
        columns(i).wait_recv()
        return total + precv[i].astype(F32)

    out_ref[...] = lax.fori_loop(1, TP, gather, total).astype(BF16)

    for copy in pair:
        copy.wait_send()

    def sent(k, _):
        query_copy(k, 0, 1).wait_send()
        result_copy(k, 0, 1).wait_send()
        return 0

    lax.fori_loop(1, SLOTS, sent, 0)

    def sent_columns(i, _):
        columns(i).wait_send()
        return 0

    lax.fori_loop(1, TP, sent_columns, 0)


def per_device(
    queries, new_keys, new_values, cache_keys, cache_values, lengths, positions, out_weight
):
    vmem = pl.BlockSpec(memory_space=pltpu.VMEM)
    smem = pl.BlockSpec(memory_space=pltpu.SMEM)
    anywhere = pl.BlockSpec(memory_space=pl.ANY)
    dma = pltpu.SemaphoreType.DMA
    out = pl.pallas_call(
        kernel,
        out_shape=jax.ShapeDtypeStruct((ROWS, COLS), BF16),
        in_specs=[smem, smem, vmem, vmem, vmem, anywhere, anywhere, anywhere],
        out_specs=vmem,
        scratch_shapes=[
            pltpu.VMEM((PAIR + NEWPAD, HD), BF16),
            pltpu.VMEM((PAIR + NEWPAD, 2 * HD), BF16),
            pltpu.VMEM((TP, COLS, COLS), BF16),
            pltpu.VMEM((SLOTS, BLOCK, HD), BF16),
            pltpu.VMEM((SLOTS, MESSAGE, HD), BF16),
            pltpu.VMEM((SLOTS, MESSAGE, HD), BF16),
            pltpu.VMEM((CHUNKS, TILE, CHUNK), F32),
            pltpu.VMEM((CHUNKS, TILE, CHUNK), F32),
            pltpu.VMEM((TILE, HD), F32),
            pltpu.VMEM((TILE, HD), F32),
            pltpu.VMEM((TILE, HD), F32),
            pltpu.VMEM((TILE, HD), F32),
            pltpu.VMEM((TILE, 2 * HD), F32),
            pltpu.VMEM((ROWS, HEADS * HD), BF16),
            pltpu.VMEM((TP, ROWS, COLS), BF16),
            pltpu.VMEM((TP, ROWS, COLS), BF16),
            pltpu.VMEM((2, 8, HD), F32),
            dma((2 + TP,)),
            dma((5,)),
            dma((5,)),
            dma((SLOTS,)),
            dma((SLOTS,)),
            dma((SLOTS,)),
            dma((SLOTS,)),
            dma((TP,)),
            dma((TP,)),
        ],
        compiler_params=pltpu.CompilerParams(
            collective_id=0, has_side_effects=True, vmem_limit_bytes=58 * 1024 * 1024
        ),
    )(
        positions.reshape(ROWS),
        lengths,
        queries[0].transpose(1, 0, 2).reshape(BLOCK, HD),
        new_keys.reshape(ROWS, HD),
        new_values.reshape(ROWS, HD),
        cache_keys.reshape(CACHE, HD),
        cache_values.reshape(CACHE, HD),
        out_weight,
    )
    return out[None]


def solution(mesh):
    in_specs = (
        P("work", None, "tp", None),
        P("work", None, "tp", None),
        P("work", None, "tp", None),
        P("work", None, "tp", None),
        P("work", None, "tp", None),
        P("work"),
        P("work", None),
        P("tp", None),
    )
    out_specs = P("work", None, "tp")
    return jax.shard_map(
        per_device, mesh=mesh, in_specs=in_specs, out_specs=out_specs, check_vma=False
    )
```

```python
import math

import jax
import jax.numpy as jnp
from jax import lax
from jax.experimental import pallas as pl
from jax.experimental.pallas import tpu as pltpu
from jax.sharding import PartitionSpec as P

MESH = pl.DeviceIdType.MESH
F32 = jnp.float32
BF16 = jnp.bfloat16

HEADS = 5
ROWS = 16
HD = 128
CACHE = 4096
PAIR = 2 * CACHE
NEWPAD = 128
BLOCK = HEADS * ROWS
GROUP = 2
PARTS = 2 * GROUP
TILE = PARTS * BLOCK
CHUNK = 2048
CHUNKS = PAIR // CHUNK
TP = 8
COLS = 640
PLANES = 8
TILES = PLANES // GROUP
ORDER = (0, 7, 3, 5, 4, 2, 6, 1)
BLOCKS = 1 + 2 * PLANES
FIRST = ((2, 1 + PARTS), (0, 1 + PARTS))
WIDEST = (1 + PARTS) * BLOCK
MESSAGE = BLOCK + 16
LEAST = 1024
STEP = 1024

SCALE2 = HD**-0.5 * math.log2(math.e)
LOG_BASE = math.log(1000000.0)
NT = (((1,), (1,)), ((), ()))


def cos_sin(angle):
    turn = jnp.floor(angle * (2.0 / math.pi) + 0.5)
    rest = angle - turn * 1.5703125
    rest = rest - turn * 4.837512969970703125e-4
    rest = rest - turn * 7.54978995489188e-8
    z = rest * rest
    sine = rest + rest * z * ((-1.9515295891e-4 * z + 8.3321608736e-3) * z - 1.6666654611e-1)
    cosine = 1.0 - 0.5 * z + z * z * (
        (2.443315711809948e-5 * z - 1.388731625493765e-3) * z + 4.166664568298827e-2
    )
    quarter = turn.astype(jnp.int32) & 3
    odd = (quarter & 1) == 1
    c = jnp.where(odd, sine, cosine)
    s = jnp.where(odd, cosine, sine)
    c = jnp.where((quarter == 1) | (quarter == 2), -c, c)
    s = jnp.where(quarter >= 2, -s, s)
    return c, s


def kernel(
    pos_ref, len_ref, q_ref, nk_ref, nv_ref, ck_ref, cv_ref, w_ref, out_ref,
    kall, vaug, wv, qbuf, nsend, nrecv, s0, s1, t0, t1, mx0, mx1, acc,
    flat, psend, precv, lens,
    loc_sem, pair_send, pair_recv, q_send, q_recv, n_send, n_recv,
    p_send, p_recv,
):
    me = lax.axis_index("work")
    t = lax.axis_index("tp")
    z = me // 4
    yh = (me // 2) % 2
    c = me % 2

    def device(d, rel, core):
        hi = (yh + rel) % 2
        return {"work": 4 * ((z + d + PLANES) % PLANES) + 2 * hi + core, "tp": t}

    def remote(src, dst, send, recv, to):
        return pltpu.make_async_remote_copy(
            src, dst, send, recv, device_id=to, device_id_type=MESH
        )

    sibling = device(0, 0, 1 - c)
    partner = device(0, 1, c)

    copy_k = pltpu.make_async_copy(ck_ref, kall.at[pl.ds(0, CACHE)], loc_sem.at[0])
    copy_v = pltpu.make_async_copy(
        cv_ref, vaug.at[pl.ds(0, CACHE), pl.ds(0, HD)], loc_sem.at[1]
    )
    copy_k.start()
    copy_v.start()

    barrier = pltpu.get_barrier_semaphore()

    def signal(to):
        pl.semaphore_signal(barrier, inc=1, device_id=to, device_id_type=MESH)

    def greet(i, _):
        signal(device(i // 2, i % 2, c))
        return 0

    lax.fori_loop(1, BLOCKS - 1, greet, 0)
    signal(sibling)

    def greet_tp(i, _):
        signal({"work": me, "tp": (t + i) % TP})
        return 0

    lax.fori_loop(1, TP, greet_tp, 0)

    lane = lax.broadcasted_iota(jnp.int32, (ROWS, HD), 1)
    place = pos_ref[0] + lax.broadcasted_iota(jnp.int32, (ROWS, HD), 0)
    ladder = (lane % (HD // 2)).astype(F32) * (2.0 / HD)
    angle = place.astype(F32) * jnp.exp(ladder * -LOG_BASE)
    cosine, sine = cos_sin(angle)
    sine = jnp.where(lane < HD // 2, -sine, sine)

    def rotated(x):
        x = x.astype(F32)
        return (x * cosine + pltpu.roll(x, HD // 2, 1) * sine).astype(BF16)

    for g in range(HEADS):
        qbuf[1, g * ROWS : (g + 1) * ROWS, :] = rotated(q_ref[g * ROWS : (g + 1) * ROWS, :])
    kall[PAIR : PAIR + ROWS, :] = rotated(nk_ref[...])
    lens[0] = jnp.full((8, HD), len_ref[0], jnp.int32).astype(F32)

    pl.semaphore_wait(barrier, 2 * PLANES - 1 + 1 + TP - 1)

    def query_copy(k, to):
        return remote(qbuf.at[1], qbuf.at[k], q_send.at[k], q_recv.at[k], to)

    def on_core(core):
        return pl.when(c == core)

    pair = [
        remote(src, dst, pair_send.at[k], pair_recv.at[k], sibling)
        for k, (src, dst) in enumerate(
            (
                (lens.at[0], lens.at[1]),
                (kall.at[pl.ds(PAIR, ROWS)], kall.at[pl.ds(PAIR + ROWS, ROWS)]),
                (nv_ref, vaug.at[pl.ds(PAIR + ROWS, ROWS), pl.ds(0, HD)]),
                (ck_ref, kall.at[pl.ds(CACHE, CACHE)]),
                (cv_ref, vaug.at[pl.ds(CACHE, CACHE), pl.ds(0, HD)]),
            )
        )
    ]
    query_copy(2, partner).start()

    @on_core(0)
    def _():
        query_copy(0, sibling).start()

    for copy in pair[:4]:
        copy.start()
    for i in range(1, PLANES):
        for rel in range(2):
            query_copy(1 + 2 * i + rel, device(-ORDER[i], rel, c)).start()
    pair[4].start()

    def weight_copy(k):
        return pltpu.make_async_copy(
            w_ref.at[:, pl.ds(pl.multiple_of(k * COLS, HD), COLS)], wv.at[k], loc_sem.at[2 + k]
        )

    def start_weights(k, _):
        weight_copy(k).start()
        return 0

    lax.fori_loop(0, TP, start_weights, 0)

    kall[PAIR + 2 * ROWS :, :] = jnp.zeros((NEWPAD - 2 * ROWS, HD), BF16)
    vaug[PAIR : PAIR + ROWS, 0:HD] = nv_ref[...]
    vaug[PAIR + 2 * ROWS :, 0:HD] = jnp.zeros((NEWPAD - 2 * ROWS, HD), BF16)
    vaug[PAIR:, HD:] = jnp.ones((NEWPAD, HD), BF16)

    def live_rows(base, j):
        rows = lax.broadcasted_iota(jnp.int32, (STEP, HD), 0) + j * STEP
        return jnp.where(rows.astype(F32) < lens[base // CACHE, 0:1, :], 1.0, 0.0).astype(BF16)

    def mask_keys(base):
        first = kall[base : base + 16, :].astype(F32)[0:1, :]
        first = jnp.broadcast_to(first, (STEP, HD)).astype(BF16)

        def body(j, _):
            live = live_rows(base, j)
            rows = pl.ds(base + pl.multiple_of(j * STEP, STEP), STEP)
            kall[rows, :] = kall[rows, :] * live + first * (1.0 - live)
            return 0

        lax.fori_loop(LEAST // STEP, CACHE // STEP, body, 0)

    def mask_values(base):
        def ones(j, _):
            rows = pl.ds(base + pl.multiple_of(j * STEP, STEP), STEP)
            vaug[rows, HD:] = jnp.ones((STEP, HD), BF16)
            return 0

        lax.fori_loop(0, LEAST // STEP, ones, 0)

        def body(j, _):
            live = live_rows(base, j)
            rows = pl.ds(base + pl.multiple_of(j * STEP, STEP), STEP)
            vaug[rows, 0:HD] = vaug[rows, 0:HD] * live
            vaug[rows, HD:] = live
            return 0

        lax.fori_loop(LEAST // STEP, CACHE // STEP, body, 0)

    def tile_blocks(i):
        return 1 + PARTS * i, 1 + PARTS * (i + 1)

    def wait_queries(first, last):
        for k in range(first, last):
            if k != 1:
                query_copy(k, partner).wait_recv()

    def queries_of(first, last):
        return qbuf[first:last].reshape((last - first) * BLOCK, HD)

    def chunk(j):
        return pl.ds(pl.multiple_of(j * CHUNK, CHUNK), CHUNK)

    def scores(q, j, s_ref, mx):
        rows = q.shape[0]
        s = lax.dot_general(q, kall[chunk(j), :], NT, preferred_element_type=F32)
        s_ref[j, 0:rows, :] = s
        top = mx[0:rows, :]
        for u in range(CHUNK // HD):
            top = jnp.maximum(top, s[:, u * HD : (u + 1) * HD])
        mx[0:rows, :] = top

    def new_scores(first, q, t_ref, mx):
        rows = q.shape[0]
        row = lax.broadcasted_iota(jnp.int32, (rows, HD), 0)
        col = lax.broadcasted_iota(jnp.int32, (rows, HD), 1)
        r, r2 = row & 15, col & 15
        seen = (r2 >> 2) < (r >> 2)
        if first == 0:
            sibling_own = (row < BLOCK) & (col >= ROWS)
            mine = (row >= BLOCK) & (row < 2 * BLOCK) & (col < ROWS)
            seen = seen | ((sibling_own | mine) & ((r2 >> 2) == (r >> 2)) & (r2 <= r))
        s = lax.dot_general(q, kall[PAIR:, :], NT, preferred_element_type=F32)
        s = jnp.where(seen & (col < 2 * ROWS), s, -1e30)
        t_ref[0:rows, :] = s
        mx[0:rows, :] = s

    def close_max(rows, mx):
        mx[0:rows, :] = jnp.broadcast_to(
            jnp.max(mx[0:rows, :], axis=1, keepdims=True), (rows, HD)
        )

    def weights(s, top):
        return jnp.exp2((s - top) * SCALE2).astype(BF16)

    def chunk_weights(rows, j, s_ref, mx):
        top = mx[0:rows, :]
        return jnp.concatenate(
            [
                weights(s_ref[j, 0:rows, u * HD : (u + 1) * HD], top)
                for u in range(CHUNK // HD)
            ],
            axis=1,
        )

    def add_values(rows, j, p):
        acc[0:rows, :] += jnp.dot(p, vaug[chunk(j), :], preferred_element_type=F32)

    def new_values(rows, t_ref, mx):
        p = weights(t_ref[0:rows, :], mx[0:rows, :])
        acc[0:rows, :] = jnp.dot(p, vaug[PAIR:, :], preferred_element_type=F32)

    def as_rows(level):
        padded = jnp.concatenate([level, jnp.zeros((HD - BLOCK, HD), F32)], axis=0)
        row = jnp.transpose(padded)[0:8, :]
        high = row.astype(BF16).astype(F32)
        middle = (row - high).astype(BF16).astype(F32)
        low = row - high - middle
        place = lax.broadcasted_iota(jnp.int32, (8, HD), 0)
        terms = jnp.where(
            place == 0, high, jnp.where(place == 1, middle, jnp.where(place == 2, low, 0.0))
        )
        return jnp.concatenate([terms, jnp.zeros((8, HD), F32)], axis=0).astype(BF16)

    def result_copy(k, to, place=None):
        place = k if place is None else place
        return remote(nsend.at[k], nrecv.at[place], n_send.at[k], n_recv.at[place], to)

    def finish(first, last, mx):
        rows = (last - first) * BLOCK
        total = acc[0:rows, HD:]
        n = (acc[0:rows, :HD] / total).astype(BF16)
        level = mx[0:rows, :] * SCALE2 + jnp.log(total) * math.log2(math.e)
        for k in range(first, last):
            part = slice((k - first) * BLOCK, (k - first + 1) * BLOCK)
            nsend[k, 0:BLOCK, :] = n[part]
            nsend[k, BLOCK:, :] = as_rows(level[part])
            if k == 0:
                result_copy(0, sibling, 1).start()
            elif k == 1:
                nrecv[1] = nsend[1]
            else:
                result_copy(k, device(ORDER[(k - 1) // 2], (k - 1) % 2, c)).start()

    copy_k.wait()
    mask_keys(0)
    for copy in pair[:3]:
        copy.wait_recv()
    for core in range(2):
        @on_core(core)
        def _(first=FIRST[core][0], last=FIRST[core][1]):
            wait_queries(first, last)
            q = queries_of(first, last)
            new_scores(first, q, t0, mx0)

            def body(j, _):
                @pl.when(j == CHUNKS // 2)
                def _():
                    pair[3].wait_recv()
                    mask_keys(CACHE)

                scores(q, j, s0, mx0)
                return 0

            lax.fori_loop(0, CHUNKS, body, 0)
            close_max(q.shape[0], mx0)

    copy_v.wait()
    mask_values(0)

    def step(i, first, last):
        s_now, t_now, mx_now = ((s0, t0, mx0), (s1, t1, mx1))[i % 2]
        s_later, t_later, mx_later = ((s1, t1, mx1), (s0, t0, mx0))[i % 2]
        rows = (last - first) * BLOCK
        if i + 1 < TILES:
            wait_queries(*tile_blocks(i + 1))
            q = queries_of(*tile_blocks(i + 1))
            new_scores(tile_blocks(i + 1)[0], q, t_later, mx_later)
        new_values(rows, t_now, mx_now)

        def body(j, _):
            if i == 0:
                @pl.when(j == CHUNKS // 2)
                def _():
                    pair[4].wait_recv()
                    mask_values(CACHE)

            p = chunk_weights(rows, j, s_now, mx_now)
            if i + 1 < TILES:
                scores(q, j, s_later, mx_later)
            add_values(rows, j, p)
            return 0

        lax.fori_loop(0, CHUNKS, body, 0)
        if i + 1 < TILES:
            close_max(q.shape[0], mx_later)
        finish(first, last, mx_now)

    for core in range(2):
        @on_core(core)
        def _(first=FIRST[core][0], last=FIRST[core][1]):
            step(0, first, last)

    for i in range(1, TILES):
        step(i, *tile_blocks(i))

    def wait_result(k, _):
        result_copy(k, partner).wait_recv()
        return 0

    def level_of(v):
        terms = nrecv[v, BLOCK:, :].astype(F32)
        return jnp.broadcast_to(jnp.sum(terms, axis=0, keepdims=True), (8, HD))

    def as_columns(rows):
        place = lax.broadcasted_iota(jnp.int32, (8, HD), 0)
        packed = []
        for first in range(0, len(rows), 8):
            block = jnp.zeros((8, HD), F32)
            for v in range(first, min(first + 8, len(rows))):
                block = jnp.where(place == v - first, rows[v], block)
            packed.append(block)
        packed.append(jnp.zeros((HD - 8 * len(packed), HD), F32))
        return jnp.transpose(jnp.concatenate(packed, axis=0))[0:BLOCK, :]

    def largest(levels):
        top = levels[0]
        for level in levels[1:]:
            top = jnp.maximum(top, level)
        return top

    early = BLOCKS - PARTS

    @on_core(0)
    def _():
        wait_result(1, 0)

    lax.fori_loop(2, early, wait_result, 0)
    levels = [level_of(v) for v in range(1, early)]
    early_top = largest(levels)
    shares = [jnp.exp2(level - early_top) for level in levels]
    early_sum = sum(shares[1:], shares[0])
    share = as_columns(shares)
    early_total = jnp.zeros((BLOCK, HD), F32)
    for v in range(1, early):
        early_total = early_total + nrecv[v, 0:BLOCK, :].astype(F32) * share[:, v - 1 : v]

    lax.fori_loop(early, BLOCKS, wait_result, 0)
    levels = [early_top] + [level_of(v) for v in range(early, BLOCKS)]
    summit = largest(levels)
    shares = [jnp.exp2(level - summit) for level in levels]
    denom = sum(shares[1:], shares[0] * early_sum)
    share = as_columns([part / denom for part in shares])
    attention = early_total * share[:, 0:1]
    for k in range(PARTS):
        part = nrecv[early + k, 0:BLOCK, :].astype(F32)
        attention = attention + part * share[:, k + 1 : k + 2]
    attention = attention.astype(BF16)
    for g in range(HEADS):
        flat[:, g * HD : (g + 1) * HD] = attention[g * ROWS : (g + 1) * ROWS, :]

    def wait_weights(k, _):
        weight_copy(k).wait()
        return 0

    lax.fori_loop(0, TP, wait_weights, 0)

    def columns(i):
        return remote(
            psend.at[i], precv.at[i], p_send.at[i], p_recv.at[i],
            {"work": me, "tp": (t + i) % TP},
        )

    joined = flat[...]
    for i in (4, 5, 3, 2, 6, 7, 1):
        psend[i] = jnp.dot(joined, wv[(t + i) % TP], preferred_element_type=F32).astype(BF16)
        columns(i).start()
    total = jnp.dot(joined, wv[t], preferred_element_type=F32)

    def gather(i, total):
        columns(i).wait_recv()
        return total + precv[i].astype(F32)

    out_ref[...] = lax.fori_loop(1, TP, gather, total).astype(BF16)

    for copy in pair:
        copy.wait_send()

    def sent(k, _):
        query_copy(k, partner).wait_send()
        result_copy(k, partner).wait_send()
        return 0

    lax.fori_loop(2, BLOCKS, sent, 0)

    @on_core(0)
    def _():
        query_copy(0, sibling).wait_send()

    @on_core(1)
    def _():
        result_copy(0, sibling, 1).wait_send()


    def sent_columns(i, _):
        columns(i).wait_send()
        return 0

    lax.fori_loop(1, TP, sent_columns, 0)


def per_device(
    queries, new_keys, new_values, cache_keys, cache_values, lengths, positions, out_weight
):
    vmem = pl.BlockSpec(memory_space=pltpu.VMEM)
    smem = pl.BlockSpec(memory_space=pltpu.SMEM)
    anywhere = pl.BlockSpec(memory_space=pl.ANY)
    dma = pltpu.SemaphoreType.DMA
    out = pl.pallas_call(
        kernel,
        out_shape=jax.ShapeDtypeStruct((ROWS, COLS), BF16),
        in_specs=[smem, smem, vmem, vmem, vmem, anywhere, anywhere, anywhere],
        out_specs=vmem,
        scratch_shapes=[
            pltpu.VMEM((PAIR + NEWPAD, HD), BF16),
            pltpu.VMEM((PAIR + NEWPAD, 2 * HD), BF16),
            pltpu.VMEM((TP, COLS, COLS), BF16),
            pltpu.VMEM((BLOCKS, BLOCK, HD), BF16),
            pltpu.VMEM((BLOCKS, MESSAGE, HD), BF16),
            pltpu.VMEM((BLOCKS, MESSAGE, HD), BF16),
            pltpu.VMEM((CHUNKS, WIDEST, CHUNK), F32),
            pltpu.VMEM((CHUNKS, TILE, CHUNK), F32),
            pltpu.VMEM((WIDEST, HD), F32),
            pltpu.VMEM((TILE, HD), F32),
            pltpu.VMEM((WIDEST, HD), F32),
            pltpu.VMEM((TILE, HD), F32),
            pltpu.VMEM((WIDEST, 2 * HD), F32),
            pltpu.VMEM((ROWS, HEADS * HD), BF16),
            pltpu.VMEM((TP, ROWS, COLS), BF16),
            pltpu.VMEM((TP, ROWS, COLS), BF16),
            pltpu.VMEM((2, 8, HD), F32),
            dma((2 + TP,)),
            dma((5,)),
            dma((5,)),
            dma((BLOCKS,)),
            dma((BLOCKS,)),
            dma((BLOCKS,)),
            dma((BLOCKS,)),
            dma((TP,)),
            dma((TP,)),
        ],
        compiler_params=pltpu.CompilerParams(
            collective_id=0, has_side_effects=True, vmem_limit_bytes=58 * 1024 * 1024
        ),
    )(
        positions.reshape(ROWS),
        lengths,
        queries[0].transpose(1, 0, 2).reshape(BLOCK, HD),
        new_keys.reshape(ROWS, HD),
        new_values.reshape(ROWS, HD),
        cache_keys.reshape(CACHE, HD),
        cache_values.reshape(CACHE, HD),
        out_weight,
    )
    return out[None]


def solution(mesh):
    in_specs = (
        P("work", None, "tp", None),
        P("work", None, "tp", None),
        P("work", None, "tp", None),
        P("work", None, "tp", None),
        P("work", None, "tp", None),
        P("work"),
        P("work", None),
        P("tp", None),
    )
    out_specs = P("work", None, "tp")
    return jax.shard_map(
        per_device, mesh=mesh, in_specs=in_specs, out_specs=out_specs, check_vma=False
    )
```

```python
import math

import jax
import jax.numpy as jnp
from jax import lax
from jax.experimental import pallas as pl
from jax.experimental.pallas import tpu as pltpu
from jax.sharding import PartitionSpec as P

MESH = pl.DeviceIdType.MESH
F32 = jnp.float32
BF16 = jnp.bfloat16

HEADS = 5
ROWS = 16
HD = 128
CACHE = 4096
PAIR = 2 * CACHE
NEWPAD = 128
BLOCK = HEADS * ROWS
GROUP = 2
PARTS = 2 * GROUP
TILE = PARTS * BLOCK
CHUNK = 2048
CHUNKS = PAIR // CHUNK
TP = 8
COLS = 640
PLANES = 8
TILES = PLANES // GROUP
ORDER = (0, 2, 4, 6, 3, 5, 1, 7)
CODE = sum(d * PLANES**i for i, d in enumerate(ORDER))
SLOTS = 2 * PLANES
MESSAGE = BLOCK + 16
LEAST = 1024
STEP = 1024

SCALE2 = HD**-0.5 * math.log2(math.e)
LOG_BASE = math.log(1000000.0)
NT = (((1,), (1,)), ((), ()))


def cos_sin(angle):
    turn = jnp.floor(angle * (2.0 / math.pi) + 0.5)
    rest = angle - turn * 1.5703125
    rest = rest - turn * 4.837512969970703125e-4
    rest = rest - turn * 7.54978995489188e-8
    z = rest * rest
    sine = rest + rest * z * ((-1.9515295891e-4 * z + 8.3321608736e-3) * z - 1.6666654611e-1)
    cosine = 1.0 - 0.5 * z + z * z * (
        (2.443315711809948e-5 * z - 1.388731625493765e-3) * z + 4.166664568298827e-2
    )
    quarter = turn.astype(jnp.int32) & 3
    odd = (quarter & 1) == 1
    c = jnp.where(odd, sine, cosine)
    s = jnp.where(odd, cosine, sine)
    c = jnp.where((quarter == 1) | (quarter == 2), -c, c)
    s = jnp.where(quarter >= 2, -s, s)
    return c, s


def kernel(
    pos_ref, len_ref, q_ref, nk_ref, nv_ref, ck_ref, cv_ref, w_ref, out_ref,
    kall, vaug, wv, qbuf, nsend, nrecv, s0, s1, t0, t1, mx0, mx1, acc,
    flat, psend, precv, lens,
    loc_sem, pair_send, pair_recv, q_send, q_recv, n_send, n_recv,
    p_send, p_recv,
):
    me = lax.axis_index("work")
    t = lax.axis_index("tp")
    z = me // 4
    yh = (me // 2) % 2
    c = me % 2

    def device(d, rel, core):
        hi = (yh + rel) % 2
        return {"work": 4 * ((z + d + PLANES) % PLANES) + 2 * hi + core, "tp": t}

    def remote(src, dst, send, recv, to):
        return pltpu.make_async_remote_copy(
            src, dst, send, recv, device_id=to, device_id_type=MESH
        )

    sibling = device(0, 0, 1 - c)
    partner = device(0, 1, c)

    copy_k = pltpu.make_async_copy(ck_ref, kall.at[pl.ds(0, CACHE)], loc_sem.at[0])
    copy_v = pltpu.make_async_copy(
        cv_ref, vaug.at[pl.ds(0, CACHE), pl.ds(0, HD)], loc_sem.at[1]
    )
    copy_k.start()
    copy_v.start()

    barrier = pltpu.get_barrier_semaphore()

    def signal(to):
        pl.semaphore_signal(barrier, inc=1, device_id=to, device_id_type=MESH)

    def greet(i, _):
        signal(device(i // 2, i % 2, c))
        return 0

    lax.fori_loop(1, SLOTS, greet, 0)
    signal(sibling)

    def greet_tp(i, _):
        signal({"work": me, "tp": (t + i) % TP})
        return 0

    lax.fori_loop(1, TP, greet_tp, 0)

    lane = lax.broadcasted_iota(jnp.int32, (ROWS, HD), 1)
    place = pos_ref[0] + lax.broadcasted_iota(jnp.int32, (ROWS, HD), 0)
    ladder = (lane % (HD // 2)).astype(F32) * (2.0 / HD)
    angle = place.astype(F32) * jnp.exp(ladder * -LOG_BASE)
    cosine, sine = cos_sin(angle)
    sine = jnp.where(lane < HD // 2, -sine, sine)

    def rotated(x):
        x = x.astype(F32)
        return (x * cosine + pltpu.roll(x, HD // 2, 1) * sine).astype(BF16)

    for g in range(HEADS):
        qbuf[0, g * ROWS : (g + 1) * ROWS, :] = rotated(q_ref[g * ROWS : (g + 1) * ROWS, :])
    kall[PAIR : PAIR + ROWS, :] = rotated(nk_ref[...])
    lens[0] = jnp.full((8, HD), len_ref[0], jnp.int32).astype(F32)

    pl.semaphore_wait(barrier, SLOTS - 1 + 1 + TP - 1)

    def query_copy(k, d, rel):
        return remote(qbuf.at[0], qbuf.at[k], q_send.at[k], q_recv.at[k], device(-d, rel, c))

    pair = [
        remote(src, dst, pair_send.at[k], pair_recv.at[k], sibling)
        for k, (src, dst) in enumerate(
            (
                (lens.at[0], lens.at[1]),
                (kall.at[pl.ds(PAIR, ROWS)], kall.at[pl.ds(PAIR + ROWS, ROWS)]),
                (nv_ref, vaug.at[pl.ds(PAIR + ROWS, ROWS), pl.ds(0, HD)]),
                (ck_ref, kall.at[pl.ds(CACHE, CACHE)]),
                (cv_ref, vaug.at[pl.ds(CACHE, CACHE), pl.ds(0, HD)]),
            )
        )
    ]
    def send_queries(first, last):
        for i in range(first, last):
            for rel in range(2):
                query_copy(2 * i + rel, ORDER[i], rel).start()

    query_copy(1, 0, 1).start()
    send_queries(1, 2 * GROUP)
    for copy in pair:
        copy.start()
    send_queries(2 * GROUP, PLANES)

    def weight_copy(k):
        return pltpu.make_async_copy(
            w_ref.at[:, pl.ds(pl.multiple_of(k * COLS, HD), COLS)], wv.at[k], loc_sem.at[2 + k]
        )

    def start_weights(k, _):
        weight_copy(k).start()
        return 0

    lax.fori_loop(0, TP, start_weights, 0)

    kall[PAIR + 2 * ROWS :, :] = jnp.zeros((NEWPAD - 2 * ROWS, HD), BF16)
    vaug[PAIR : PAIR + ROWS, 0:HD] = nv_ref[...]
    vaug[PAIR + 2 * ROWS :, 0:HD] = jnp.zeros((NEWPAD - 2 * ROWS, HD), BF16)
    vaug[PAIR:, HD:] = jnp.ones((NEWPAD, HD), BF16)

    def live_rows(base, j):
        rows = lax.broadcasted_iota(jnp.int32, (STEP, HD), 0) + j * STEP
        return jnp.where(rows.astype(F32) < lens[base // CACHE, 0:1, :], 1.0, 0.0).astype(BF16)

    def mask_keys(base):
        first = kall[base : base + 16, :].astype(F32)[0:1, :]
        first = jnp.broadcast_to(first, (STEP, HD)).astype(BF16)

        def body(j, _):
            live = live_rows(base, j)
            rows = pl.ds(base + pl.multiple_of(j * STEP, STEP), STEP)
            kall[rows, :] = kall[rows, :] * live + first * (1.0 - live)
            return 0

        lax.fori_loop(LEAST // STEP, CACHE // STEP, body, 0)

    def mask_values(base):
        def ones(j, _):
            rows = pl.ds(base + pl.multiple_of(j * STEP, STEP), STEP)
            vaug[rows, HD:] = jnp.ones((STEP, HD), BF16)
            return 0

        lax.fori_loop(0, LEAST // STEP, ones, 0)

        def body(j, _):
            live = live_rows(base, j)
            rows = pl.ds(base + pl.multiple_of(j * STEP, STEP), STEP)
            vaug[rows, 0:HD] = vaug[rows, 0:HD] * live
            vaug[rows, HD:] = live
            return 0

        lax.fori_loop(LEAST // STEP, CACHE // STEP, body, 0)

    def wait_queries(i):
        for part in range(PARTS):
            query_copy(PARTS * i + part, 0, 1).wait_recv()

    def queries_of(i):
        return qbuf[pl.ds(PARTS * i, PARTS)].reshape(TILE, HD)

    def chunk(j):
        return pl.ds(pl.multiple_of(j * CHUNK, CHUNK), CHUNK)

    def scores(q, j, s_ref, mx):
        s = lax.dot_general(q, kall[chunk(j), :], NT, preferred_element_type=F32)
        s_ref[j] = s
        top = mx[...]
        for u in range(CHUNK // HD):
            top = jnp.maximum(top, s[:, u * HD : (u + 1) * HD])
        mx[...] = top

    def new_scores(first, q, t_ref, mx):
        row = lax.broadcasted_iota(jnp.int32, (TILE, HD), 0)
        col = lax.broadcasted_iota(jnp.int32, (TILE, HD), 1)
        r, r2 = row & 15, col & 15
        seen = (r2 >> 2) < (r >> 2)
        if first:
            own = (row < BLOCK) & (col < ROWS)
            seen = seen | (own & ((r2 >> 2) == (r >> 2)) & (r2 <= r))
        s = lax.dot_general(q, kall[PAIR:, :], NT, preferred_element_type=F32)
        s = jnp.where(seen & (col < 2 * ROWS), s, -1e30)
        t_ref[...] = s
        mx[...] = s

    def close_max(mx):
        mx[...] = jnp.broadcast_to(jnp.max(mx[...], axis=1, keepdims=True), (TILE, HD))

    def weights(s, top):
        return jnp.exp2((s - top) * SCALE2).astype(BF16)

    def chunk_weights(j, s_ref, mx):
        top = mx[...]
        return jnp.concatenate(
            [weights(s_ref[j, :, u * HD : (u + 1) * HD], top) for u in range(CHUNK // HD)], axis=1
        )

    def add_values(j, p):
        acc[...] += jnp.dot(p, vaug[chunk(j), :], preferred_element_type=F32)

    def new_values(t_ref, mx):
        p = weights(t_ref[...], mx[...])
        acc[...] = jnp.dot(p, vaug[PAIR:, :], preferred_element_type=F32)

    def as_rows(level):
        padded = jnp.concatenate([level, jnp.zeros((HD - BLOCK, HD), F32)], axis=0)
        row = jnp.transpose(padded)[0:8, :]
        high = row.astype(BF16).astype(F32)
        middle = (row - high).astype(BF16).astype(F32)
        low = row - high - middle
        place = lax.broadcasted_iota(jnp.int32, (8, HD), 0)
        terms = jnp.where(
            place == 0, high, jnp.where(place == 1, middle, jnp.where(place == 2, low, 0.0))
        )
        return jnp.concatenate([terms, jnp.zeros((8, HD), F32)], axis=0).astype(BF16)

    def result_copy(k, d, rel):
        return remote(nsend.at[k], nrecv.at[k], n_send.at[k], n_recv.at[k], device(d, rel, c))

    def finish(i, code, mx, maybe_first):
        total = acc[:, HD:]
        n = (acc[:, :HD] / total).astype(BF16)
        level = mx[...] * SCALE2 + jnp.log(total) * math.log2(math.e)
        for part in range(PARTS):
            rows = slice(part * BLOCK, (part + 1) * BLOCK)
            k = PARTS * i + part
            nsend[k, 0:BLOCK, :] = n[rows]
            nsend[k, BLOCK:, :] = as_rows(level[rows])
            copy = result_copy(k, (code // PLANES ** (part // 2)) % PLANES, part % 2)
            if maybe_first and part == 0:
                @pl.when(i > 0)
                def _():
                    copy.start()

                @pl.when(i == 0)
                def _():
                    nrecv[0] = nsend[0]
            else:
                copy.start()
        return code // PLANES**GROUP

    copy_k.wait()
    mask_keys(0)
    for copy in pair[:3]:
        copy.wait_recv()
    for part in range(1, PARTS):
        query_copy(part, 0, 1).wait_recv()
    q = queries_of(0)
    new_scores(True, q, t0, mx0)

    def first_scores(j, _):
        @pl.when(j == CHUNKS // 2)
        def _():
            pair[3].wait_recv()
            mask_keys(CACHE)

        scores(q, j, s0, mx0)
        return 0

    lax.fori_loop(0, CHUNKS, first_scores, 0)
    close_max(mx0)
    copy_v.wait()
    mask_values(0)

    def both(i, s_now, t_now, mx_now, s_later, t_later, mx_later, maybe_first):
        wait_queries(i + 1)
        q = queries_of(i + 1)
        new_scores(False, q, t_later, mx_later)
        new_values(t_now, mx_now)

        def body(j, _):
            if maybe_first:
                @pl.when((i == 0) & (j == CHUNKS // 2))
                def _():
                    pair[4].wait_recv()
                    mask_values(CACHE)

            p = chunk_weights(j, s_now, mx_now)
            scores(q, j, s_later, mx_later)
            add_values(j, p)
            return 0

        lax.fori_loop(0, CHUNKS, body, 0)
        close_max(mx_later)

    def two_tiles(k, code):
        i = 2 * k
        both(i, s0, t0, mx0, s1, t1, mx1, True)
        code = finish(i, code, mx0, True)

        @pl.when(i + 2 < TILES)
        def _():
            both(i + 1, s1, t1, mx1, s0, t0, mx0, False)

        @pl.when(i + 2 == TILES)
        def _():
            new_values(t1, mx1)

            def body(j, _):
                add_values(j, chunk_weights(j, s1, mx1))
                return 0

            lax.fori_loop(0, CHUNKS, body, 0)

        return finish(i + 1, code, mx1, False)

    lax.fori_loop(0, TILES // 2, two_tiles, CODE)

    def wait_result(k, _):
        result_copy(k, 0, 1).wait_recv()
        return 0

    def level_of(v):
        terms = nrecv[v, BLOCK:, :].astype(F32)
        return jnp.broadcast_to(jnp.sum(terms, axis=0, keepdims=True), (8, HD))

    def as_columns(rows):
        place = lax.broadcasted_iota(jnp.int32, (8, HD), 0)
        packed = []
        for first in range(0, len(rows), 8):
            block = jnp.zeros((8, HD), F32)
            for v in range(first, min(first + 8, len(rows))):
                block = jnp.where(place == v - first, rows[v], block)
            packed.append(block)
        packed.append(jnp.zeros((HD - 8 * len(packed), HD), F32))
        return jnp.transpose(jnp.concatenate(packed, axis=0))[0:BLOCK, :]

    def largest(levels):
        top = levels[0]
        for level in levels[1:]:
            top = jnp.maximum(top, level)
        return top

    early = SLOTS - PARTS
    lax.fori_loop(1, early, wait_result, 0)
    levels = [level_of(v) for v in range(early)]
    early_top = largest(levels)
    shares = [jnp.exp2(level - early_top) for level in levels]
    early_sum = sum(shares[1:], shares[0])
    share = as_columns(shares)
    early_total = jnp.zeros((BLOCK, HD), F32)
    for v in range(early):
        early_total = early_total + nrecv[v, 0:BLOCK, :].astype(F32) * share[:, v : v + 1]

    lax.fori_loop(early, SLOTS, wait_result, 0)
    levels = [early_top] + [level_of(v) for v in range(early, SLOTS)]
    summit = largest(levels)
    shares = [jnp.exp2(level - summit) for level in levels]
    denom = sum(shares[1:], shares[0] * early_sum)
    share = as_columns([part / denom for part in shares])
    attention = early_total * share[:, 0:1]
    for k in range(PARTS):
        part = nrecv[early + k, 0:BLOCK, :].astype(F32)
        attention = attention + part * share[:, k + 1 : k + 2]
    attention = attention.astype(BF16)
    for g in range(HEADS):
        flat[:, g * HD : (g + 1) * HD] = attention[g * ROWS : (g + 1) * ROWS, :]

    def wait_weights(k, _):
        weight_copy(k).wait()
        return 0

    lax.fori_loop(0, TP, wait_weights, 0)

    def columns(i):
        return remote(
            psend.at[i], precv.at[i], p_send.at[i], p_recv.at[i],
            {"work": me, "tp": (t + i) % TP},
        )

    joined = flat[...]
    for i in (4, 5, 3, 2, 6, 7, 1):
        psend[i] = jnp.dot(joined, wv[(t + i) % TP], preferred_element_type=F32).astype(BF16)
        columns(i).start()
    total = jnp.dot(joined, wv[t], preferred_element_type=F32)

    def gather(i, total):
        columns(i).wait_recv()
        return total + precv[i].astype(F32)

    out_ref[...] = lax.fori_loop(1, TP, gather, total).astype(BF16)

    for copy in pair:
        copy.wait_send()

    def sent(k, _):
        query_copy(k, 0, 1).wait_send()
        result_copy(k, 0, 1).wait_send()
        return 0

    lax.fori_loop(1, SLOTS, sent, 0)

    def sent_columns(i, _):
        columns(i).wait_send()
        return 0

    lax.fori_loop(1, TP, sent_columns, 0)


def per_device(
    queries, new_keys, new_values, cache_keys, cache_values, lengths, positions, out_weight
):
    vmem = pl.BlockSpec(memory_space=pltpu.VMEM)
    smem = pl.BlockSpec(memory_space=pltpu.SMEM)
    anywhere = pl.BlockSpec(memory_space=pl.ANY)
    dma = pltpu.SemaphoreType.DMA
    out = pl.pallas_call(
        kernel,
        out_shape=jax.ShapeDtypeStruct((ROWS, COLS), BF16),
        in_specs=[smem, smem, vmem, vmem, vmem, anywhere, anywhere, anywhere],
        out_specs=vmem,
        scratch_shapes=[
            pltpu.VMEM((PAIR + NEWPAD, HD), BF16),
            pltpu.VMEM((PAIR + NEWPAD, 2 * HD), BF16),
            pltpu.VMEM((TP, COLS, COLS), BF16),
            pltpu.VMEM((SLOTS, BLOCK, HD), BF16),
            pltpu.VMEM((SLOTS, MESSAGE, HD), BF16),
            pltpu.VMEM((SLOTS, MESSAGE, HD), BF16),
            pltpu.VMEM((CHUNKS, TILE, CHUNK), F32),
            pltpu.VMEM((CHUNKS, TILE, CHUNK), F32),
            pltpu.VMEM((TILE, HD), F32),
            pltpu.VMEM((TILE, HD), F32),
            pltpu.VMEM((TILE, HD), F32),
            pltpu.VMEM((TILE, HD), F32),
            pltpu.VMEM((TILE, 2 * HD), F32),
            pltpu.VMEM((ROWS, HEADS * HD), BF16),
            pltpu.VMEM((TP, ROWS, COLS), BF16),
            pltpu.VMEM((TP, ROWS, COLS), BF16),
            pltpu.VMEM((2, 8, HD), F32),
            dma((2 + TP,)),
            dma((5,)),
            dma((5,)),
            dma((SLOTS,)),
            dma((SLOTS,)),
            dma((SLOTS,)),
            dma((SLOTS,)),
            dma((TP,)),
            dma((TP,)),
        ],
        compiler_params=pltpu.CompilerParams(
            collective_id=0, has_side_effects=True, vmem_limit_bytes=58 * 1024 * 1024
        ),
    )(
        positions.reshape(ROWS),
        lengths,
        queries[0].transpose(1, 0, 2).reshape(BLOCK, HD),
        new_keys.reshape(ROWS, HD),
        new_values.reshape(ROWS, HD),
        cache_keys.reshape(CACHE, HD),
        cache_values.reshape(CACHE, HD),
        out_weight,
    )
    return out[None]


def solution(mesh):
    in_specs = (
        P("work", None, "tp", None),
        P("work", None, "tp", None),
        P("work", None, "tp", None),
        P("work", None, "tp", None),
        P("work", None, "tp", None),
        P("work"),
        P("work", None),
        P("tp", None),
    )
    out_specs = P("work", None, "tp")
    return jax.shard_map(
        per_device, mesh=mesh, in_specs=in_specs, out_specs=out_specs, check_vma=False
    )
```

```python
import math

import jax
import jax.numpy as jnp
from jax import lax
from jax.experimental import pallas as pl
from jax.experimental.pallas import tpu as pltpu
from jax.sharding import PartitionSpec as P

MESH = pl.DeviceIdType.MESH
F32 = jnp.float32
BF16 = jnp.bfloat16

HEADS = 5
ROWS = 16
HD = 128
CACHE = 4096
PAIR = 2 * CACHE
NEWPAD = 128
BLOCK = HEADS * ROWS
GROUP = 2
PARTS = 2 * GROUP
TILE = PARTS * BLOCK
CHUNK = 2048
CHUNKS = CACHE // CHUNK
TP = 8
COLS = 640
PLANES = 8
TILES = PLANES // GROUP
ORDER = (0, 7, 3, 5, 4, 2, 6, 1)
UNITS = ((0, 0), (1, 0), (2, 0), (0, 1), (3, 0), (1, 1), (2, 1), (3, 1))
SLOTS = 2 * PLANES
MESSAGE = BLOCK + 16
LEAST = 1024
STEP = 1024

SCALE2 = HD**-0.5 * math.log2(math.e)
LOG_BASE = math.log(1000000.0)
NT = (((1,), (1,)), ((), ()))


def cos_sin(angle):
    turn = jnp.floor(angle * (2.0 / math.pi) + 0.5)
    rest = angle - turn * 1.5703125
    rest = rest - turn * 4.837512969970703125e-4
    rest = rest - turn * 7.54978995489188e-8
    z = rest * rest
    sine = rest + rest * z * ((-1.9515295891e-4 * z + 8.3321608736e-3) * z - 1.6666654611e-1)
    cosine = 1.0 - 0.5 * z + z * z * (
        (2.443315711809948e-5 * z - 1.388731625493765e-3) * z + 4.166664568298827e-2
    )
    quarter = turn.astype(jnp.int32) & 3
    odd = (quarter & 1) == 1
    c = jnp.where(odd, sine, cosine)
    s = jnp.where(odd, cosine, sine)
    c = jnp.where((quarter == 1) | (quarter == 2), -c, c)
    s = jnp.where(quarter >= 2, -s, s)
    return c, s


def kernel(
    pos_ref, len_ref, q_ref, nk_ref, nv_ref, ck_ref, cv_ref, w_ref, out_ref,
    kall, vaug, wv, qbuf, nsend, nrecv, s0, s1, t0, t1, tops, acc,
    flat, psend, precv, lens,
    loc_sem, pair_send, pair_recv, q_send, q_recv, n_send, n_recv,
    p_send, p_recv,
):
    me = lax.axis_index("work")
    t = lax.axis_index("tp")
    z = me // 4
    yh = (me // 2) % 2
    c = me % 2

    def device(d, rel, core):
        hi = (yh + rel) % 2
        return {"work": 4 * ((z + d + PLANES) % PLANES) + 2 * hi + core, "tp": t}

    def remote(src, dst, send, recv, to):
        return pltpu.make_async_remote_copy(
            src, dst, send, recv, device_id=to, device_id_type=MESH
        )

    sibling = device(0, 0, 1 - c)
    partner = device(0, 1, c)

    copy_k = pltpu.make_async_copy(ck_ref, kall.at[pl.ds(0, CACHE)], loc_sem.at[0])
    copy_v = pltpu.make_async_copy(
        cv_ref, vaug.at[pl.ds(0, CACHE), pl.ds(0, HD)], loc_sem.at[1]
    )
    copy_k.start()
    copy_v.start()

    barrier = pltpu.get_barrier_semaphore()

    def signal(to):
        pl.semaphore_signal(barrier, inc=1, device_id=to, device_id_type=MESH)

    def greet(i, _):
        signal(device(i // 2, i % 2, c))
        return 0

    lax.fori_loop(1, SLOTS, greet, 0)
    signal(sibling)

    def greet_tp(i, _):
        signal({"work": me, "tp": (t + i) % TP})
        return 0

    lax.fori_loop(1, TP, greet_tp, 0)

    lane = lax.broadcasted_iota(jnp.int32, (ROWS, HD), 1)
    place = pos_ref[0] + lax.broadcasted_iota(jnp.int32, (ROWS, HD), 0)
    ladder = (lane % (HD // 2)).astype(F32) * (2.0 / HD)
    angle = place.astype(F32) * jnp.exp(ladder * -LOG_BASE)
    cosine, sine = cos_sin(angle)
    sine = jnp.where(lane < HD // 2, -sine, sine)

    def rotated(x):
        x = x.astype(F32)
        return (x * cosine + pltpu.roll(x, HD // 2, 1) * sine).astype(BF16)

    for g in range(HEADS):
        qbuf[0, g * ROWS : (g + 1) * ROWS, :] = rotated(q_ref[g * ROWS : (g + 1) * ROWS, :])
    kall[PAIR : PAIR + ROWS, :] = rotated(nk_ref[...])
    lens[0] = jnp.full((8, HD), len_ref[0], jnp.int32).astype(F32)

    pl.semaphore_wait(barrier, SLOTS - 1 + 1 + TP - 1)

    def query_copy(k, d, rel):
        return remote(qbuf.at[0], qbuf.at[k], q_send.at[k], q_recv.at[k], device(-d, rel, c))

    pair = [
        remote(src, dst, pair_send.at[k], pair_recv.at[k], sibling)
        for k, (src, dst) in enumerate(
            (
                (lens.at[0], lens.at[1]),
                (kall.at[pl.ds(PAIR, ROWS)], kall.at[pl.ds(PAIR + ROWS, ROWS)]),
                (nv_ref, vaug.at[pl.ds(PAIR + ROWS, ROWS), pl.ds(0, HD)]),
                (ck_ref, kall.at[pl.ds(CACHE, CACHE)]),
                (cv_ref, vaug.at[pl.ds(CACHE, CACHE), pl.ds(0, HD)]),
            )
        )
    ]
    def send_queries(first, last):
        for i in range(first, last):
            for rel in range(2):
                query_copy(2 * i + rel, ORDER[i], rel).start()

    query_copy(1, 0, 1).start()
    send_queries(1, GROUP)
    for copy in pair[:3]:
        copy.start()
    send_queries(GROUP, 2 * GROUP)
    pair[3].start()
    send_queries(2 * GROUP, 3 * GROUP)
    pair[4].start()
    send_queries(3 * GROUP, PLANES)

    def weight_copy(k):
        return pltpu.make_async_copy(
            w_ref.at[:, pl.ds(pl.multiple_of(k * COLS, HD), COLS)], wv.at[k], loc_sem.at[2 + k]
        )

    def start_weights(k, _):
        weight_copy(k).start()
        return 0

    lax.fori_loop(0, TP, start_weights, 0)

    kall[PAIR + 2 * ROWS :, :] = jnp.zeros((NEWPAD - 2 * ROWS, HD), BF16)
    vaug[PAIR : PAIR + ROWS, 0:HD] = nv_ref[...]
    vaug[PAIR + 2 * ROWS :, 0:HD] = jnp.zeros((NEWPAD - 2 * ROWS, HD), BF16)
    vaug[PAIR:, HD:] = jnp.ones((NEWPAD, HD), BF16)

    def live_rows(base, j):
        rows = lax.broadcasted_iota(jnp.int32, (STEP, HD), 0) + j * STEP
        return jnp.where(rows.astype(F32) < lens[base // CACHE, 0:1, :], 1.0, 0.0).astype(BF16)

    def mask_keys(base):
        first = kall[base : base + 16, :].astype(F32)[0:1, :]
        first = jnp.broadcast_to(first, (STEP, HD)).astype(BF16)

        def body(j, _):
            live = live_rows(base, j)
            rows = pl.ds(base + pl.multiple_of(j * STEP, STEP), STEP)
            kall[rows, :] = kall[rows, :] * live + first * (1.0 - live)
            return 0

        lax.fori_loop(LEAST // STEP, CACHE // STEP, body, 0)

    def mask_values(base):
        def ones(j, _):
            rows = pl.ds(base + pl.multiple_of(j * STEP, STEP), STEP)
            vaug[rows, HD:] = jnp.ones((STEP, HD), BF16)
            return 0

        lax.fori_loop(0, LEAST // STEP, ones, 0)

        def body(j, _):
            live = live_rows(base, j)
            rows = pl.ds(base + pl.multiple_of(j * STEP, STEP), STEP)
            vaug[rows, 0:HD] = vaug[rows, 0:HD] * live
            vaug[rows, HD:] = live
            return 0

        lax.fori_loop(LEAST // STEP, CACHE // STEP, body, 0)

    def wait_queries(i):
        for part in range(PARTS):
            if (i, part) != (0, 0):
                query_copy(PARTS * i + part, 0, 1).wait_recv()

    def queries_of(i):
        return qbuf[PARTS * i : PARTS * (i + 1)].reshape(TILE, HD)

    def chunk(half, j):
        return pl.ds(half * CACHE + pl.multiple_of(j * CHUNK, CHUNK), CHUNK)

    def open_scores(i, half, q, t_ref):
        if half:
            tops[1, i] = tops[0, i]
            return
        row = lax.broadcasted_iota(jnp.int32, (TILE, HD), 0)
        col = lax.broadcasted_iota(jnp.int32, (TILE, HD), 1)
        r, r2 = row & 15, col & 15
        seen = (r2 >> 2) < (r >> 2)
        if i == 0:
            own = (row < BLOCK) & (col < ROWS)
            seen = seen | (own & ((r2 >> 2) == (r >> 2)) & (r2 <= r))
        s = lax.dot_general(q, kall[PAIR:, :], NT, preferred_element_type=F32)
        s = jnp.where(seen & (col < 2 * ROWS), s, -1e30)
        t_ref[...] = s
        tops[0, i] = s

    def scores(i, half, q, j, s_ref):
        s = lax.dot_general(q, kall[chunk(half, j), :], NT, preferred_element_type=F32)
        s_ref[j] = s
        top = tops[half, i]
        for u in range(CHUNK // HD):
            top = jnp.maximum(top, s[:, u * HD : (u + 1) * HD])
        tops[half, i] = top

    def close_scores(i, half):
        tops[half, i] = jnp.broadcast_to(
            jnp.max(tops[half, i], axis=1, keepdims=True), (TILE, HD)
        )

    def weights(s, top):
        return jnp.exp2((s - top) * SCALE2).astype(BF16)

    def open_values(i, half, t_ref):
        if half:
            shrink = jnp.exp2((tops[0, i] - tops[1, i]) * SCALE2)
            acc[i, :, :HD] = acc[i, :, :HD] * shrink
            acc[i, :, HD:] = acc[i, :, HD:] * shrink
        else:
            p = weights(t_ref[...], tops[0, i])
            acc[i] = jnp.dot(p, vaug[PAIR:, :], preferred_element_type=F32)

    def chunk_weights(i, half, j, s_ref):
        top = tops[half, i]
        return jnp.concatenate(
            [weights(s_ref[j, :, u * HD : (u + 1) * HD], top) for u in range(CHUNK // HD)], axis=1
        )

    def add_values(i, half, j, p):
        acc[i] += jnp.dot(p, vaug[chunk(half, j), :], preferred_element_type=F32)

    def as_rows(level):
        padded = jnp.concatenate([level, jnp.zeros((HD - BLOCK, HD), F32)], axis=0)
        row = jnp.transpose(padded)[0:8, :]
        high = row.astype(BF16).astype(F32)
        middle = (row - high).astype(BF16).astype(F32)
        low = row - high - middle
        place = lax.broadcasted_iota(jnp.int32, (8, HD), 0)
        terms = jnp.where(
            place == 0, high, jnp.where(place == 1, middle, jnp.where(place == 2, low, 0.0))
        )
        return jnp.concatenate([terms, jnp.zeros((8, HD), F32)], axis=0).astype(BF16)

    def result_copy(k, d, rel):
        return remote(nsend.at[k], nrecv.at[k], n_send.at[k], n_recv.at[k], device(d, rel, c))

    def finish(i):
        total = acc[i, :, HD:]
        n = (acc[i, :, :HD] / total).astype(BF16)
        level = tops[1, i] * SCALE2 + jnp.log(total) * math.log2(math.e)
        for part in range(PARTS):
            rows = slice(part * BLOCK, (part + 1) * BLOCK)
            k = PARTS * i + part
            nsend[k, 0:BLOCK, :] = n[rows]
            nsend[k, BLOCK:, :] = as_rows(level[rows])
            if k == 0:
                nrecv[0] = nsend[0]
            else:
                result_copy(k, ORDER[k // 2], k % 2).start()

    def ready_keys(i, half):
        if half == 0:
            wait_queries(i)
        elif i == 0:
            pair[3].wait_recv()
            mask_keys(CACHE)

    def ready_values(i, half):
        if (i, half) == (0, 0):
            copy_v.wait()
            mask_values(0)
        elif i == 0:
            pair[4].wait_recv()
            mask_values(CACHE)

    copy_k.wait()
    mask_keys(0)
    for copy in pair[:3]:
        copy.wait_recv()

    for n in range(-1, len(UNITS)):
        now = UNITS[n] if n >= 0 else None
        later = UNITS[n + 1] if n + 1 < len(UNITS) else None
        s_now, t_now = ((s0, t0), (s1, t1))[n % 2]
        s_later, t_later = ((s1, t1), (s0, t0))[n % 2]
        q = None
        if later is not None:
            ready_keys(*later)
            q = queries_of(later[0])
            open_scores(*later, q, t_later)
        if now is not None:
            ready_values(*now)
            open_values(*now, t_now)

        def body(j, _, now=now, later=later, s_now=s_now, s_later=s_later, q=q):
            if now is not None:
                p = chunk_weights(*now, j, s_now)
            if later is not None:
                scores(*later, q, j, s_later)
            if now is not None:
                add_values(*now, j, p)
            return 0

        lax.fori_loop(0, CHUNKS, body, 0)
        if later is not None:
            close_scores(*later)
        if now is not None and now[1] == 1:
            finish(now[0])

    def wait_result(k, _):
        result_copy(k, 0, 1).wait_recv()
        return 0

    def level_of(v):
        terms = nrecv[v, BLOCK:, :].astype(F32)
        return jnp.broadcast_to(jnp.sum(terms, axis=0, keepdims=True), (8, HD))

    def as_columns(rows):
        place = lax.broadcasted_iota(jnp.int32, (8, HD), 0)
        packed = []
        for first in range(0, len(rows), 8):
            block = jnp.zeros((8, HD), F32)
            for v in range(first, min(first + 8, len(rows))):
                block = jnp.where(place == v - first, rows[v], block)
            packed.append(block)
        packed.append(jnp.zeros((HD - 8 * len(packed), HD), F32))
        return jnp.transpose(jnp.concatenate(packed, axis=0))[0:BLOCK, :]

    def largest(levels):
        top = levels[0]
        for level in levels[1:]:
            top = jnp.maximum(top, level)
        return top

    early = SLOTS - PARTS
    lax.fori_loop(1, early, wait_result, 0)
    levels = [level_of(v) for v in range(early)]
    early_top = largest(levels)
    shares = [jnp.exp2(level - early_top) for level in levels]
    early_sum = sum(shares[1:], shares[0])
    share = as_columns(shares)
    early_total = jnp.zeros((BLOCK, HD), F32)
    for v in range(early):
        early_total = early_total + nrecv[v, 0:BLOCK, :].astype(F32) * share[:, v : v + 1]

    lax.fori_loop(early, SLOTS, wait_result, 0)
    levels = [early_top] + [level_of(v) for v in range(early, SLOTS)]
    summit = largest(levels)
    shares = [jnp.exp2(level - summit) for level in levels]
    denom = sum(shares[1:], shares[0] * early_sum)
    share = as_columns([part / denom for part in shares])
    attention = early_total * share[:, 0:1]
    for k in range(PARTS):
        part = nrecv[early + k, 0:BLOCK, :].astype(F32)
        attention = attention + part * share[:, k + 1 : k + 2]
    attention = attention.astype(BF16)
    for g in range(HEADS):
        flat[:, g * HD : (g + 1) * HD] = attention[g * ROWS : (g + 1) * ROWS, :]

    def wait_weights(k, _):
        weight_copy(k).wait()
        return 0

    lax.fori_loop(0, TP, wait_weights, 0)

    def columns(i):
        return remote(
            psend.at[i], precv.at[i], p_send.at[i], p_recv.at[i],
            {"work": me, "tp": (t + i) % TP},
        )

    joined = flat[...]
    for i in (4, 5, 3, 2, 6, 7, 1):
        psend[i] = jnp.dot(joined, wv[(t + i) % TP], preferred_element_type=F32).astype(BF16)
        columns(i).start()
    total = jnp.dot(joined, wv[t], preferred_element_type=F32)

    def gather(i, total):
        columns(i).wait_recv()
        return total + precv[i].astype(F32)

    out_ref[...] = lax.fori_loop(1, TP, gather, total).astype(BF16)

    for copy in pair:
        copy.wait_send()

    def sent(k, _):
        query_copy(k, 0, 1).wait_send()
        result_copy(k, 0, 1).wait_send()
        return 0

    lax.fori_loop(1, SLOTS, sent, 0)

    def sent_columns(i, _):
        columns(i).wait_send()
        return 0

    lax.fori_loop(1, TP, sent_columns, 0)


def per_device(
    queries, new_keys, new_values, cache_keys, cache_values, lengths, positions, out_weight
):
    vmem = pl.BlockSpec(memory_space=pltpu.VMEM)
    smem = pl.BlockSpec(memory_space=pltpu.SMEM)
    anywhere = pl.BlockSpec(memory_space=pl.ANY)
    dma = pltpu.SemaphoreType.DMA
    out = pl.pallas_call(
        kernel,
        out_shape=jax.ShapeDtypeStruct((ROWS, COLS), BF16),
        in_specs=[smem, smem, vmem, vmem, vmem, anywhere, anywhere, anywhere],
        out_specs=vmem,
        scratch_shapes=[
            pltpu.VMEM((PAIR + NEWPAD, HD), BF16),
            pltpu.VMEM((PAIR + NEWPAD, 2 * HD), BF16),
            pltpu.VMEM((TP, COLS, COLS), BF16),
            pltpu.VMEM((SLOTS, BLOCK, HD), BF16),
            pltpu.VMEM((SLOTS, MESSAGE, HD), BF16),
            pltpu.VMEM((SLOTS, MESSAGE, HD), BF16),
            pltpu.VMEM((CHUNKS, TILE, CHUNK), F32),
            pltpu.VMEM((CHUNKS, TILE, CHUNK), F32),
            pltpu.VMEM((TILE, HD), F32),
            pltpu.VMEM((TILE, HD), F32),
            pltpu.VMEM((2, TILES, TILE, HD), F32),
            pltpu.VMEM((TILES, TILE, 2 * HD), F32),
            pltpu.VMEM((ROWS, HEADS * HD), BF16),
            pltpu.VMEM((TP, ROWS, COLS), BF16),
            pltpu.VMEM((TP, ROWS, COLS), BF16),
            pltpu.VMEM((2, 8, HD), F32),
            dma((2 + TP,)),
            dma((5,)),
            dma((5,)),
            dma((SLOTS,)),
            dma((SLOTS,)),
            dma((SLOTS,)),
            dma((SLOTS,)),
            dma((TP,)),
            dma((TP,)),
        ],
        compiler_params=pltpu.CompilerParams(
            collective_id=0, has_side_effects=True, vmem_limit_bytes=58 * 1024 * 1024
        ),
    )(
        positions.reshape(ROWS),
        lengths,
        queries[0].transpose(1, 0, 2).reshape(BLOCK, HD),
        new_keys.reshape(ROWS, HD),
        new_values.reshape(ROWS, HD),
        cache_keys.reshape(CACHE, HD),
        cache_values.reshape(CACHE, HD),
        out_weight,
    )
    return out[None]


def solution(mesh):
    in_specs = (
        P("work", None, "tp", None),
        P("work", None, "tp", None),
        P("work", None, "tp", None),
        P("work", None, "tp", None),
        P("work", None, "tp", None),
        P("work"),
        P("work", None),
        P("tp", None),
    )
    out_specs = P("work", None, "tp")
    return jax.shard_map(
        per_device, mesh=mesh, in_specs=in_specs, out_specs=out_specs, check_vma=False
    )
```

```python
import math

import jax
import jax.numpy as jnp
from jax import lax
from jax.experimental import pallas as pl
from jax.experimental.pallas import tpu as pltpu
from jax.sharding import PartitionSpec as P

MESH = pl.DeviceIdType.MESH
F32 = jnp.float32
BF16 = jnp.bfloat16

HEADS = 5
ROWS = 16
HD = 128
CACHE = 4096
PAIR = 2 * CACHE
NEWPAD = 128
BLOCK = HEADS * ROWS
GROUP = 2
PARTS = 2 * GROUP
TILE = PARTS * BLOCK
CHUNK = 2048
CHUNKS = PAIR // CHUNK
TP = 8
COLS = 640
PLANES = 8
ORDER = (0, 3, 5, 4, 6, 2, 7, 1)
BLOCKS = 1 + 2 * PLANES
BOUNDS = (1, 3, 7, 11, 15, BLOCKS)
TILES = len(BOUNDS) - 1
MESSAGE = BLOCK + 16
LEAST = 1024
STEP = 1024

SCALE2 = HD**-0.5 * math.log2(math.e)
LOG_BASE = math.log(1000000.0)
NT = (((1,), (1,)), ((), ()))


def cos_sin(angle):
    turn = jnp.floor(angle * (2.0 / math.pi) + 0.5)
    rest = angle - turn * 1.5703125
    rest = rest - turn * 4.837512969970703125e-4
    rest = rest - turn * 7.54978995489188e-8
    z = rest * rest
    sine = rest + rest * z * ((-1.9515295891e-4 * z + 8.3321608736e-3) * z - 1.6666654611e-1)
    cosine = 1.0 - 0.5 * z + z * z * (
        (2.443315711809948e-5 * z - 1.388731625493765e-3) * z + 4.166664568298827e-2
    )
    quarter = turn.astype(jnp.int32) & 3
    odd = (quarter & 1) == 1
    c = jnp.where(odd, sine, cosine)
    s = jnp.where(odd, cosine, sine)
    c = jnp.where((quarter == 1) | (quarter == 2), -c, c)
    s = jnp.where(quarter >= 2, -s, s)
    return c, s


def kernel(
    pos_ref, len_ref, q_ref, nk_ref, nv_ref, ck_ref, cv_ref, w_ref, out_ref,
    kall, vaug, wv, qbuf, nsend, nrecv, s0, s1, t0, t1, mx0, mx1, acc,
    flat, psend, precv, lens,
    loc_sem, pair_send, pair_recv, q_send, q_recv, n_send, n_recv,
    p_send, p_recv,
):
    me = lax.axis_index("work")
    t = lax.axis_index("tp")
    z = me // 4
    yh = (me // 2) % 2
    c = me % 2

    def device(d, rel, core):
        hi = (yh + rel) % 2
        return {"work": 4 * ((z + d + PLANES) % PLANES) + 2 * hi + core, "tp": t}

    def remote(src, dst, send, recv, to):
        return pltpu.make_async_remote_copy(
            src, dst, send, recv, device_id=to, device_id_type=MESH
        )

    sibling = device(0, 0, 1 - c)
    partner = device(0, 1, c)

    copy_k = pltpu.make_async_copy(ck_ref, kall.at[pl.ds(0, CACHE)], loc_sem.at[0])
    copy_v = pltpu.make_async_copy(
        cv_ref, vaug.at[pl.ds(0, CACHE), pl.ds(0, HD)], loc_sem.at[1]
    )
    copy_k.start()
    copy_v.start()

    barrier = pltpu.get_barrier_semaphore()

    def signal(to):
        pl.semaphore_signal(barrier, inc=1, device_id=to, device_id_type=MESH)

    def greet(i, _):
        signal(device(i // 2, i % 2, c))
        return 0

    lax.fori_loop(1, BLOCKS - 1, greet, 0)
    signal(sibling)

    def greet_tp(i, _):
        signal({"work": me, "tp": (t + i) % TP})
        return 0

    lax.fori_loop(1, TP, greet_tp, 0)

    lane = lax.broadcasted_iota(jnp.int32, (ROWS, HD), 1)
    place = pos_ref[0] + lax.broadcasted_iota(jnp.int32, (ROWS, HD), 0)
    ladder = (lane % (HD // 2)).astype(F32) * (2.0 / HD)
    angle = place.astype(F32) * jnp.exp(ladder * -LOG_BASE)
    cosine, sine = cos_sin(angle)
    sine = jnp.where(lane < HD // 2, -sine, sine)

    def rotated(x):
        x = x.astype(F32)
        return (x * cosine + pltpu.roll(x, HD // 2, 1) * sine).astype(BF16)

    for g in range(HEADS):
        qbuf[1, g * ROWS : (g + 1) * ROWS, :] = rotated(q_ref[g * ROWS : (g + 1) * ROWS, :])
    kall[PAIR : PAIR + ROWS, :] = rotated(nk_ref[...])
    lens[0] = jnp.full((8, HD), len_ref[0], jnp.int32).astype(F32)

    pl.semaphore_wait(barrier, 2 * PLANES - 1 + 1 + TP - 1)

    def query_copy(k, to):
        return remote(qbuf.at[1], qbuf.at[k], q_send.at[k], q_recv.at[k], to)

    pair = [
        remote(src, dst, pair_send.at[k], pair_recv.at[k], sibling)
        for k, (src, dst) in enumerate(
            (
                (lens.at[0], lens.at[1]),
                (kall.at[pl.ds(PAIR, ROWS)], kall.at[pl.ds(PAIR + ROWS, ROWS)]),
                (nv_ref, vaug.at[pl.ds(PAIR + ROWS, ROWS), pl.ds(0, HD)]),
                (ck_ref, kall.at[pl.ds(CACHE, CACHE)]),
                (cv_ref, vaug.at[pl.ds(CACHE, CACHE), pl.ds(0, HD)]),
            )
        )
    ]
    def send_queries(first, last):
        for k in range(first, last):
            query_copy(k, device(-ORDER[(k - 1) // 2], (k - 1) % 2, c)).start()

    send_queries(2, BOUNDS[1])
    for copy in pair[:4]:
        copy.start()
    send_queries(BOUNDS[1], BOUNDS[2])
    pair[4].start()
    send_queries(BOUNDS[2], BLOCKS)

    def weight_copy(k):
        return pltpu.make_async_copy(
            w_ref.at[:, pl.ds(pl.multiple_of(k * COLS, HD), COLS)], wv.at[k], loc_sem.at[2 + k]
        )

    def start_weights(k, _):
        weight_copy(k).start()
        return 0

    lax.fori_loop(0, TP, start_weights, 0)

    kall[PAIR + 2 * ROWS :, :] = jnp.zeros((NEWPAD - 2 * ROWS, HD), BF16)
    vaug[PAIR : PAIR + ROWS, 0:HD] = nv_ref[...]
    vaug[PAIR + 2 * ROWS :, 0:HD] = jnp.zeros((NEWPAD - 2 * ROWS, HD), BF16)
    vaug[PAIR:, HD:] = jnp.ones((NEWPAD, HD), BF16)

    def live_rows(base, j):
        rows = lax.broadcasted_iota(jnp.int32, (STEP, HD), 0) + j * STEP
        return jnp.where(rows.astype(F32) < lens[base // CACHE, 0:1, :], 1.0, 0.0).astype(BF16)

    def mask_keys(base):
        first = kall[base : base + 16, :].astype(F32)[0:1, :]
        first = jnp.broadcast_to(first, (STEP, HD)).astype(BF16)

        def body(j, _):
            live = live_rows(base, j)
            rows = pl.ds(base + pl.multiple_of(j * STEP, STEP), STEP)
            kall[rows, :] = kall[rows, :] * live + first * (1.0 - live)
            return 0

        lax.fori_loop(LEAST // STEP, CACHE // STEP, body, 0)

    def mask_values(base):
        def ones(j, _):
            rows = pl.ds(base + pl.multiple_of(j * STEP, STEP), STEP)
            vaug[rows, HD:] = jnp.ones((STEP, HD), BF16)
            return 0

        lax.fori_loop(0, LEAST // STEP, ones, 0)

        def body(j, _):
            live = live_rows(base, j)
            rows = pl.ds(base + pl.multiple_of(j * STEP, STEP), STEP)
            vaug[rows, 0:HD] = vaug[rows, 0:HD] * live
            vaug[rows, HD:] = live
            return 0

        lax.fori_loop(LEAST // STEP, CACHE // STEP, body, 0)

    def tile_blocks(i):
        return BOUNDS[i], BOUNDS[i + 1]

    def wait_queries(first, last):
        for k in range(first, last):
            if k != 1:
                query_copy(k, partner).wait_recv()

    def queries_of(first, last):
        return qbuf[first:last].reshape((last - first) * BLOCK, HD)

    def chunk(j):
        return pl.ds(pl.multiple_of(j * CHUNK, CHUNK), CHUNK)

    def scores(q, j, s_ref, mx):
        rows = q.shape[0]
        s = lax.dot_general(q, kall[chunk(j), :], NT, preferred_element_type=F32)
        s_ref[j, 0:rows, :] = s
        top = mx[0:rows, :]
        for u in range(CHUNK // HD):
            top = jnp.maximum(top, s[:, u * HD : (u + 1) * HD])
        mx[0:rows, :] = top

    def new_scores(first, q, t_ref, mx):
        rows = q.shape[0]
        row = lax.broadcasted_iota(jnp.int32, (rows, HD), 0)
        col = lax.broadcasted_iota(jnp.int32, (rows, HD), 1)
        r, r2 = row & 15, col & 15
        seen = (r2 >> 2) < (r >> 2)
        if first == 1:
            own = (row < BLOCK) & (col < ROWS)
            seen = seen | (own & ((r2 >> 2) == (r >> 2)) & (r2 <= r))
        s = lax.dot_general(q, kall[PAIR:, :], NT, preferred_element_type=F32)
        s = jnp.where(seen & (col < 2 * ROWS), s, -1e30)
        t_ref[0:rows, :] = s
        mx[0:rows, :] = s

    def close_max(rows, mx):
        mx[0:rows, :] = jnp.broadcast_to(
            jnp.max(mx[0:rows, :], axis=1, keepdims=True), (rows, HD)
        )

    def weights(s, top):
        return jnp.exp2((s - top) * SCALE2).astype(BF16)

    def chunk_weights(rows, j, s_ref, mx):
        top = mx[0:rows, :]
        return jnp.concatenate(
            [
                weights(s_ref[j, 0:rows, u * HD : (u + 1) * HD], top)
                for u in range(CHUNK // HD)
            ],
            axis=1,
        )

    def add_values(rows, j, p):
        acc[0:rows, :] += jnp.dot(p, vaug[chunk(j), :], preferred_element_type=F32)

    def new_values(rows, t_ref, mx):
        p = weights(t_ref[0:rows, :], mx[0:rows, :])
        acc[0:rows, :] = jnp.dot(p, vaug[PAIR:, :], preferred_element_type=F32)

    def as_rows(level):
        padded = jnp.concatenate([level, jnp.zeros((HD - BLOCK, HD), F32)], axis=0)
        row = jnp.transpose(padded)[0:8, :]
        high = row.astype(BF16).astype(F32)
        middle = (row - high).astype(BF16).astype(F32)
        low = row - high - middle
        place = lax.broadcasted_iota(jnp.int32, (8, HD), 0)
        terms = jnp.where(
            place == 0, high, jnp.where(place == 1, middle, jnp.where(place == 2, low, 0.0))
        )
        return jnp.concatenate([terms, jnp.zeros((8, HD), F32)], axis=0).astype(BF16)

    def result_copy(k, to):
        return remote(nsend.at[k], nrecv.at[k], n_send.at[k], n_recv.at[k], to)

    def finish(first, last, mx):
        rows = (last - first) * BLOCK
        total = acc[0:rows, HD:]
        n = (acc[0:rows, :HD] / total).astype(BF16)
        level = mx[0:rows, :] * SCALE2 + jnp.log(total) * math.log2(math.e)
        for k in range(first, last):
            part = slice((k - first) * BLOCK, (k - first + 1) * BLOCK)
            nsend[k, 0:BLOCK, :] = n[part]
            nsend[k, BLOCK:, :] = as_rows(level[part])
            if k == 1:
                nrecv[1] = nsend[1]
            else:
                result_copy(k, device(ORDER[(k - 1) // 2], (k - 1) % 2, c)).start()

    copy_k.wait()
    mask_keys(0)
    for copy in pair[:3]:
        copy.wait_recv()
    wait_queries(*tile_blocks(0))
    q = queries_of(*tile_blocks(0))
    new_scores(1, q, t0, mx0)

    def first_scores(j, _):
        @pl.when(j == CHUNKS // 2)
        def _():
            pair[3].wait_recv()
            mask_keys(CACHE)

        scores(q, j, s0, mx0)
        return 0

    lax.fori_loop(0, CHUNKS, first_scores, 0)
    close_max(q.shape[0], mx0)
    copy_v.wait()
    mask_values(0)

    def step(i, first, last):
        s_now, t_now, mx_now = ((s0, t0, mx0), (s1, t1, mx1))[i % 2]
        s_later, t_later, mx_later = ((s1, t1, mx1), (s0, t0, mx0))[i % 2]
        rows = (last - first) * BLOCK
        if i + 1 < TILES:
            wait_queries(*tile_blocks(i + 1))
            q = queries_of(*tile_blocks(i + 1))
            new_scores(tile_blocks(i + 1)[0], q, t_later, mx_later)
        new_values(rows, t_now, mx_now)

        def body(j, _):
            if i == 0:
                @pl.when(j == CHUNKS // 2)
                def _():
                    pair[4].wait_recv()
                    mask_values(CACHE)

            p = chunk_weights(rows, j, s_now, mx_now)
            if i + 1 < TILES:
                scores(q, j, s_later, mx_later)
            add_values(rows, j, p)
            return 0

        lax.fori_loop(0, CHUNKS, body, 0)
        if i + 1 < TILES:
            close_max(q.shape[0], mx_later)
        finish(first, last, mx_now)

    for i in range(TILES):
        step(i, *tile_blocks(i))

    def wait_result(k, _):
        result_copy(k, partner).wait_recv()
        return 0

    def level_of(v):
        terms = nrecv[v, BLOCK:, :].astype(F32)
        return jnp.broadcast_to(jnp.sum(terms, axis=0, keepdims=True), (8, HD))

    def as_columns(rows):
        place = lax.broadcasted_iota(jnp.int32, (8, HD), 0)
        packed = []
        for first in range(0, len(rows), 8):
            block = jnp.zeros((8, HD), F32)
            for v in range(first, min(first + 8, len(rows))):
                block = jnp.where(place == v - first, rows[v], block)
            packed.append(block)
        packed.append(jnp.zeros((HD - 8 * len(packed), HD), F32))
        return jnp.transpose(jnp.concatenate(packed, axis=0))[0:BLOCK, :]

    def largest(levels):
        top = levels[0]
        for level in levels[1:]:
            top = jnp.maximum(top, level)
        return top

    early = BOUNDS[-2]
    lax.fori_loop(2, early, wait_result, 0)
    levels = [level_of(v) for v in range(1, early)]
    early_top = largest(levels)
    shares = [jnp.exp2(level - early_top) for level in levels]
    early_sum = sum(shares[1:], shares[0])
    share = as_columns(shares)
    early_total = jnp.zeros((BLOCK, HD), F32)
    for v in range(1, early):
        early_total = early_total + nrecv[v, 0:BLOCK, :].astype(F32) * share[:, v - 1 : v]

    lax.fori_loop(early, BLOCKS, wait_result, 0)
    levels = [early_top] + [level_of(v) for v in range(early, BLOCKS)]
    summit = largest(levels)
    shares = [jnp.exp2(level - summit) for level in levels]
    denom = sum(shares[1:], shares[0] * early_sum)
    share = as_columns([part / denom for part in shares])
    attention = early_total * share[:, 0:1]
    for k in range(BLOCKS - early):
        part = nrecv[early + k, 0:BLOCK, :].astype(F32)
        attention = attention + part * share[:, k + 1 : k + 2]
    attention = attention.astype(BF16)
    for g in range(HEADS):
        flat[:, g * HD : (g + 1) * HD] = attention[g * ROWS : (g + 1) * ROWS, :]

    def wait_weights(k, _):
        weight_copy(k).wait()
        return 0

    lax.fori_loop(0, TP, wait_weights, 0)

    def columns(i):
        return remote(
            psend.at[i], precv.at[i], p_send.at[i], p_recv.at[i],
            {"work": me, "tp": (t + i) % TP},
        )

    joined = flat[...]
    for i in (4, 5, 3, 2, 6, 7, 1):
        psend[i] = jnp.dot(joined, wv[(t + i) % TP], preferred_element_type=F32).astype(BF16)
        columns(i).start()
    total = jnp.dot(joined, wv[t], preferred_element_type=F32)

    def gather(i, total):
        columns(i).wait_recv()
        return total + precv[i].astype(F32)

    out_ref[...] = lax.fori_loop(1, TP, gather, total).astype(BF16)

    for copy in pair:
        copy.wait_send()

    def sent(k, _):
        query_copy(k, partner).wait_send()
        result_copy(k, partner).wait_send()
        return 0

    lax.fori_loop(2, BLOCKS, sent, 0)

    def sent_columns(i, _):
        columns(i).wait_send()
        return 0

    lax.fori_loop(1, TP, sent_columns, 0)


def per_device(
    queries, new_keys, new_values, cache_keys, cache_values, lengths, positions, out_weight
):
    vmem = pl.BlockSpec(memory_space=pltpu.VMEM)
    smem = pl.BlockSpec(memory_space=pltpu.SMEM)
    anywhere = pl.BlockSpec(memory_space=pl.ANY)
    dma = pltpu.SemaphoreType.DMA
    out = pl.pallas_call(
        kernel,
        out_shape=jax.ShapeDtypeStruct((ROWS, COLS), BF16),
        in_specs=[smem, smem, vmem, vmem, vmem, anywhere, anywhere, anywhere],
        out_specs=vmem,
        scratch_shapes=[
            pltpu.VMEM((PAIR + NEWPAD, HD), BF16),
            pltpu.VMEM((PAIR + NEWPAD, 2 * HD), BF16),
            pltpu.VMEM((TP, COLS, COLS), BF16),
            pltpu.VMEM((BLOCKS, BLOCK, HD), BF16),
            pltpu.VMEM((BLOCKS, MESSAGE, HD), BF16),
            pltpu.VMEM((BLOCKS, MESSAGE, HD), BF16),
            pltpu.VMEM((CHUNKS, TILE, CHUNK), F32),
            pltpu.VMEM((CHUNKS, TILE, CHUNK), F32),
            pltpu.VMEM((TILE, HD), F32),
            pltpu.VMEM((TILE, HD), F32),
            pltpu.VMEM((TILE, HD), F32),
            pltpu.VMEM((TILE, HD), F32),
            pltpu.VMEM((TILE, 2 * HD), F32),
            pltpu.VMEM((ROWS, HEADS * HD), BF16),
            pltpu.VMEM((TP, ROWS, COLS), BF16),
            pltpu.VMEM((TP, ROWS, COLS), BF16),
            pltpu.VMEM((2, 8, HD), F32),
            dma((2 + TP,)),
            dma((5,)),
            dma((5,)),
            dma((BLOCKS,)),
            dma((BLOCKS,)),
            dma((BLOCKS,)),
            dma((BLOCKS,)),
            dma((TP,)),
            dma((TP,)),
        ],
        compiler_params=pltpu.CompilerParams(
            collective_id=0, has_side_effects=True, vmem_limit_bytes=58 * 1024 * 1024
        ),
    )(
        positions.reshape(ROWS),
        lengths,
        queries[0].transpose(1, 0, 2).reshape(BLOCK, HD),
        new_keys.reshape(ROWS, HD),
        new_values.reshape(ROWS, HD),
        cache_keys.reshape(CACHE, HD),
        cache_values.reshape(CACHE, HD),
        out_weight,
    )
    return out[None]


def solution(mesh):
    in_specs = (
        P("work", None, "tp", None),
        P("work", None, "tp", None),
        P("work", None, "tp", None),
        P("work", None, "tp", None),
        P("work", None, "tp", None),
        P("work"),
        P("work", None),
        P("tp", None),
    )
    out_specs = P("work", None, "tp")
    return jax.shard_map(
        per_device, mesh=mesh, in_specs=in_specs, out_specs=out_specs, check_vma=False
    )
```

```python
import math

import jax
import jax.numpy as jnp
from jax import lax
from jax.experimental import pallas as pl
from jax.experimental.pallas import tpu as pltpu
from jax.sharding import PartitionSpec as P

MESH = pl.DeviceIdType.MESH
F32 = jnp.float32
BF16 = jnp.bfloat16

HEADS = 5
ROWS = 16
HD = 128
CACHE = 4096
PAIR = 2 * CACHE
NEWPAD = 128
BLOCK = HEADS * ROWS
GROUP = 2
PARTS = 2 * GROUP
TILE = PARTS * BLOCK
CHUNK = 2048
CHUNKS = PAIR // CHUNK
TP = 8
COLS = 640
PLANES = 8
TILES = PLANES // GROUP
ORDER = (0, 7, 3, 5, 4, 2, 6, 1)
CODE = sum(d * PLANES**i for i, d in enumerate(ORDER))
SLOTS = 2 * PLANES
MESSAGE = BLOCK + 16
LEAST = 1024
STEP = 1024

SCALE2 = HD**-0.5 * math.log2(math.e)
LOG_BASE = math.log(1000000.0)
NT = (((1,), (1,)), ((), ()))


def cos_sin(angle):
    turn = jnp.floor(angle * (2.0 / math.pi) + 0.5)
    rest = angle - turn * 1.5703125
    rest = rest - turn * 4.837512969970703125e-4
    rest = rest - turn * 7.54978995489188e-8
    z = rest * rest
    sine = rest + rest * z * ((-1.9515295891e-4 * z + 8.3321608736e-3) * z - 1.6666654611e-1)
    cosine = 1.0 - 0.5 * z + z * z * (
        (2.443315711809948e-5 * z - 1.388731625493765e-3) * z + 4.166664568298827e-2
    )
    quarter = turn.astype(jnp.int32) & 3
    odd = (quarter & 1) == 1
    c = jnp.where(odd, sine, cosine)
    s = jnp.where(odd, cosine, sine)
    c = jnp.where((quarter == 1) | (quarter == 2), -c, c)
    s = jnp.where(quarter >= 2, -s, s)
    return c, s


def kernel(
    pos_ref, len_ref, q_ref, nk_ref, nv_ref, ck_ref, cv_ref, w_ref, out_ref,
    kall, vaug, wv, qbuf, nsend, nrecv, s0, s1, t0, t1, mx0, mx1, acc,
    flat, psend, precv, lens,
    loc_sem, pair_send, pair_recv, q_send, q_recv, n_send, n_recv,
    p_send, p_recv,
):
    me = lax.axis_index("work")
    t = lax.axis_index("tp")
    z = me // 4
    yh = (me // 2) % 2
    c = me % 2

    def device(d, rel, core):
        hi = (yh + rel) % 2
        return {"work": 4 * ((z + d + PLANES) % PLANES) + 2 * hi + core, "tp": t}

    def remote(src, dst, send, recv, to):
        return pltpu.make_async_remote_copy(
            src, dst, send, recv, device_id=to, device_id_type=MESH
        )

    sibling = device(0, 0, 1 - c)
    partner = device(0, 1, c)

    copy_k = pltpu.make_async_copy(ck_ref, kall.at[pl.ds(0, CACHE)], loc_sem.at[0])
    copy_v = pltpu.make_async_copy(
        cv_ref, vaug.at[pl.ds(0, CACHE), pl.ds(0, HD)], loc_sem.at[1]
    )
    copy_k.start()
    copy_v.start()

    barrier = pltpu.get_barrier_semaphore()

    def signal(to):
        pl.semaphore_signal(barrier, inc=1, device_id=to, device_id_type=MESH)

    def greet(i, _):
        signal(device(i // 2, i % 2, c))
        return 0

    lax.fori_loop(1, SLOTS, greet, 0)
    signal(sibling)

    def greet_tp(i, _):
        signal({"work": me, "tp": (t + i) % TP})
        return 0

    lax.fori_loop(1, TP, greet_tp, 0)

    lane = lax.broadcasted_iota(jnp.int32, (ROWS, HD), 1)
    place = pos_ref[0] + lax.broadcasted_iota(jnp.int32, (ROWS, HD), 0)
    ladder = (lane % (HD // 2)).astype(F32) * (2.0 / HD)
    angle = place.astype(F32) * jnp.exp(ladder * -LOG_BASE)
    cosine, sine = cos_sin(angle)
    sine = jnp.where(lane < HD // 2, -sine, sine)

    def rotated(x):
        x = x.astype(F32)
        return (x * cosine + pltpu.roll(x, HD // 2, 1) * sine).astype(BF16)

    for g in range(HEADS):
        qbuf[0, g * ROWS : (g + 1) * ROWS, :] = rotated(q_ref[g * ROWS : (g + 1) * ROWS, :])
    kall[PAIR : PAIR + ROWS, :] = rotated(nk_ref[...])
    lens[0] = jnp.full((8, HD), len_ref[0], jnp.int32).astype(F32)

    def live_rows(owner, j):
        rows = lax.broadcasted_iota(jnp.int32, (STEP, HD), 0) + j * STEP
        return jnp.where(rows.astype(F32) < lens[owner, 0:1, :], 1.0, 0.0).astype(BF16)

    def mark_live(owner):
        def body(j, _):
            rows = pl.ds(owner * CACHE + pl.multiple_of(j * STEP, STEP), STEP)
            vaug[rows, HD:] = live_rows(owner, j)
            return 0

        lax.fori_loop(0, CACHE // STEP, body, 0)

    def mask_keys(j, _):
        live = live_rows(0, j)
        rows = pl.ds(pl.multiple_of(j * STEP, STEP), STEP)
        kall[rows, :] = kall[rows, :] * live + head_key * (1.0 - live)
        return 0

    def mask_values(j, _):
        rows = pl.ds(pl.multiple_of(j * STEP, STEP), STEP)
        vaug[rows, 0:HD] = vaug[rows, 0:HD] * live_rows(0, j)
        return 0

    copy_k.wait()
    head_key = kall[0:16, :].astype(F32)[0:1, :]
    head_key = jnp.broadcast_to(head_key, (STEP, HD)).astype(BF16)
    lax.fori_loop(LEAST // STEP, CACHE // STEP, mask_keys, 0)
    copy_v.wait()
    lax.fori_loop(LEAST // STEP, CACHE // STEP, mask_values, 0)
    mark_live(0)

    pl.semaphore_wait(barrier, SLOTS - 1 + 1 + TP - 1)

    def query_copy(k, d, rel):
        return remote(qbuf.at[0], qbuf.at[k], q_send.at[k], q_recv.at[k], device(-d, rel, c))

    pair = [
        remote(src, dst, pair_send.at[k], pair_recv.at[k], sibling)
        for k, (src, dst) in enumerate(
            (
                (lens.at[0], lens.at[1]),
                (kall.at[pl.ds(PAIR, ROWS)], kall.at[pl.ds(PAIR + ROWS, ROWS)]),
                (nv_ref, vaug.at[pl.ds(PAIR + ROWS, ROWS), pl.ds(0, HD)]),
                (kall.at[pl.ds(0, CACHE)], kall.at[pl.ds(CACHE, CACHE)]),
                (
                    vaug.at[pl.ds(0, CACHE), pl.ds(0, HD)],
                    vaug.at[pl.ds(CACHE, CACHE), pl.ds(0, HD)],
                ),
            )
        )
    ]
    query_copy(1, 0, 1).start()
    for copy in pair[:4]:
        copy.start()

    def send_queries(i, code):
        for rel in range(2):
            query_copy(2 * i + rel, code % PLANES, rel).start()
        return code // PLANES

    lax.fori_loop(1, PLANES, send_queries, CODE // PLANES)
    pair[4].start()

    def weight_copy(k):
        return pltpu.make_async_copy(
            w_ref.at[:, pl.ds(pl.multiple_of(k * COLS, HD), COLS)], wv.at[k], loc_sem.at[2 + k]
        )

    def start_weights(k, _):
        weight_copy(k).start()
        return 0

    lax.fori_loop(0, TP, start_weights, 0)

    kall[PAIR + 2 * ROWS :, :] = jnp.zeros((NEWPAD - 2 * ROWS, HD), BF16)
    vaug[PAIR : PAIR + ROWS, 0:HD] = nv_ref[...]
    vaug[PAIR + 2 * ROWS :, 0:HD] = jnp.zeros((NEWPAD - 2 * ROWS, HD), BF16)
    vaug[PAIR:, HD:] = jnp.ones((NEWPAD, HD), BF16)

    def wait_queries(i):
        for part in range(PARTS):
            query_copy(PARTS * i + part, 0, 1).wait_recv()

    def queries_of(i):
        return qbuf[pl.ds(PARTS * i, PARTS)].reshape(TILE, HD)

    def chunk(j):
        return pl.ds(pl.multiple_of(j * CHUNK, CHUNK), CHUNK)

    def scores(q, j, s_ref, mx):
        s = lax.dot_general(q, kall[chunk(j), :], NT, preferred_element_type=F32)
        s_ref[j] = s
        top = mx[...]
        for u in range(CHUNK // HD):
            top = jnp.maximum(top, s[:, u * HD : (u + 1) * HD])
        mx[...] = top

    def new_scores(first, q, t_ref, mx):
        row = lax.broadcasted_iota(jnp.int32, (TILE, HD), 0)
        col = lax.broadcasted_iota(jnp.int32, (TILE, HD), 1)
        r, r2 = row & 15, col & 15
        seen = (r2 >> 2) < (r >> 2)
        if first:
            own = (row < BLOCK) & (col < ROWS)
            seen = seen | (own & ((r2 >> 2) == (r >> 2)) & (r2 <= r))
        s = lax.dot_general(q, kall[PAIR:, :], NT, preferred_element_type=F32)
        s = jnp.where(seen & (col < 2 * ROWS), s, -1e30)
        t_ref[...] = s
        mx[...] = s

    def close_max(mx):
        mx[...] = jnp.broadcast_to(jnp.max(mx[...], axis=1, keepdims=True), (TILE, HD))

    def weights(s, top):
        return jnp.exp2((s - top) * SCALE2).astype(BF16)

    def chunk_weights(j, s_ref, mx):
        top = mx[...]
        return jnp.concatenate(
            [weights(s_ref[j, :, u * HD : (u + 1) * HD], top) for u in range(CHUNK // HD)], axis=1
        )

    def add_values(j, p):
        acc[...] += jnp.dot(p, vaug[chunk(j), :], preferred_element_type=F32)

    def new_values(t_ref, mx):
        p = weights(t_ref[...], mx[...])
        acc[...] = jnp.dot(p, vaug[PAIR:, :], preferred_element_type=F32)

    def as_rows(level):
        padded = jnp.concatenate([level, jnp.zeros((HD - BLOCK, HD), F32)], axis=0)
        row = jnp.transpose(padded)[0:8, :]
        high = row.astype(BF16).astype(F32)
        middle = (row - high).astype(BF16).astype(F32)
        low = row - high - middle
        place = lax.broadcasted_iota(jnp.int32, (8, HD), 0)
        terms = jnp.where(
            place == 0, high, jnp.where(place == 1, middle, jnp.where(place == 2, low, 0.0))
        )
        return jnp.concatenate([terms, jnp.zeros((8, HD), F32)], axis=0).astype(BF16)

    def result_copy(k, d, rel):
        return remote(nsend.at[k], nrecv.at[k], n_send.at[k], n_recv.at[k], device(d, rel, c))

    def finish(i, code, mx, maybe_first):
        total = acc[:, HD:]
        n = (acc[:, :HD] / total).astype(BF16)
        level = mx[...] * SCALE2 + jnp.log(total) * math.log2(math.e)
        for part in range(PARTS):
            rows = slice(part * BLOCK, (part + 1) * BLOCK)
            k = PARTS * i + part
            nsend[k, 0:BLOCK, :] = n[rows]
            nsend[k, BLOCK:, :] = as_rows(level[rows])
            copy = result_copy(k, (code // PLANES ** (part // 2)) % PLANES, part % 2)
            if maybe_first and part == 0:
                @pl.when(i > 0)
                def _():
                    copy.start()

                @pl.when(i == 0)
                def _():
                    nrecv[0] = nsend[0]
            else:
                copy.start()
        return code // PLANES**GROUP

    for copy in pair[:3]:
        copy.wait_recv()
    for part in range(1, PARTS):
        query_copy(part, 0, 1).wait_recv()
    q = queries_of(0)
    new_scores(True, q, t0, mx0)

    def first_scores(j, _):
        @pl.when(j == CHUNKS // 2)
        def _():
            mark_live(1)
            pair[3].wait_recv()

        scores(q, j, s0, mx0)
        return 0

    lax.fori_loop(0, CHUNKS, first_scores, 0)
    close_max(mx0)
    def both(i, s_now, t_now, mx_now, s_later, t_later, mx_later, maybe_first):
        wait_queries(i + 1)
        q = queries_of(i + 1)
        new_scores(False, q, t_later, mx_later)
        new_values(t_now, mx_now)

        def body(j, _):
            if maybe_first:
                @pl.when((i == 0) & (j == CHUNKS // 2))
                def _():
                    pair[4].wait_recv()

            p = chunk_weights(j, s_now, mx_now)
            scores(q, j, s_later, mx_later)
            add_values(j, p)
            return 0

        lax.fori_loop(0, CHUNKS, body, 0)
        close_max(mx_later)

    def two_tiles(k, code):
        i = 2 * k
        both(i, s0, t0, mx0, s1, t1, mx1, True)
        code = finish(i, code, mx0, True)

        @pl.when(i + 2 < TILES)
        def _():
            both(i + 1, s1, t1, mx1, s0, t0, mx0, False)

        @pl.when(i + 2 == TILES)
        def _():
            new_values(t1, mx1)

            def body(j, _):
                add_values(j, chunk_weights(j, s1, mx1))
                return 0

            lax.fori_loop(0, CHUNKS, body, 0)

        return finish(i + 1, code, mx1, False)

    lax.fori_loop(0, TILES // 2, two_tiles, CODE)

    def wait_result(k, _):
        result_copy(k, 0, 1).wait_recv()
        return 0

    def level_of(v):
        terms = nrecv[v, BLOCK:, :].astype(F32)
        return jnp.broadcast_to(jnp.sum(terms, axis=0, keepdims=True), (8, HD))

    def as_columns(rows):
        place = lax.broadcasted_iota(jnp.int32, (8, HD), 0)
        packed = []
        for first in range(0, len(rows), 8):
            block = jnp.zeros((8, HD), F32)
            for v in range(first, min(first + 8, len(rows))):
                block = jnp.where(place == v - first, rows[v], block)
            packed.append(block)
        packed.append(jnp.zeros((HD - 8 * len(packed), HD), F32))
        return jnp.transpose(jnp.concatenate(packed, axis=0))[0:BLOCK, :]

    def largest(levels):
        top = levels[0]
        for level in levels[1:]:
            top = jnp.maximum(top, level)
        return top

    early = SLOTS - PARTS
    lax.fori_loop(1, early, wait_result, 0)
    levels = [level_of(v) for v in range(early)]
    early_top = largest(levels)
    shares = [jnp.exp2(level - early_top) for level in levels]
    early_sum = sum(shares[1:], shares[0])
    share = as_columns(shares)
    early_total = jnp.zeros((BLOCK, HD), F32)
    for v in range(early):
        early_total = early_total + nrecv[v, 0:BLOCK, :].astype(F32) * share[:, v : v + 1]

    lax.fori_loop(early, SLOTS, wait_result, 0)
    levels = [early_top] + [level_of(v) for v in range(early, SLOTS)]
    summit = largest(levels)
    shares = [jnp.exp2(level - summit) for level in levels]
    denom = sum(shares[1:], shares[0] * early_sum)
    share = as_columns([part / denom for part in shares])
    attention = early_total * share[:, 0:1]
    for k in range(PARTS):
        part = nrecv[early + k, 0:BLOCK, :].astype(F32)
        attention = attention + part * share[:, k + 1 : k + 2]
    attention = attention.astype(BF16)
    for g in range(HEADS):
        flat[:, g * HD : (g + 1) * HD] = attention[g * ROWS : (g + 1) * ROWS, :]

    def wait_weights(k, _):
        weight_copy(k).wait()
        return 0

    lax.fori_loop(0, TP, wait_weights, 0)

    def columns(i):
        return remote(
            psend.at[i], precv.at[i], p_send.at[i], p_recv.at[i],
            {"work": me, "tp": (t + i) % TP},
        )

    joined = flat[...]
    for i in (4, 5, 3, 2, 6, 7, 1):
        psend[i] = jnp.dot(joined, wv[(t + i) % TP], preferred_element_type=F32).astype(BF16)
        columns(i).start()
    total = jnp.dot(joined, wv[t], preferred_element_type=F32)

    def gather(i, total):
        columns(i).wait_recv()
        return total + precv[i].astype(F32)

    out_ref[...] = lax.fori_loop(1, TP, gather, total).astype(BF16)

    for copy in pair:
        copy.wait_send()

    def sent(k, _):
        query_copy(k, 0, 1).wait_send()
        result_copy(k, 0, 1).wait_send()
        return 0

    lax.fori_loop(1, SLOTS, sent, 0)

    def sent_columns(i, _):
        columns(i).wait_send()
        return 0

    lax.fori_loop(1, TP, sent_columns, 0)


def per_device(
    queries, new_keys, new_values, cache_keys, cache_values, lengths, positions, out_weight
):
    vmem = pl.BlockSpec(memory_space=pltpu.VMEM)
    smem = pl.BlockSpec(memory_space=pltpu.SMEM)
    anywhere = pl.BlockSpec(memory_space=pl.ANY)
    dma = pltpu.SemaphoreType.DMA
    out = pl.pallas_call(
        kernel,
        out_shape=jax.ShapeDtypeStruct((ROWS, COLS), BF16),
        in_specs=[smem, smem, vmem, vmem, vmem, anywhere, anywhere, anywhere],
        out_specs=vmem,
        scratch_shapes=[
            pltpu.VMEM((PAIR + NEWPAD, HD), BF16),
            pltpu.VMEM((PAIR + NEWPAD, 2 * HD), BF16),
            pltpu.VMEM((TP, COLS, COLS), BF16),
            pltpu.VMEM((SLOTS, BLOCK, HD), BF16),
            pltpu.VMEM((SLOTS, MESSAGE, HD), BF16),
            pltpu.VMEM((SLOTS, MESSAGE, HD), BF16),
            pltpu.VMEM((CHUNKS, TILE, CHUNK), F32),
            pltpu.VMEM((CHUNKS, TILE, CHUNK), F32),
            pltpu.VMEM((TILE, HD), F32),
            pltpu.VMEM((TILE, HD), F32),
            pltpu.VMEM((TILE, HD), F32),
            pltpu.VMEM((TILE, HD), F32),
            pltpu.VMEM((TILE, 2 * HD), F32),
            pltpu.VMEM((ROWS, HEADS * HD), BF16),
            pltpu.VMEM((TP, ROWS, COLS), BF16),
            pltpu.VMEM((TP, ROWS, COLS), BF16),
            pltpu.VMEM((2, 8, HD), F32),
            dma((2 + TP,)),
            dma((5,)),
            dma((5,)),
            dma((SLOTS,)),
            dma((SLOTS,)),
            dma((SLOTS,)),
            dma((SLOTS,)),
            dma((TP,)),
            dma((TP,)),
        ],
        compiler_params=pltpu.CompilerParams(
            collective_id=0, has_side_effects=True, vmem_limit_bytes=58 * 1024 * 1024
        ),
    )(
        positions.reshape(ROWS),
        lengths,
        queries[0].transpose(1, 0, 2).reshape(BLOCK, HD),
        new_keys.reshape(ROWS, HD),
        new_values.reshape(ROWS, HD),
        cache_keys.reshape(CACHE, HD),
        cache_values.reshape(CACHE, HD),
        out_weight,
    )
    return out[None]


def solution(mesh):
    in_specs = (
        P("work", None, "tp", None),
        P("work", None, "tp", None),
        P("work", None, "tp", None),
        P("work", None, "tp", None),
        P("work", None, "tp", None),
        P("work"),
        P("work", None),
        P("tp", None),
    )
    out_specs = P("work", None, "tp")
    return jax.shard_map(
        per_device, mesh=mesh, in_specs=in_specs, out_specs=out_specs, check_vma=False
    )
```

```python
import math

import jax
import jax.numpy as jnp
from jax import lax
from jax.experimental import pallas as pl
from jax.experimental.pallas import tpu as pltpu
from jax.sharding import PartitionSpec as P

MESH = pl.DeviceIdType.MESH
F32 = jnp.float32
BF16 = jnp.bfloat16

HEADS = 5
ROWS = 16
HD = 128
CACHE = 4096
PAIR = 2 * CACHE
NEWPAD = 128
BLOCK = HEADS * ROWS
GROUP = 2
PARTS = 2 * GROUP
TILE = PARTS * BLOCK
CHUNK = 2048
CHUNKS = PAIR // CHUNK
TP = 8
COLS = 640
PLANES = 8
TILES = PLANES // GROUP
ORDER = (0, 7, 3, 5, 4, 2, 6, 1)
CODE = sum(d * PLANES**i for i, d in enumerate(ORDER))
SLOTS = 2 * PLANES
MESSAGE = BLOCK + 16
LEAST = 1024
STEP = 1024

SCALE2 = HD**-0.5 * math.log2(math.e)
LOG_BASE = math.log(1000000.0)
NT = (((1,), (1,)), ((), ()))


def cos_sin(angle):
    turn = jnp.floor(angle * (2.0 / math.pi) + 0.5)
    rest = angle - turn * 1.5703125
    rest = rest - turn * 4.837512969970703125e-4
    rest = rest - turn * 7.54978995489188e-8
    z = rest * rest
    sine = rest + rest * z * ((-1.9515295891e-4 * z + 8.3321608736e-3) * z - 1.6666654611e-1)
    cosine = 1.0 - 0.5 * z + z * z * (
        (2.443315711809948e-5 * z - 1.388731625493765e-3) * z + 4.166664568298827e-2
    )
    quarter = turn.astype(jnp.int32) & 3
    odd = (quarter & 1) == 1
    c = jnp.where(odd, sine, cosine)
    s = jnp.where(odd, cosine, sine)
    c = jnp.where((quarter == 1) | (quarter == 2), -c, c)
    s = jnp.where(quarter >= 2, -s, s)
    return c, s


def kernel(
    pos_ref, len_ref, q_ref, nk_ref, nv_ref, ck_ref, cv_ref, w_ref, out_ref,
    kall, vaug, wv, qbuf, nsend, nrecv, s0, s1, t0, t1, mx0, mx1, acc,
    flat, psend, precv, lens,
    loc_sem, pair_send, pair_recv, q_send, q_recv, n_send, n_recv,
    p_send, p_recv,
):
    me = lax.axis_index("work")
    t = lax.axis_index("tp")
    z = me // 4
    yh = (me // 2) % 2
    c = me % 2

    def device(d, rel, core):
        hi = (yh + rel) % 2
        return {"work": 4 * ((z + d + PLANES) % PLANES) + 2 * hi + core, "tp": t}

    def remote(src, dst, send, recv, to):
        return pltpu.make_async_remote_copy(
            src, dst, send, recv, device_id=to, device_id_type=MESH
        )

    sibling = device(0, 0, 1 - c)
    partner = device(0, 1, c)

    copy_k = pltpu.make_async_copy(ck_ref, kall.at[pl.ds(0, CACHE)], loc_sem.at[0])
    copy_v = pltpu.make_async_copy(
        cv_ref, vaug.at[pl.ds(0, CACHE), pl.ds(0, HD)], loc_sem.at[1]
    )
    copy_k.start()
    copy_v.start()

    barrier = pltpu.get_barrier_semaphore()

    def signal(to):
        pl.semaphore_signal(barrier, inc=1, device_id=to, device_id_type=MESH)

    def greet(i, _):
        signal(device(i // 2, i % 2, c))
        return 0

    lax.fori_loop(1, SLOTS, greet, 0)
    signal(sibling)

    def greet_tp(i, _):
        signal({"work": me, "tp": (t + i) % TP})
        return 0

    lax.fori_loop(1, TP, greet_tp, 0)

    lane = lax.broadcasted_iota(jnp.int32, (ROWS, HD), 1)
    place = pos_ref[0] + lax.broadcasted_iota(jnp.int32, (ROWS, HD), 0)
    ladder = (lane % (HD // 2)).astype(F32) * (2.0 / HD)
    angle = place.astype(F32) * jnp.exp(ladder * -LOG_BASE)
    cosine, sine = cos_sin(angle)
    sine = jnp.where(lane < HD // 2, -sine, sine)

    def rotated(x):
        x = x.astype(F32)
        return (x * cosine + pltpu.roll(x, HD // 2, 1) * sine).astype(BF16)

    for g in range(HEADS):
        qbuf[0, g * ROWS : (g + 1) * ROWS, :] = rotated(q_ref[g * ROWS : (g + 1) * ROWS, :])
    kall[PAIR : PAIR + ROWS, :] = rotated(nk_ref[...])
    lens[0] = jnp.full((8, HD), len_ref[0], jnp.int32).astype(F32)

    def live_rows(owner, j):
        rows = lax.broadcasted_iota(jnp.int32, (STEP, HD), 0) + j * STEP
        return jnp.where(rows.astype(F32) < lens[owner, 0:1, :], 1.0, 0.0).astype(BF16)

    def mark_live(owner):
        def body(j, _):
            rows = pl.ds(owner * CACHE + pl.multiple_of(j * STEP, STEP), STEP)
            vaug[rows, HD:] = live_rows(owner, j)
            return 0

        lax.fori_loop(0, CACHE // STEP, body, 0)

    def mask_keys(j, _):
        live = live_rows(0, j)
        rows = pl.ds(pl.multiple_of(j * STEP, STEP), STEP)
        kall[rows, :] = kall[rows, :] * live + head_key * (1.0 - live)
        return 0

    def mask_values(j, _):
        rows = pl.ds(pl.multiple_of(j * STEP, STEP), STEP)
        vaug[rows, 0:HD] = vaug[rows, 0:HD] * live_rows(0, j)
        return 0

    copy_k.wait()
    head_key = kall[0:16, :].astype(F32)[0:1, :]
    head_key = jnp.broadcast_to(head_key, (STEP, HD)).astype(BF16)
    lax.fori_loop(LEAST // STEP, CACHE // STEP, mask_keys, 0)
    copy_v.wait()
    lax.fori_loop(LEAST // STEP, CACHE // STEP, mask_values, 0)
    mark_live(0)

    pl.semaphore_wait(barrier, SLOTS - 1 + 1 + TP - 1)

    def query_copy(k, d, rel):
        return remote(qbuf.at[0], qbuf.at[k], q_send.at[k], q_recv.at[k], device(-d, rel, c))

    pair = [
        remote(src, dst, pair_send.at[k], pair_recv.at[k], sibling)
        for k, (src, dst) in enumerate(
            (
                (lens.at[0], lens.at[1]),
                (kall.at[pl.ds(PAIR, ROWS)], kall.at[pl.ds(PAIR + ROWS, ROWS)]),
                (nv_ref, vaug.at[pl.ds(PAIR + ROWS, ROWS), pl.ds(0, HD)]),
                *[
                    (kall.at[pl.ds(r, CHUNK)], kall.at[pl.ds(CACHE + r, CHUNK)])
                    for r in range(0, CACHE, CHUNK)
                ],
                *[
                    (
                        vaug.at[pl.ds(r, CHUNK), pl.ds(0, HD)],
                        vaug.at[pl.ds(CACHE + r, CHUNK), pl.ds(0, HD)],
                    )
                    for r in range(0, CACHE, CHUNK)
                ],
            )
        )
    ]
    query_copy(1, 0, 1).start()
    pair_keys, pair_values = pair[3 : 3 + CHUNKS // 2], pair[3 + CHUNKS // 2 :]
    for copy in pair[:3] + pair_keys:
        copy.start()

    def send_queries(i, code):
        for rel in range(2):
            query_copy(2 * i + rel, code % PLANES, rel).start()
        return code // PLANES

    lax.fori_loop(1, PLANES, send_queries, CODE // PLANES)
    for copy in pair_values:
        copy.start()

    def weight_copy(k):
        return pltpu.make_async_copy(
            w_ref.at[:, pl.ds(pl.multiple_of(k * COLS, HD), COLS)], wv.at[k], loc_sem.at[2 + k]
        )

    def start_weights(k, _):
        weight_copy(k).start()
        return 0

    lax.fori_loop(0, TP, start_weights, 0)

    kall[PAIR + 2 * ROWS :, :] = jnp.zeros((NEWPAD - 2 * ROWS, HD), BF16)
    vaug[PAIR : PAIR + ROWS, 0:HD] = nv_ref[...]
    vaug[PAIR + 2 * ROWS :, 0:HD] = jnp.zeros((NEWPAD - 2 * ROWS, HD), BF16)
    vaug[PAIR:, HD:] = jnp.ones((NEWPAD, HD), BF16)

    def wait_queries(i):
        for part in range(PARTS):
            query_copy(PARTS * i + part, 0, 1).wait_recv()

    def queries_of(i):
        return qbuf[pl.ds(PARTS * i, PARTS)].reshape(TILE, HD)

    def chunk(j):
        return pl.ds(pl.multiple_of(j * CHUNK, CHUNK), CHUNK)

    def scores(q, j, s_ref, mx):
        s = lax.dot_general(q, kall[chunk(j), :], NT, preferred_element_type=F32)
        s_ref[j] = s
        top = mx[...]
        for u in range(CHUNK // HD):
            top = jnp.maximum(top, s[:, u * HD : (u + 1) * HD])
        mx[...] = top

    def new_scores(first, q, t_ref, mx):
        row = lax.broadcasted_iota(jnp.int32, (TILE, HD), 0)
        col = lax.broadcasted_iota(jnp.int32, (TILE, HD), 1)
        r, r2 = row & 15, col & 15
        seen = (r2 >> 2) < (r >> 2)
        if first:
            own = (row < BLOCK) & (col < ROWS)
            seen = seen | (own & ((r2 >> 2) == (r >> 2)) & (r2 <= r))
        s = lax.dot_general(q, kall[PAIR:, :], NT, preferred_element_type=F32)
        s = jnp.where(seen & (col < 2 * ROWS), s, -1e30)
        t_ref[...] = s
        mx[...] = s

    def close_max(mx):
        mx[...] = jnp.broadcast_to(jnp.max(mx[...], axis=1, keepdims=True), (TILE, HD))

    def weights(s, top):
        return jnp.exp2((s - top) * SCALE2).astype(BF16)

    def chunk_weights(j, s_ref, mx):
        top = mx[...]
        return jnp.concatenate(
            [weights(s_ref[j, :, u * HD : (u + 1) * HD], top) for u in range(CHUNK // HD)], axis=1
        )

    def add_values(j, p):
        acc[...] += jnp.dot(p, vaug[chunk(j), :], preferred_element_type=F32)

    def new_values(t_ref, mx):
        p = weights(t_ref[...], mx[...])
        acc[...] = jnp.dot(p, vaug[PAIR:, :], preferred_element_type=F32)

    def as_rows(level):
        padded = jnp.concatenate([level, jnp.zeros((HD - BLOCK, HD), F32)], axis=0)
        row = jnp.transpose(padded)[0:8, :]
        high = row.astype(BF16).astype(F32)
        middle = (row - high).astype(BF16).astype(F32)
        low = row - high - middle
        place = lax.broadcasted_iota(jnp.int32, (8, HD), 0)
        terms = jnp.where(
            place == 0, high, jnp.where(place == 1, middle, jnp.where(place == 2, low, 0.0))
        )
        return jnp.concatenate([terms, jnp.zeros((8, HD), F32)], axis=0).astype(BF16)

    def result_copy(k, d, rel):
        return remote(nsend.at[k], nrecv.at[k], n_send.at[k], n_recv.at[k], device(d, rel, c))

    def finish(i, code, mx, maybe_first):
        total = acc[:, HD:]
        n = (acc[:, :HD] / total).astype(BF16)
        level = mx[...] * SCALE2 + jnp.log(total) * math.log2(math.e)
        for part in range(PARTS):
            rows = slice(part * BLOCK, (part + 1) * BLOCK)
            k = PARTS * i + part
            nsend[k, 0:BLOCK, :] = n[rows]
            nsend[k, BLOCK:, :] = as_rows(level[rows])
            copy = result_copy(k, (code // PLANES ** (part // 2)) % PLANES, part % 2)
            if maybe_first and part == 0:
                @pl.when(i > 0)
                def _():
                    copy.start()

                @pl.when(i == 0)
                def _():
                    nrecv[0] = nsend[0]
            else:
                copy.start()
        return code // PLANES**GROUP

    for copy in pair[:3]:
        copy.wait_recv()
    for part in range(1, PARTS):
        query_copy(part, 0, 1).wait_recv()
    q = queries_of(0)
    new_scores(True, q, t0, mx0)

    def first_scores(j, _):
        @pl.when(j == CHUNKS // 2)
        def _():
            mark_live(1)

        for k, copy in enumerate(pair_keys):
            pl.when(j == CHUNKS // 2 + k)(copy.wait_recv)

        scores(q, j, s0, mx0)
        return 0

    lax.fori_loop(0, CHUNKS, first_scores, 0)
    close_max(mx0)
    def both(i, s_now, t_now, mx_now, s_later, t_later, mx_later, maybe_first):
        wait_queries(i + 1)
        q = queries_of(i + 1)
        new_scores(False, q, t_later, mx_later)
        new_values(t_now, mx_now)

        def body(j, _):
            if maybe_first:
                for k, copy in enumerate(pair_values):
                    pl.when((i == 0) & (j == CHUNKS // 2 + k))(copy.wait_recv)

            p = chunk_weights(j, s_now, mx_now)
            scores(q, j, s_later, mx_later)
            add_values(j, p)
            return 0

        lax.fori_loop(0, CHUNKS, body, 0)
        close_max(mx_later)

    def two_tiles(k, code):
        i = 2 * k
        both(i, s0, t0, mx0, s1, t1, mx1, True)
        code = finish(i, code, mx0, True)

        @pl.when(i + 2 < TILES)
        def _():
            both(i + 1, s1, t1, mx1, s0, t0, mx0, False)

        @pl.when(i + 2 == TILES)
        def _():
            new_values(t1, mx1)

            def body(j, _):
                add_values(j, chunk_weights(j, s1, mx1))
                return 0

            lax.fori_loop(0, CHUNKS, body, 0)

        return finish(i + 1, code, mx1, False)

    lax.fori_loop(0, TILES // 2, two_tiles, CODE)

    def wait_result(k, _):
        result_copy(k, 0, 1).wait_recv()
        return 0

    def level_of(v):
        terms = nrecv[v, BLOCK:, :].astype(F32)
        return jnp.broadcast_to(jnp.sum(terms, axis=0, keepdims=True), (8, HD))

    def as_columns(rows):
        place = lax.broadcasted_iota(jnp.int32, (8, HD), 0)
        packed = []
        for first in range(0, len(rows), 8):
            block = jnp.zeros((8, HD), F32)
            for v in range(first, min(first + 8, len(rows))):
                block = jnp.where(place == v - first, rows[v], block)
            packed.append(block)
        packed.append(jnp.zeros((HD - 8 * len(packed), HD), F32))
        return jnp.transpose(jnp.concatenate(packed, axis=0))[0:BLOCK, :]

    def largest(levels):
        top = levels[0]
        for level in levels[1:]:
            top = jnp.maximum(top, level)
        return top

    early = SLOTS - PARTS
    lax.fori_loop(1, early, wait_result, 0)
    levels = [level_of(v) for v in range(early)]
    early_top = largest(levels)
    shares = [jnp.exp2(level - early_top) for level in levels]
    early_sum = sum(shares[1:], shares[0])
    share = as_columns(shares)
    early_total = jnp.zeros((BLOCK, HD), F32)
    for v in range(early):
        early_total = early_total + nrecv[v, 0:BLOCK, :].astype(F32) * share[:, v : v + 1]

    lax.fori_loop(early, SLOTS, wait_result, 0)
    levels = [early_top] + [level_of(v) for v in range(early, SLOTS)]
    summit = largest(levels)
    shares = [jnp.exp2(level - summit) for level in levels]
    denom = sum(shares[1:], shares[0] * early_sum)
    share = as_columns([part / denom for part in shares])
    attention = early_total * share[:, 0:1]
    for k in range(PARTS):
        part = nrecv[early + k, 0:BLOCK, :].astype(F32)
        attention = attention + part * share[:, k + 1 : k + 2]
    attention = attention.astype(BF16)
    for g in range(HEADS):
        flat[:, g * HD : (g + 1) * HD] = attention[g * ROWS : (g + 1) * ROWS, :]

    def wait_weights(k, _):
        weight_copy(k).wait()
        return 0

    lax.fori_loop(0, TP, wait_weights, 0)

    def columns(i):
        return remote(
            psend.at[i], precv.at[i], p_send.at[i], p_recv.at[i],
            {"work": me, "tp": (t + i) % TP},
        )

    joined = flat[...]
    for i in (4, 5, 3, 2, 6, 7, 1):
        psend[i] = jnp.dot(joined, wv[(t + i) % TP], preferred_element_type=F32).astype(BF16)
        columns(i).start()
    total = jnp.dot(joined, wv[t], preferred_element_type=F32)

    def gather(i, total):
        columns(i).wait_recv()
        return total + precv[i].astype(F32)

    out_ref[...] = lax.fori_loop(1, TP, gather, total).astype(BF16)

    for copy in pair:
        copy.wait_send()

    def sent(k, _):
        query_copy(k, 0, 1).wait_send()
        result_copy(k, 0, 1).wait_send()
        return 0

    lax.fori_loop(1, SLOTS, sent, 0)

    def sent_columns(i, _):
        columns(i).wait_send()
        return 0

    lax.fori_loop(1, TP, sent_columns, 0)


def per_device(
    queries, new_keys, new_values, cache_keys, cache_values, lengths, positions, out_weight
):
    vmem = pl.BlockSpec(memory_space=pltpu.VMEM)
    smem = pl.BlockSpec(memory_space=pltpu.SMEM)
    anywhere = pl.BlockSpec(memory_space=pl.ANY)
    dma = pltpu.SemaphoreType.DMA
    out = pl.pallas_call(
        kernel,
        out_shape=jax.ShapeDtypeStruct((ROWS, COLS), BF16),
        in_specs=[smem, smem, vmem, vmem, vmem, anywhere, anywhere, anywhere],
        out_specs=vmem,
        scratch_shapes=[
            pltpu.VMEM((PAIR + NEWPAD, HD), BF16),
            pltpu.VMEM((PAIR + NEWPAD, 2 * HD), BF16),
            pltpu.VMEM((TP, COLS, COLS), BF16),
            pltpu.VMEM((SLOTS, BLOCK, HD), BF16),
            pltpu.VMEM((SLOTS, MESSAGE, HD), BF16),
            pltpu.VMEM((SLOTS, MESSAGE, HD), BF16),
            pltpu.VMEM((CHUNKS, TILE, CHUNK), F32),
            pltpu.VMEM((CHUNKS, TILE, CHUNK), F32),
            pltpu.VMEM((TILE, HD), F32),
            pltpu.VMEM((TILE, HD), F32),
            pltpu.VMEM((TILE, HD), F32),
            pltpu.VMEM((TILE, HD), F32),
            pltpu.VMEM((TILE, 2 * HD), F32),
            pltpu.VMEM((ROWS, HEADS * HD), BF16),
            pltpu.VMEM((TP, ROWS, COLS), BF16),
            pltpu.VMEM((TP, ROWS, COLS), BF16),
            pltpu.VMEM((2, 8, HD), F32),
            dma((2 + TP,)),
            dma((3 + CHUNKS,)),
            dma((3 + CHUNKS,)),
            dma((SLOTS,)),
            dma((SLOTS,)),
            dma((SLOTS,)),
            dma((SLOTS,)),
            dma((TP,)),
            dma((TP,)),
        ],
        compiler_params=pltpu.CompilerParams(
            collective_id=0, has_side_effects=True, vmem_limit_bytes=58 * 1024 * 1024
        ),
    )(
        positions.reshape(ROWS),
        lengths,
        queries[0].transpose(1, 0, 2).reshape(BLOCK, HD),
        new_keys.reshape(ROWS, HD),
        new_values.reshape(ROWS, HD),
        cache_keys.reshape(CACHE, HD),
        cache_values.reshape(CACHE, HD),
        out_weight,
    )
    return out[None]


def solution(mesh):
    in_specs = (
        P("work", None, "tp", None),
        P("work", None, "tp", None),
        P("work", None, "tp", None),
        P("work", None, "tp", None),
        P("work", None, "tp", None),
        P("work"),
        P("work", None),
        P("tp", None),
    )
    out_specs = P("work", None, "tp")
    return jax.shard_map(
        per_device, mesh=mesh, in_specs=in_specs, out_specs=out_specs, check_vma=False
    )
```

```python
import math

import jax
import jax.numpy as jnp
from jax import lax
from jax.experimental import pallas as pl
from jax.experimental.pallas import tpu as pltpu
from jax.sharding import PartitionSpec as P

MESH = pl.DeviceIdType.MESH
F32 = jnp.float32
BF16 = jnp.bfloat16

HEADS = 5
ROWS = 16
HD = 128
CACHE = 4096
PAIR = 2 * CACHE
NEWPAD = 128
BLOCK = HEADS * ROWS
GROUP = 2
PARTS = 2 * GROUP
TILE = PARTS * BLOCK
CHUNK = 2048
CHUNKS = PAIR // CHUNK
TP = 8
COLS = 640
PLANES = 8
TILES = PLANES // GROUP
ORDER = (0, 7, 3, 5, 4, 2, 6, 1)
CODE = sum(d * PLANES**i for i, d in enumerate(ORDER))
SLOTS = 2 * PLANES
MESSAGE = BLOCK + 16
LEAST = 1024
STEP = 1024

SCALE2 = HD**-0.5 * math.log2(math.e)
LOG_BASE = math.log(1000000.0)
NT = (((1,), (1,)), ((), ()))


def cos_sin(angle):
    turn = jnp.floor(angle * (2.0 / math.pi) + 0.5)
    rest = angle - turn * 1.5703125
    rest = rest - turn * 4.837512969970703125e-4
    rest = rest - turn * 7.54978995489188e-8
    z = rest * rest
    sine = rest + rest * z * ((-1.9515295891e-4 * z + 8.3321608736e-3) * z - 1.6666654611e-1)
    cosine = 1.0 - 0.5 * z + z * z * (
        (2.443315711809948e-5 * z - 1.388731625493765e-3) * z + 4.166664568298827e-2
    )
    quarter = turn.astype(jnp.int32) & 3
    odd = (quarter & 1) == 1
    c = jnp.where(odd, sine, cosine)
    s = jnp.where(odd, cosine, sine)
    c = jnp.where((quarter == 1) | (quarter == 2), -c, c)
    s = jnp.where(quarter >= 2, -s, s)
    return c, s


def kernel(
    pos_ref, len_ref, q_ref, nk_ref, nv_ref, ck_ref, cv_ref, w_ref, out_ref,
    kall, vaug, wv, qbuf, nsend, nrecv, s0, s1, t0, t1, mx0, mx1, acc,
    flat, psend, precv, lens,
    loc_sem, pair_send, pair_recv, q_send, q_recv, n_send, n_recv,
    p_send, p_recv,
):
    me = lax.axis_index("work")
    t = lax.axis_index("tp")
    z = me // 4
    yh = (me // 2) % 2
    c = me % 2

    def device(d, rel, core):
        hi = (yh + rel) % 2
        return {"work": 4 * ((z + d + PLANES) % PLANES) + 2 * hi + core, "tp": t}

    def remote(src, dst, send, recv, to):
        return pltpu.make_async_remote_copy(
            src, dst, send, recv, device_id=to, device_id_type=MESH
        )

    sibling = device(0, 0, 1 - c)
    partner = device(0, 1, c)

    copy_k = pltpu.make_async_copy(ck_ref, kall.at[pl.ds(0, CACHE)], loc_sem.at[0])
    copy_v = pltpu.make_async_copy(
        cv_ref, vaug.at[pl.ds(0, CACHE), pl.ds(0, HD)], loc_sem.at[1]
    )
    copy_k.start()
    copy_v.start()

    barrier = pltpu.get_barrier_semaphore()

    def signal(to):
        pl.semaphore_signal(barrier, inc=1, device_id=to, device_id_type=MESH)

    def greet(i, _):
        signal(device(i // 2, i % 2, c))
        return 0

    lax.fori_loop(1, SLOTS, greet, 0)
    signal(sibling)

    def greet_tp(i, _):
        signal({"work": me, "tp": (t + i) % TP})
        return 0

    lax.fori_loop(1, TP, greet_tp, 0)

    lane = lax.broadcasted_iota(jnp.int32, (ROWS, HD), 1)
    place = pos_ref[0] + lax.broadcasted_iota(jnp.int32, (ROWS, HD), 0)
    ladder = (lane % (HD // 2)).astype(F32) * (2.0 / HD)
    angle = place.astype(F32) * jnp.exp(ladder * -LOG_BASE)
    cosine, sine = cos_sin(angle)
    sine = jnp.where(lane < HD // 2, -sine, sine)

    def rotated(x):
        x = x.astype(F32)
        return (x * cosine + pltpu.roll(x, HD // 2, 1) * sine).astype(BF16)

    for g in range(HEADS):
        qbuf[0, g * ROWS : (g + 1) * ROWS, :] = rotated(q_ref[g * ROWS : (g + 1) * ROWS, :])
    kall[PAIR : PAIR + ROWS, :] = rotated(nk_ref[...])
    lens[0] = jnp.full((8, HD), len_ref[0], jnp.int32).astype(F32)

    def live_rows(owner, j):
        rows = lax.broadcasted_iota(jnp.int32, (STEP, HD), 0) + j * STEP
        return jnp.where(rows.astype(F32) < lens[owner, 0:1, :], 1.0, 0.0).astype(BF16)

    def mark_live(owner):
        def body(j, _):
            rows = pl.ds(owner * CACHE + pl.multiple_of(j * STEP, STEP), STEP)
            vaug[rows, HD:] = live_rows(owner, j)
            return 0

        lax.fori_loop(0, CACHE // STEP, body, 0)

    def mask_keys(j, _):
        live = live_rows(0, j)
        rows = pl.ds(pl.multiple_of(j * STEP, STEP), STEP)
        kall[rows, :] = kall[rows, :] * live + head_key * (1.0 - live)
        return 0

    def mask_values(j, _):
        rows = pl.ds(pl.multiple_of(j * STEP, STEP), STEP)
        vaug[rows, 0:HD] = vaug[rows, 0:HD] * live_rows(0, j)
        return 0

    copy_k.wait()
    head_key = kall[0:16, :].astype(F32)[0:1, :]
    head_key = jnp.broadcast_to(head_key, (STEP, HD)).astype(BF16)
    lax.fori_loop(LEAST // STEP, CACHE // STEP, mask_keys, 0)
    copy_v.wait()
    lax.fori_loop(LEAST // STEP, CACHE // STEP, mask_values, 0)
    mark_live(0)

    pl.semaphore_wait(barrier, SLOTS - 1 + 1 + TP - 1)

    def query_copy(k, d, rel):
        return remote(qbuf.at[0], qbuf.at[k], q_send.at[k], q_recv.at[k], device(-d, rel, c))

    pair = [
        remote(src, dst, pair_send.at[k], pair_recv.at[k], sibling)
        for k, (src, dst) in enumerate(
            (
                (lens.at[0], lens.at[1]),
                (kall.at[pl.ds(PAIR, ROWS)], kall.at[pl.ds(PAIR + ROWS, ROWS)]),
                (nv_ref, vaug.at[pl.ds(PAIR + ROWS, ROWS), pl.ds(0, HD)]),
                *[
                    (kall.at[pl.ds(r, CHUNK)], kall.at[pl.ds(CACHE + r, CHUNK)])
                    for r in range(0, CACHE, CHUNK)
                ],
                *[
                    (
                        vaug.at[pl.ds(r, CHUNK), pl.ds(0, HD)],
                        vaug.at[pl.ds(CACHE + r, CHUNK), pl.ds(0, HD)],
                    )
                    for r in range(0, CACHE, CHUNK)
                ],
            )
        )
    ]
    query_copy(1, 0, 1).start()
    pair_keys, pair_values = pair[3 : 3 + CHUNKS // 2], pair[3 + CHUNKS // 2 :]
    for copy in pair[:3] + pair_keys:
        copy.start()

    def send_queries(i, code):
        for rel in range(2):
            query_copy(2 * i + rel, code % PLANES, rel).start()
        return code // PLANES

    code = lax.fori_loop(1, 2 * GROUP, send_queries, CODE // PLANES)
    for copy in pair_values:
        copy.start()
    lax.fori_loop(2 * GROUP, PLANES, send_queries, code)

    def weight_copy(k):
        return pltpu.make_async_copy(
            w_ref.at[:, pl.ds(pl.multiple_of(k * COLS, HD), COLS)], wv.at[k], loc_sem.at[2 + k]
        )

    def start_weights(k, _):
        weight_copy(k).start()
        return 0

    lax.fori_loop(0, TP, start_weights, 0)

    kall[PAIR + 2 * ROWS :, :] = jnp.zeros((NEWPAD - 2 * ROWS, HD), BF16)
    vaug[PAIR : PAIR + ROWS, 0:HD] = nv_ref[...]
    vaug[PAIR + 2 * ROWS :, 0:HD] = jnp.zeros((NEWPAD - 2 * ROWS, HD), BF16)
    vaug[PAIR:, HD:] = jnp.ones((NEWPAD, HD), BF16)

    def wait_queries(i):
        for part in range(PARTS):
            query_copy(PARTS * i + part, 0, 1).wait_recv()

    def queries_of(i):
        return qbuf[pl.ds(PARTS * i, PARTS)].reshape(TILE, HD)

    def chunk(j):
        return pl.ds(pl.multiple_of(j * CHUNK, CHUNK), CHUNK)

    def scores(q, j, s_ref, mx):
        s = lax.dot_general(q, kall[chunk(j), :], NT, preferred_element_type=F32)
        s_ref[j] = s
        top = mx[...]
        for u in range(CHUNK // HD):
            top = jnp.maximum(top, s[:, u * HD : (u + 1) * HD])
        mx[...] = top

    def new_scores(first, q, t_ref, mx):
        row = lax.broadcasted_iota(jnp.int32, (TILE, HD), 0)
        col = lax.broadcasted_iota(jnp.int32, (TILE, HD), 1)
        r, r2 = row & 15, col & 15
        seen = (r2 >> 2) < (r >> 2)
        if first:
            own = (row < BLOCK) & (col < ROWS)
            seen = seen | (own & ((r2 >> 2) == (r >> 2)) & (r2 <= r))
        s = lax.dot_general(q, kall[PAIR:, :], NT, preferred_element_type=F32)
        s = jnp.where(seen & (col < 2 * ROWS), s, -1e30)
        t_ref[...] = s
        mx[...] = s

    def close_max(mx):
        mx[...] = jnp.broadcast_to(jnp.max(mx[...], axis=1, keepdims=True), (TILE, HD))

    def weights(s, top):
        return jnp.exp2((s - top) * SCALE2).astype(BF16)

    def chunk_weights(j, s_ref, mx):
        top = mx[...]
        return jnp.concatenate(
            [weights(s_ref[j, :, u * HD : (u + 1) * HD], top) for u in range(CHUNK // HD)], axis=1
        )

    def add_values(j, p):
        acc[...] += jnp.dot(p, vaug[chunk(j), :], preferred_element_type=F32)

    def new_values(t_ref, mx):
        p = weights(t_ref[...], mx[...])
        acc[...] = jnp.dot(p, vaug[PAIR:, :], preferred_element_type=F32)

    def as_rows(level):
        padded = jnp.concatenate([level, jnp.zeros((HD - BLOCK, HD), F32)], axis=0)
        row = jnp.transpose(padded)[0:8, :]
        high = row.astype(BF16).astype(F32)
        middle = (row - high).astype(BF16).astype(F32)
        low = row - high - middle
        place = lax.broadcasted_iota(jnp.int32, (8, HD), 0)
        terms = jnp.where(
            place == 0, high, jnp.where(place == 1, middle, jnp.where(place == 2, low, 0.0))
        )
        return jnp.concatenate([terms, jnp.zeros((8, HD), F32)], axis=0).astype(BF16)

    def result_copy(k, d, rel):
        return remote(nsend.at[k], nrecv.at[k], n_send.at[k], n_recv.at[k], device(d, rel, c))

    def finish(i, code, mx, maybe_first):
        total = acc[:, HD:]
        n = (acc[:, :HD] / total).astype(BF16)
        level = mx[...] * SCALE2 + jnp.log(total) * math.log2(math.e)
        for part in range(PARTS):
            rows = slice(part * BLOCK, (part + 1) * BLOCK)
            k = PARTS * i + part
            nsend[k, 0:BLOCK, :] = n[rows]
            nsend[k, BLOCK:, :] = as_rows(level[rows])
            copy = result_copy(k, (code // PLANES ** (part // 2)) % PLANES, part % 2)
            if maybe_first and part == 0:
                @pl.when(i > 0)
                def _():
                    copy.start()

                @pl.when(i == 0)
                def _():
                    nrecv[0] = nsend[0]
            else:
                copy.start()
        return code // PLANES**GROUP

    for copy in pair[:3]:
        copy.wait_recv()
    for part in range(1, PARTS):
        query_copy(part, 0, 1).wait_recv()
    q = queries_of(0)
    new_scores(True, q, t0, mx0)

    def first_scores(j, _):
        @pl.when(j == CHUNKS // 2)
        def _():
            mark_live(1)

        for k, copy in enumerate(pair_keys):
            pl.when(j == CHUNKS // 2 + k)(copy.wait_recv)

        scores(q, j, s0, mx0)
        return 0

    lax.fori_loop(0, CHUNKS, first_scores, 0)
    close_max(mx0)
    def both(i, s_now, t_now, mx_now, s_later, t_later, mx_later, maybe_first):
        wait_queries(i + 1)
        q = queries_of(i + 1)
        new_scores(False, q, t_later, mx_later)
        new_values(t_now, mx_now)

        def body(j, _):
            if maybe_first:
                for k, copy in enumerate(pair_values):
                    pl.when((i == 0) & (j == CHUNKS // 2 + k))(copy.wait_recv)

            p = chunk_weights(j, s_now, mx_now)
            scores(q, j, s_later, mx_later)
            add_values(j, p)
            return 0

        lax.fori_loop(0, CHUNKS, body, 0)
        close_max(mx_later)

    def two_tiles(k, code):
        i = 2 * k
        both(i, s0, t0, mx0, s1, t1, mx1, True)
        code = finish(i, code, mx0, True)

        @pl.when(i + 2 < TILES)
        def _():
            both(i + 1, s1, t1, mx1, s0, t0, mx0, False)

        @pl.when(i + 2 == TILES)
        def _():
            new_values(t1, mx1)

            def body(j, _):
                add_values(j, chunk_weights(j, s1, mx1))
                return 0

            lax.fori_loop(0, CHUNKS, body, 0)

        return finish(i + 1, code, mx1, False)

    lax.fori_loop(0, TILES // 2, two_tiles, CODE)

    def wait_result(k, _):
        result_copy(k, 0, 1).wait_recv()
        return 0

    def level_of(v):
        terms = nrecv[v, BLOCK:, :].astype(F32)
        return jnp.broadcast_to(jnp.sum(terms, axis=0, keepdims=True), (8, HD))

    def as_columns(rows):
        place = lax.broadcasted_iota(jnp.int32, (8, HD), 0)
        packed = []
        for first in range(0, len(rows), 8):
            block = jnp.zeros((8, HD), F32)
            for v in range(first, min(first + 8, len(rows))):
                block = jnp.where(place == v - first, rows[v], block)
            packed.append(block)
        packed.append(jnp.zeros((HD - 8 * len(packed), HD), F32))
        return jnp.transpose(jnp.concatenate(packed, axis=0))[0:BLOCK, :]

    def largest(levels):
        top = levels[0]
        for level in levels[1:]:
            top = jnp.maximum(top, level)
        return top

    early = SLOTS - PARTS
    lax.fori_loop(1, early, wait_result, 0)
    levels = [level_of(v) for v in range(early)]
    early_top = largest(levels)
    shares = [jnp.exp2(level - early_top) for level in levels]
    early_sum = sum(shares[1:], shares[0])
    share = as_columns(shares)
    early_total = jnp.zeros((BLOCK, HD), F32)
    for v in range(early):
        early_total = early_total + nrecv[v, 0:BLOCK, :].astype(F32) * share[:, v : v + 1]

    lax.fori_loop(early, SLOTS, wait_result, 0)
    levels = [early_top] + [level_of(v) for v in range(early, SLOTS)]
    summit = largest(levels)
    shares = [jnp.exp2(level - summit) for level in levels]
    denom = sum(shares[1:], shares[0] * early_sum)
    share = as_columns([part / denom for part in shares])
    attention = early_total * share[:, 0:1]
    for k in range(PARTS):
        part = nrecv[early + k, 0:BLOCK, :].astype(F32)
        attention = attention + part * share[:, k + 1 : k + 2]
    attention = attention.astype(BF16)
    for g in range(HEADS):
        flat[:, g * HD : (g + 1) * HD] = attention[g * ROWS : (g + 1) * ROWS, :]

    def wait_weights(k, _):
        weight_copy(k).wait()
        return 0

    lax.fori_loop(0, TP, wait_weights, 0)

    def columns(i):
        return remote(
            psend.at[i], precv.at[i], p_send.at[i], p_recv.at[i],
            {"work": me, "tp": (t + i) % TP},
        )

    joined = flat[...]
    for i in (4, 5, 3, 2, 6, 7, 1):
        psend[i] = jnp.dot(joined, wv[(t + i) % TP], preferred_element_type=F32).astype(BF16)
        columns(i).start()
    total = jnp.dot(joined, wv[t], preferred_element_type=F32)

    def gather(i, total):
        columns(i).wait_recv()
        return total + precv[i].astype(F32)

    out_ref[...] = lax.fori_loop(1, TP, gather, total).astype(BF16)

    for copy in pair:
        copy.wait_send()

    def sent(k, _):
        query_copy(k, 0, 1).wait_send()
        result_copy(k, 0, 1).wait_send()
        return 0

    lax.fori_loop(1, SLOTS, sent, 0)

    def sent_columns(i, _):
        columns(i).wait_send()
        return 0

    lax.fori_loop(1, TP, sent_columns, 0)


def per_device(
    queries, new_keys, new_values, cache_keys, cache_values, lengths, positions, out_weight
):
    vmem = pl.BlockSpec(memory_space=pltpu.VMEM)
    smem = pl.BlockSpec(memory_space=pltpu.SMEM)
    anywhere = pl.BlockSpec(memory_space=pl.ANY)
    dma = pltpu.SemaphoreType.DMA
    out = pl.pallas_call(
        kernel,
        out_shape=jax.ShapeDtypeStruct((ROWS, COLS), BF16),
        in_specs=[smem, smem, vmem, vmem, vmem, anywhere, anywhere, anywhere],
        out_specs=vmem,
        scratch_shapes=[
            pltpu.VMEM((PAIR + NEWPAD, HD), BF16),
            pltpu.VMEM((PAIR + NEWPAD, 2 * HD), BF16),
            pltpu.VMEM((TP, COLS, COLS), BF16),
            pltpu.VMEM((SLOTS, BLOCK, HD), BF16),
            pltpu.VMEM((SLOTS, MESSAGE, HD), BF16),
            pltpu.VMEM((SLOTS, MESSAGE, HD), BF16),
            pltpu.VMEM((CHUNKS, TILE, CHUNK), F32),
            pltpu.VMEM((CHUNKS, TILE, CHUNK), F32),
            pltpu.VMEM((TILE, HD), F32),
            pltpu.VMEM((TILE, HD), F32),
            pltpu.VMEM((TILE, HD), F32),
            pltpu.VMEM((TILE, HD), F32),
            pltpu.VMEM((TILE, 2 * HD), F32),
            pltpu.VMEM((ROWS, HEADS * HD), BF16),
            pltpu.VMEM((TP, ROWS, COLS), BF16),
            pltpu.VMEM((TP, ROWS, COLS), BF16),
            pltpu.VMEM((2, 8, HD), F32),
            dma((2 + TP,)),
            dma((3 + CHUNKS,)),
            dma((3 + CHUNKS,)),
            dma((SLOTS,)),
            dma((SLOTS,)),
            dma((SLOTS,)),
            dma((SLOTS,)),
            dma((TP,)),
            dma((TP,)),
        ],
        compiler_params=pltpu.CompilerParams(
            collective_id=0, has_side_effects=True, vmem_limit_bytes=58 * 1024 * 1024
        ),
    )(
        positions.reshape(ROWS),
        lengths,
        queries[0].transpose(1, 0, 2).reshape(BLOCK, HD),
        new_keys.reshape(ROWS, HD),
        new_values.reshape(ROWS, HD),
        cache_keys.reshape(CACHE, HD),
        cache_values.reshape(CACHE, HD),
        out_weight,
    )
    return out[None]


def solution(mesh):
    in_specs = (
        P("work", None, "tp", None),
        P("work", None, "tp", None),
        P("work", None, "tp", None),
        P("work", None, "tp", None),
        P("work", None, "tp", None),
        P("work"),
        P("work", None),
        P("tp", None),
    )
    out_specs = P("work", None, "tp")
    return jax.shard_map(
        per_device, mesh=mesh, in_specs=in_specs, out_specs=out_specs, check_vma=False
    )
```
